128 devices in a mesh: dp: 8 (over x, core), fsdp: 16 (over y, z).
Axes of the slice: x: 4, y: 4, z: 4, core: 2. Of those that a mesh axis runs over, the one named last changes fastest.
Arguments:
- tokens: bfloat16 [256, 256, 768], P(('dp', 'fsdp')), may hold values from -24 to 24
- lengths: int32 [256], P(('dp', 'fsdp')), may hold values from 128 to 256, as said below
- positions: int32 [256, 64], P(('dp', 'fsdp')), may hold values from 0 to 127
- cotangent: bfloat16 [256, 64, 768], P(('dp', 'fsdp')), may hold values from -24 to 24
- qkv_weight: bfloat16 [768, 2304], P(('dp', 'fsdp')), may hold values from -0.21875 to 0.21875
- out_weight: bfloat16 [768, 768], P(('dp', 'fsdp')), may hold values from -1.25 to 1.25
- up_weight: bfloat16 [768, 3072], P(('dp', 'fsdp')), may hold values from -0.21875 to 0.21875
- down_weight: bfloat16 [3072, 768], P(('dp', 'fsdp')), may hold values from -0.109375 to 0.109375
- norm_gains: bfloat16 [2, 768], P(None, ('dp', 'fsdp')), may hold values from 0.25 to 1.75
- biases: bfloat16 [6, 768], P(None, ('dp', 'fsdp')), may hold values from -3 to 3
- up_bias: bfloat16 [3072], P(('dp', 'fsdp')), may hold values from -3 to 3
Outputs:
- mixed: bfloat16 [256, 256, 768], P(('dp', 'fsdp'))
- token_grad: float32 [256, 256, 768], P(('dp', 'fsdp'))
- qkv_grad: float32 [768, 2304], P(('dp', 'fsdp'))
- out_grad: float32 [768, 768], P(('dp', 'fsdp'))
- up_grad: float32 [768, 3072], P(('dp', 'fsdp'))
- down_grad: float32 [3072, 768], P(('dp', 'fsdp'))
- gains_grad: float32 [2, 768], P(None, ('dp', 'fsdp'))
- biases_grad: float32 [6, 768], P(None, ('dp', 'fsdp'))
- up_bias_grad: float32 [3072], P(('dp', 'fsdp'))
The draws below stay inside these ranges and needn't reach their ends.
Inputs may be any that keep to these rules, and one draw needn't show every extreme that they name: `lengths`: one cell in every draw has exactly 256 genes; the other slots of a cell are padding. `positions`: all lie below 128, so within the cell's genes; a row may repeat, and repeated rows add.
All inputs are finite; a program needn't handle non-finite values.
Results may differ from the reference program's by a relative error of at most 0.012.
Values may be sent and summed in bfloat16 or wider, within the bound.
No kernel may reach another device: no remote copies, remote signals or barrier semaphores. Data moves between devices by JAX's collectives and lax.ppermute only.
A program may use at most 192 MiB of HBM per device.

```python
import math
import jax
import jax.numpy as jnp
from jax import lax

HEADS = 12
HEAD_DIM = 64
D = 768
FF = 3072
LEN = 256
MASKED = 64
CELLS = 256


def draw_lengths(key, part):
    key = jax.random.fold_in(key, 11)
    counts = jax.random.randint(key, (CELLS,), LEN // 2, LEN + 1)
    chosen = jax.random.randint(jax.random.fold_in(key, 1), (), 0, CELLS)
    return jnp.where(jnp.arange(CELLS) == chosen, LEN, counts).astype(jnp.int32)


def set_ends(result, own_key, low, top_value):
    longest = result.shape.index(max(result.shape))
    spots = []
    for shift in (0, 1):
        where = [jax.random.randint(jax.random.fold_in(own_key, axis), (), 0, length) for axis, length in enumerate(result.shape)]
        where[longest] = (where[longest] + shift) % result.shape[longest]
        spots.append(tuple(where))
    return result.at[spots[0]].set(low).at[spots[1]].set(top_value)


def strengthened(result, own_key, source, target, blocks, factor):
    owner, partner = [(jnp.arange(result.shape[position]) // (result.shape[position] // blocks)).reshape([-1 if axis == position else 1 for axis in range(result.ndim)]) for position in (source, target)]
    chosen = jax.random.permutation(own_key, blocks)[partner]
    strong = (owner == chosen) | (owner == (partner + blocks // 2) % blocks)
    return jnp.where(strong, factor * result, result)


def shard_levels(key, extent, shards, low, largest):
    level = 1.0
    for position, blocks in shards:
        steps = jax.random.uniform(jax.random.fold_in(jax.random.fold_in(key, 6), position), (blocks,), jnp.float32, low / len(shards), largest / len(shards))
        level = level * jnp.repeat(jnp.exp(steps), extent[position] // blocks).reshape((-1,) + (1,) * (len(extent) - 1 - position))
    return level


def gaussian(rng, shape, deviation, reach, shards=(), kind=jnp.bfloat16):
    values = deviation * jax.random.normal(rng, shape, jnp.float32)
    if shards:
        values = values * shard_levels(rng, shape, shards, -0.22, 0.18)
    return jnp.clip(values, -reach, reach).astype(kind)


def heavy_noise(own_key, shape, deviation, limit, cuts, heavy, kind=jnp.bfloat16):
    array = deviation * jax.random.normal(own_key, shape, jnp.float32)
    if cuts:
        array = array * shard_levels(own_key, shape, cuts, -0.22, 0.18)
    return jnp.clip(strengthened(array, jax.random.fold_in(own_key, 3), *heavy), -limit, limit).astype(kind)


def setup_inputs(seed: int = 0) -> dict:
    arg_keys = jax.random.split(jax.random.key(seed), 12)
    return {
        "tokens": heavy_noise(arg_keys[0], (CELLS, LEN, D), 1.0, 24.0, ((0, 128),), (0, 2, 128, 5.5)),
        "lengths": draw_lengths(jax.random.fold_in(arg_keys[11], 71), 0),
        "positions": set_ends(jax.random.randint(arg_keys[2], (CELLS, MASKED), 0, LEN // 2), jax.random.fold_in(arg_keys[2], 1), 0, (LEN // 2) - 1).astype(jnp.int32),
        "cotangent": heavy_noise(arg_keys[3], (CELLS, MASKED, D), 1.0, 24.0, ((0, 128),), (0, 2, 128, 5.5)),
        "qkv_weight": gaussian(arg_keys[4], (D, 3 * D), D ** -0.5, 0.21875, ((0, 128),)),
        "out_weight": gaussian(arg_keys[5], (D, D), (D * 8 // LEN) ** -0.5, 1.25, ((0, 128),)),
        "up_weight": gaussian(arg_keys[6], (D, FF), D ** -0.5, 0.21875, ((0, 128),)),
        "down_weight": gaussian(arg_keys[7], (FF, D), FF ** -0.5, 0.109375, ((0, 128),)),
        "norm_gains": jnp.clip(1.0 + 0.15 * jax.random.normal(arg_keys[8], (2, D), jnp.float32), 0.25, 1.75).astype(jnp.bfloat16),
        "biases": gaussian(arg_keys[9], (6, D), 0.5, 3.0, ((1, 128),)),
        "up_bias": gaussian(arg_keys[10], (FF,), 0.5, 3.0, ((0, 128),)),
    }


@jax.custom_vjp
def low(v):
    return lax.optimization_barrier(v.astype(jnp.bfloat16)).astype(jnp.float32)

@jax.custom_vjp
def low_back(v):
    return v

def low_keep(v):
    return (low(v), None)

def low_pass(kept, grad):
    return (grad,)

def back_keep(v):
    return (v, None)

def back_low(kept, grad):
    return (low(grad),)
low.defvjp(low_keep, low_pass)
low_back.defvjp(back_keep, back_low)
HIGHEST = lax.Precision.HIGHEST

def layer_norm(inputs, gain, shift):
    center_mean = lax.optimization_barrier(jnp.mean(inputs, axis=-1, keepdims=True))
    centered = inputs - center_mean
    variance = lax.optimization_barrier(jnp.mean(centered * centered, axis=-1, keepdims=True))
    return centered * lax.rsqrt(variance + 1e-05) * gain + shift

def encoder_layer(inputs, valid_keys, qkv_weight, out_weight, up_weight, down_weight, norm_gains, biases, up_bias):
    group_size = inputs.shape[0]
    normed_one = low(layer_norm(inputs, norm_gains[0], biases[0]))
    qkv_shift = jnp.concatenate([biases[1], jnp.zeros_like(biases[1]), biases[2]])
    qkv_all = jnp.einsum('gld,de->gle', normed_one, qkv_weight, precision=HIGHEST) + qkv_shift
    qkv_all = low(low_back(qkv_all))
    parts = qkv_all.reshape(group_size, LEN, 3, HEADS, HEAD_DIM)
    queries = parts[:, :, 0]
    key_rows = parts[:, :, 1]
    value_rows = parts[:, :, 2]
    scores = jnp.einsum('gqhe,gkhe->ghqk', queries, key_rows, precision=HIGHEST) * HEAD_DIM ** (-0.5)
    scores = low_back(scores)
    scores = jnp.where(valid_keys[:, None, None, :], scores, -1000000000.0)
    row_peak = lax.optimization_barrier(jnp.max(scores, axis=-1, keepdims=True))
    exp_scores = jnp.exp(scores - row_peak)
    soft_weights = exp_scores / lax.optimization_barrier(jnp.sum(exp_scores, axis=-1, keepdims=True))
    attended = jnp.einsum('ghqk,gkhe->gqhe', low(soft_weights), value_rows, precision=HIGHEST)
    attended = low(low_back(attended.reshape(group_size, LEN, D)))
    branch_one = jnp.einsum('gld,de->gle', attended, out_weight, precision=HIGHEST) + biases[3]
    mid_stream = inputs + low_back(branch_one)
    normed_two = low(layer_norm(mid_stream, norm_gains[1], biases[4]))
    up_pre = jnp.einsum('gld,df->glf', normed_two, up_weight, precision=HIGHEST) + up_bias
    up_pre = low_back(up_pre)
    activated = low(jax.nn.gelu(up_pre, approximate=False))
    branch_two = jnp.einsum('glf,fd->gld', activated, down_weight, precision=HIGHEST) + biases[5]
    return mid_stream + low_back(branch_two)

def reference(tokens, lengths, positions, cotangent, qkv_weight, out_weight, up_weight, down_weight, norm_gains, biases, up_bias):
    params = tuple((w.astype(jnp.float32) for w in (qkv_weight, out_weight, up_weight, down_weight, norm_gains, biases, up_bias)))
    group_size = math.gcd(CELLS, max(1, 4096 // LEN))
    group_count = CELLS // group_size
    all_inputs = tokens.astype(jnp.float32).reshape(group_count, group_size, LEN, D)
    all_lengths = lengths.reshape(group_count, group_size)
    all_positions = positions.reshape(group_count, group_size, MASKED)
    all_cot = cotangent.astype(jnp.float32).reshape(group_count, group_size, MASKED, D)

    def scatter_rows(where_rows, rows):
        return jnp.zeros((LEN, D), jnp.float32).at[where_rows].add(rows)

    def cell_group(totals, group_item):
        inputs, group_lengths, group_positions, group_cot = group_item
        valid_keys = jnp.arange(LEN, dtype=jnp.int32)[None, :] < group_lengths[:, None]

        def layer_fn(layer_in, *weights):
            return encoder_layer(layer_in, valid_keys, *weights)
        layer_out, pullback = jax.vjp(layer_fn, inputs, *params)
        out_cot = jax.vmap(scatter_rows)(group_positions, group_cot)
        grads = pullback(out_cot)
        totals = tuple((a_sum + g_new for a_sum, g_new in zip(totals, grads[1:])))
        return (totals, (layer_out.astype(jnp.bfloat16), grads[0]))
    start = tuple((jnp.zeros_like(w) for w in params))
    grad_sums, (outputs, input_grads) = lax.scan(cell_group, start, (all_inputs, all_lengths, all_positions, all_cot))
    mixed = outputs.reshape(CELLS, LEN, D)
    token_grad = input_grads.reshape(CELLS, LEN, D)
    return (mixed, token_grad, grad_sums[0], grad_sums[1], grad_sums[2], grad_sums[3], grad_sums[4], grad_sums[5], grad_sums[6])
```

```python
import functools

import jax
import jax.numpy as jnp
import numpy as np
from jax import lax
from jax.experimental import pallas as pl
from jax.experimental.pallas import tpu as pltpu
from jax.sharding import Mesh, PartitionSpec as P

B16 = jnp.bfloat16
F32 = jnp.float32
HEADS = 12
HEAD_DIM = 64
D = 768
FF = 3072
LEN = 256
HALF = 128
ROWS = 512
PAD = 1024
CHUNK = 512
SCALE = HEAD_DIM**-0.5
ALL = ("x", "core", "y", "z")
SIZES = (4, 2, 4, 4)
VMEM = 60 * 1024 * 1024
RSQRT2 = 0.5**0.5
RSQRT2PI = (2.0 * np.pi) ** -0.5


def dot(a, b, ca=1, cb=0):
    return lax.dot_general(a, b, (((ca,), (cb,)), ((), ())), preferred_element_type=F32)


def pick(a, p):
    return dot(a, p).astype(B16)


def put_back(a, p):
    high = a.astype(B16)
    rest = (a - high.astype(F32)).astype(B16)
    return dot(high, p, 1, 1) + dot(rest, p, 1, 1)


def norm_stats(v):
    centered = v - jnp.mean(v, axis=-1, keepdims=True)
    variance = jnp.mean(centered * centered, axis=-1, keepdims=True)
    scale = lax.rsqrt(variance + 1e-05)
    return centered * scale, scale


def norm_back(grad, hat, scale, gain):
    g = grad * gain
    mean_g = jnp.mean(g, axis=-1, keepdims=True)
    mean_gh = jnp.mean(g * hat, axis=-1, keepdims=True)
    return scale * (g - mean_g - hat * mean_gh)


def row_sum(v):
    return jnp.sum(v, axis=0, keepdims=True)


def softmax_of(q_one, k_two, valid):
    s = jnp.where(valid, dot(q_one, k_two, 1, 1), -1000000000.0)
    e = jnp.exp(s - jnp.max(s, axis=-1, keepdims=True))
    return e / jnp.sum(e, axis=-1, keepdims=True)


def attention_kernel(
    lens_ref, x_ref, wqk_ref, wv_ref, wo_ref, ext_ref, py_ref, pz_ref, spread_ref,
    a1_ref, qkv_ref, o_ref, x1_ref, a2_ref, par_ref, ub_ref,
):
    par = dot(ext_ref[...], py_ref[...], 0, 1)
    par_ref[...] = par[:8]
    lane = lax.broadcasted_iota(jnp.int32, (8, PAD), 1) % 8
    own = lane == lax.broadcasted_iota(jnp.int32, (8, PAD), 0)
    for j in range(3):
        wide = dot(par[8 + 8 * j : 16 + 8 * j].astype(B16), spread_ref[...])
        ub_ref[j : j + 1, :] = row_sum(jnp.where(own, wide, 0.0))
    ub_ref[3:, :] = jnp.zeros((5, PAD), F32)
    x = x_ref[...].astype(F32)
    hat, _ = norm_stats(x)
    a1 = (hat * par[0:1] + par[2:3]).astype(B16)
    a1_ref[...] = a1
    qk = dot(pick(a1, py_ref[...]), wqk_ref[...])
    qkv_ref[:, :D] = (qk[:, :D] + par[3:4]).astype(B16)
    qkv_ref[:, D : 2 * D] = qk[:, D:].astype(B16)
    qkv_ref[:, 2 * D :] = (dot(pick(a1, pz_ref[...]), wv_ref[...]) + par[4:5]).astype(B16)
    head_lane = lax.broadcasted_iota(jnp.int32, (LEN, 128), 1) < HEAD_DIM
    key = lax.broadcasted_iota(jnp.int32, (1, LEN), 1)
    for cell in range(2):
        valid = key < lens_ref[cell]
        rows = slice(cell * LEN, (cell + 1) * LEN)
        for pair in range(HEADS // 2):
            at = pair * 128
            q = qkv_ref[rows, at : at + 128] * SCALE
            k = qkv_ref[rows, D + at : D + at + 128]
            v = qkv_ref[rows, 2 * D + at : 2 * D + at + 128]
            total = None
            for head in range(2):
                mine = head_lane if head == 0 else ~head_lane
                p = softmax_of(jnp.where(mine, q, 0), k, valid).astype(B16)
                o = dot(p, jnp.where(mine, v, 0))
                total = o if total is None else total + o
            o_ref[rows, at : at + 128] = total.astype(B16)
    x1 = x + dot(pick(o_ref[...], pz_ref[...]), wo_ref[...]) + par[5:6]
    hat, _ = norm_stats(x1)
    a2 = (hat * par[1:2] + par[6:7]).astype(B16)
    for cell in range(2):
        for half in range(2):
            src = slice(cell * LEN + half * HALF, cell * LEN + (half + 1) * HALF)
            dst = slice(half * LEN + cell * HALF, half * LEN + (cell + 1) * HALF)
            x1_ref[dst, :] = x1[src]
            a2_ref[dst, :] = a2[src]


def ffn_kernel(
    offs_ref, a2_ref, x1_ref, pos_ref, cot_ref, par_ref, ub_ref, py_ref, pz_ref,
    gy_ref, gz_ref, yz_ref, wup_ref, wdn_ref,
    mixed_ref, dx1_ref, vec_ref, ubg_ref, yk_ref, ys_ref, zk_ref, zs_ref, dk_ref, ds_ref,
    a2f, a2g, dy, dz, acc, dacc, g_all,
):
    c = pl.program_id(0)

    @pl.when(c == 0)
    def _():
        a2 = a2_ref[...]
        a2f[0] = pick(a2, py_ref[...])
        a2f[1] = pick(a2, pz_ref[...])
        a2g[0] = pick(a2[:LEN], gy_ref[...])
        a2g[1] = pick(a2[:LEN], gz_ref[...])
        row = lax.broadcasted_iota(jnp.int32, (HALF, 64), 0)
        for cell in range(2):
            hot = (row == pos_ref[cell : cell + 1, :]).astype(F32).astype(B16)
            part = dot(hot, cot_ref[cell])
            dy[cell * HALF : (cell + 1) * HALF, :] = part
            dz[cell * HALF : (cell + 1) * HALF, :] = part.astype(B16)
        acc[...] = jnp.zeros_like(acc)
        dacc[...] = jnp.zeros_like(dacc)

    lane = c // 3
    wup = wup_ref[...]
    wdn = wdn_ref[...]
    u = dot(a2f[lane], wup) + ub_ref[pl.ds(c // 2, 1), pl.ds((c % 2) * CHUNK, CHUNK)]
    phi = 0.5 + 0.5 * lax.erf(u * RSQRT2)
    g = (u * phi).astype(B16)
    acc[...] += dot(g, wdn)
    top = u[:LEN]
    slope = phi[:LEN] + top * (jnp.exp(-0.5 * top * top) * RSQRT2PI)
    du_wide = dot(dz[...], wdn, 1, 1) * slope
    du = du_wide.astype(B16)
    dacc[lane] += dot(du, wup, 1, 1)
    ubg_ref[pl.ds(c // 2, 1), pl.ds((c % 2) * CHUNK, CHUNK)] = row_sum(du.astype(F32))
    dw = dot(a2g[lane], du, 0, 0).astype(B16)

    @pl.when(c < 3)
    def _():
        yk_ref[...] = dw[:384]
        ys_ref[...] = dw[384:]

    @pl.when(c >= 3)
    def _():
        zk_ref[...] = dw[:384]
        zs_ref[...] = dw[384:]

    g_all[:, pl.ds(pl.multiple_of((c % 2) * CHUNK, CHUNK), CHUNK)] = g[:LEN]

    @pl.when(c % 2 == 1)
    def _():
        for half, out in ((0, dk_ref), (1, ds_ref)):
            blocks = []
            for i in range(4):
                at = pl.multiple_of(offs_ref[half * 4 + i] * 128, 128)
                blocks.append(pick(g_all[:, pl.ds(at, 128)], yz_ref[half]))
            grad = dot(jnp.concatenate(blocks, axis=1), dz[...], 0, 0).astype(B16)
            for i in range(4):
                at = pl.multiple_of(i * 384 + (c // 2) * 128, 128)
                out[pl.ds(at, 128), :] = grad[i * 128 : (i + 1) * 128]

    @pl.when(c == 5)
    def _():
        x1 = x1_ref[...]
        mixed = (x1 + acc[...] + par_ref[7:8]).astype(B16)
        for cell in range(2):
            for half in range(2):
                dst = slice(cell * LEN + half * HALF, cell * LEN + (half + 1) * HALF)
                src = slice(half * LEN + cell * HALF, half * LEN + (cell + 1) * HALF)
                mixed_ref[dst, :] = mixed[src]
        da2 = put_back(dacc[0], py_ref[...]) + put_back(dacc[1], pz_ref[...])
        hat, scale = norm_stats(x1[:LEN])
        dx1_ref[...] = dy[...] + norm_back(da2, hat, scale, par_ref[1:2])
        vec_ref[0:1, :] = row_sum(da2 * hat)
        vec_ref[1:2, :] = row_sum(da2)
        vec_ref[2:3, :] = row_sum(dz[...].astype(F32))
        vec_ref[3:, :] = jnp.zeros((5, D), F32)
        ubg_ref[3:, :] = jnp.zeros((5, PAD), F32)


def attention_back_kernel(
    lens_ref, dx1_ref, o_ref, qkv_ref, wo_ref, pz_ref, gz_ref,
    ok_ref, os_ref, dq_ref, dk_ref, dv_ref, vec_ref, do_ref,
):
    db = dx1_ref[...].astype(B16)
    do_ref[...] = pick(dot(db, wo_ref[...], 1, 1).astype(B16), pz_ref[...].T)
    o = jnp.concatenate([o_ref[:HALF], o_ref[LEN : LEN + HALF]], axis=0)
    grad = dot(pick(o, gz_ref[...]), db, 0, 0).astype(B16)
    ok_ref[...] = grad[:384]
    os_ref[...] = grad[384:]
    head_lane = lax.broadcasted_iota(jnp.int32, (LEN, 128), 1) < HEAD_DIM
    key = lax.broadcasted_iota(jnp.int32, (1, LEN), 1)
    for cell in range(2):
        valid = key < lens_ref[cell]
        rows = slice(cell * LEN, (cell + 1) * LEN)
        first = slice(cell * LEN, cell * LEN + HALF)
        grads = slice(cell * HALF, (cell + 1) * HALF)
        for pair in range(HEADS // 2):
            at = pair * 128
            q = qkv_ref[first, at : at + 128] * SCALE
            k = qkv_ref[rows, D + at : D + at + 128]
            v = qkv_ref[rows, 2 * D + at : 2 * D + at + 128]
            do = do_ref[grads, at : at + 128]
            dq = dk = dv = None
            for head in range(2):
                mine = head_lane if head == 0 else ~head_lane
                q_one = jnp.where(mine[:HALF], q, 0)
                do_one = jnp.where(mine[:HALF], do, 0)
                p = softmax_of(q_one, k, valid)
                dp = dot(do_one, v, 1, 1)
                ds = (p * (dp - jnp.sum(dp * p, axis=-1, keepdims=True))).astype(B16)
                dq_h = dot(ds, jnp.where(mine, k, 0))
                dk_h = dot(ds, q_one, 0, 0)
                dv_h = dot(p.astype(B16), do_one, 0, 0)
                dq = dq_h if dq is None else dq + dq_h
                dk = dk_h if dk is None else dk + dk_h
                dv = dv_h if dv is None else dv + dv_h
            dq_ref[grads, at : at + 128] = (dq * SCALE).astype(B16)
            dk_ref[rows, at : at + 128] = dk.astype(B16)
            dv_ref[rows, at : at + 128] = dv.astype(B16)
    vec_ref[0:1, :] = row_sum(db.astype(F32))
    vec_ref[1:2, :] = row_sum(dq_ref[...].astype(F32))
    vec_ref[2:3, :] = row_sum(dv_ref[...].astype(F32))
    vec_ref[3:, :] = jnp.zeros((5, D), F32)


def qkv_grad_kernel(
    a1_ref, dq_ref, dk_ref, dv_ref, gy_ref, gz_ref, qkk_ref, qks_ref, vk_ref, vs_ref
):
    a1 = a1_ref[...]
    a1y = pick(a1, gy_ref[...])
    a1z = pick(a1, gz_ref[...])
    a1q = jnp.concatenate([a1y[:HALF], a1y[LEN : LEN + HALF]], axis=0)
    grad_q = dot(a1q, dq_ref[...], 0, 0).astype(B16)
    qkk_ref[:, :D] = grad_q[:384]
    qks_ref[:, :D] = grad_q[384:]
    grad_k = dot(a1y, dk_ref[...], 0, 0).astype(B16)
    qkk_ref[:, D:] = grad_k[:384]
    qks_ref[:, D:] = grad_k[384:]
    grad_v = dot(a1z, dv_ref[...], 0, 0).astype(B16)
    vk_ref[...] = grad_v[:384]
    vs_ref[...] = grad_v[384:]


def input_grad_kernel(
    dq_ref, dk_ref, dv_ref, wqk_ref, wv_ref, py_ref, pz_ref, gy_ref, spread_ref,
    x_ref, dx1_ref, par_ref, vec_b_ref, vec_c_ref, ubg_ref,
    out_ref, ek_ref, es_ref, da_ref,
):
    from_q = put_back(dot(dq_ref[...], wqk_ref[:, :D], 1, 1), py_ref[...])
    da_ref[...] = put_back(dot(dk_ref[...], wqk_ref[:, D:], 1, 1), py_ref[...])
    da_ref[...] += put_back(dot(dv_ref[...], wv_ref[...], 1, 1), pz_ref[...])
    for cell in range(2):
        first = slice(cell * LEN, cell * LEN + HALF)
        da_ref[first, :] += from_q[cell * HALF : (cell + 1) * HALF]
    da = da_ref[...]
    hat, scale = norm_stats(x_ref[...].astype(F32))
    out_ref[...] = norm_back(da, hat, scale, par_ref[0:1])
    for cell in range(2):
        first = slice(cell * LEN, cell * LEN + HALF)
        out_ref[first, :] += dx1_ref[cell * HALF : (cell + 1) * HALF]
    lane = lax.broadcasted_iota(jnp.int32, (8, PAD), 1) % 8
    own = lane == lax.broadcasted_iota(jnp.int32, (8, PAD), 0)
    lines = [
        row_sum(da * hat), vec_b_ref[0:1], row_sum(da), vec_c_ref[1:2],
        vec_c_ref[2:3], vec_c_ref[0:1], vec_b_ref[1:2], vec_b_ref[2:3],
    ]
    for j in range(3):
        part = jnp.where(own, ubg_ref[j : j + 1, :], 0.0).astype(B16)
        lines.append(dot(part, spread_ref[...], 1, 1))
    lines.append(jnp.zeros((96, D), F32))
    vecs = jnp.concatenate(lines, axis=0).astype(B16)
    ext = dot(gy_ref[...], vecs, 0, 1).astype(B16)
    ek_ref[...] = ext[:384]
    es_ref[...] = ext[384:]


def whole(kernel, outs, flops, scratch=(), smem=0):
    def call(*args):
        specs = [pl.BlockSpec(memory_space=pltpu.SMEM)] * smem
        specs += [pl.BlockSpec(memory_space=pltpu.VMEM)] * (len(args) - smem)
        size = sum(a.size * a.dtype.itemsize for a in (*args, *outs))
        return pl.pallas_call(
            kernel,
            out_shape=outs,
            in_specs=specs,
            out_specs=[pl.BlockSpec(memory_space=pltpu.VMEM)] * len(outs),
            scratch_shapes=scratch,
            compiler_params=pltpu.CompilerParams(vmem_limit_bytes=VMEM),
            cost_estimate=pl.CostEstimate(flops=flops, bytes_accessed=size, transcendentals=0),
        )(*args)

    return call


def shape(*dims, dtype=B16):
    return jax.ShapeDtypeStruct(dims, dtype)


def swap_list(axis, step):
    pairs = []
    for flat in range(128):
        at = list(np.unravel_index(flat, SIZES))
        if axis == "core":
            at[1] ^= 1
        else:
            at[ALL.index(axis)] ^= 3 if (at[1] + step) % 2 else 1
        pairs.append((flat, int(np.ravel_multi_index(at, SIZES))))
    return pairs


def swap(v, axis, step=0):
    return lax.ppermute(v, ALL, swap_list(axis, step))


def relative(core, own):
    even = jnp.array([0, 1, 3, 2], jnp.int32)
    odd = jnp.array([0, 3, 1, 2], jnp.int32)
    return own ^ jnp.where(core == 0, even, odd)


def positions_of(at, order):
    total = 0
    core = jnp.stack([at["core"], 1 - at["core"]])
    weight = {"x": 32, "core": 16, "y": 4, "z": 1}
    total = core.reshape(2, 1, 1, 1, 1) * weight["core"] * 6
    for i, axis in enumerate(order):
        dims = [2, 1, 1, 1, 1]
        dims[1 + i] = 4
        rel = jnp.stack([relative(at["core"], at[axis]), relative(1 - at["core"], at[axis])])
        total = total + rel.reshape(dims) * weight[axis] * 6
    total = total + jnp.arange(6, dtype=jnp.int32)
    return total.reshape(D)


def one_hot(count, at):
    return (jnp.arange(count, dtype=jnp.int32)[:, None] == at[None, :]).astype(B16)


def halve(own, got, axis):
    for step in range(2):
        half = own.shape[0] // 2
        send = (own[half:] + got[half:].astype(F32)).astype(B16)
        keep = own[:half] + got[:half].astype(F32)
        own, got = keep, swap(send, axis, step=1 - step)
    return own, got


def local(
    tokens, lengths, positions, cotangent, qkv_weight, out_weight, up_weight, down_weight,
    norm_gains, biases, up_bias,
):
    at = {a: lax.axis_index(a) for a in ALL}
    lane_y = one_hot(D, positions_of(at, ("y", "z", "x")))
    lane_z = one_hot(D, positions_of(at, ("z", "x", "y")))
    eights = jnp.arange(PAD, dtype=jnp.int32)
    padded = one_hot(D, jnp.where(eights % 8 < 6, eights // 8 * 6 + eights % 8, -1))
    spread = one_hot(D, eights // 8 * 6)
    inner, offs = [], []
    for core in (at["core"], 1 - at["core"]):
        y = relative(core, at["y"]).reshape(4, 1, 1)
        z = relative(core, at["z"]).reshape(1, 4, 1)
        inner.append(one_hot(128, (y * 32 + z * 8 + jnp.arange(8, dtype=jnp.int32)).reshape(128)))
        offs.append(relative(core, at["x"]) * 2 + core)
    inner, offs = jnp.stack(inner), jnp.concatenate(offs)

    ub = jnp.zeros((6, 24), B16).at[0].set(up_bias.reshape(8, 3).T.reshape(24))
    ext = jnp.concatenate([norm_gains.T, biases.T, ub, jnp.zeros((6, 96), B16)], axis=1)
    up = up_weight.reshape(6, PAD, 3).transpose(0, 2, 1).reshape(6, FF)
    shard = jnp.concatenate([qkv_weight, out_weight, up], axis=1)
    shard = jnp.pad(shard, ((0, 2), (0, 0)))
    ext = jnp.pad(ext, ((0, 2), (0, 0)))
    shard = jnp.concatenate([shard, down_weight.reshape(8, 3 * D), ext], axis=1)
    full = lax.all_gather(shard, ALL, axis=0, tiled=True)
    wqk, wv, wo = full[:, : 2 * D], full[:, 2 * D : 3 * D], full[:, 3 * D : 4 * D]
    ext_all = full[:, 8448:]
    py = pz = padded

    x = tokens.reshape(ROWS, D)
    a1, qkv, o, x1, a2, par, ubw = whole(
        attention_kernel,
        [shape(ROWS, D), shape(ROWS, 3 * D), shape(ROWS, D), shape(ROWS, D, dtype=F32),
         shape(ROWS, D), shape(8, D, dtype=F32), shape(8, PAD, dtype=F32)],
        7_000_000_000, smem=1,
    )(lengths, x, wqk, wv, wo, ext_all, py, pz, spread)

    kp = py.shape[1]
    fixed = lambda *dims: pl.BlockSpec(dims, lambda c: (0,) * len(dims))
    mixed, dx1, vec_b, ubg, yk, ys, zk, zs, dnk, dns = pl.pallas_call(
        ffn_kernel,
        grid=(6,),
        in_specs=[
            pl.BlockSpec(memory_space=pltpu.SMEM),
            fixed(ROWS, D), fixed(ROWS, D), fixed(2, 64), fixed(2, 64, D), fixed(8, D), fixed(8, PAD),
            fixed(D, kp), fixed(D, kp), fixed(D, D), fixed(D, D), fixed(2, 128, 128),
            pl.BlockSpec((kp, CHUNK), lambda c: (0, 6 + c)),
            pl.BlockSpec((CHUNK, D), lambda c: (c % 2, 8 + c // 2)),
        ],
        out_specs=[
            fixed(ROWS, D), fixed(LEN, D), fixed(8, D), fixed(8, PAD),
            pl.BlockSpec((384, CHUNK), lambda c: (0, jnp.minimum(c, 2))),
            pl.BlockSpec((384, CHUNK), lambda c: (0, jnp.minimum(c, 2))),
            pl.BlockSpec((384, CHUNK), lambda c: (0, jnp.maximum(c - 3, 0))),
            pl.BlockSpec((384, CHUNK), lambda c: (0, jnp.maximum(c - 3, 0))),
            fixed(1536, D), fixed(1536, D),
        ],
        out_shape=[
            shape(ROWS, D), shape(LEN, D, dtype=F32), shape(8, D, dtype=F32), shape(8, PAD, dtype=F32),
            shape(384, 1536), shape(384, 1536), shape(384, 1536), shape(384, 1536),
            shape(1536, D), shape(1536, D),
        ],
        scratch_shapes=[
            pltpu.VMEM((2, ROWS, kp), B16), pltpu.VMEM((2, LEN, D), B16), pltpu.VMEM((LEN, D), F32),
            pltpu.VMEM((LEN, D), B16), pltpu.VMEM((ROWS, D), F32), pltpu.VMEM((2, LEN, kp), F32),
            pltpu.VMEM((LEN, PAD), B16),
        ],
        compiler_params=pltpu.CompilerParams(vmem_limit_bytes=VMEM),
        cost_estimate=pl.CostEstimate(flops=10_000_000_000, bytes_accessed=30_000_000, transcendentals=0),
    )(offs, a2, x1, positions, cotangent, par, ubw, py, pz, lane_y, lane_z, inner, full, full)

    got = swap(dns, "core")
    own, got = halve(dnk.astype(F32), got, "x")
    own, got = own.reshape(3, 128, D), got.reshape(3, 128, D)
    for axis in ("y", "z"):
        for step in range(2):
            half = own.shape[1] // 2
            send = (own[:, half:] + got[:, half:].astype(F32)).astype(B16)
            own = own[:, :half] + got[:, :half].astype(F32)
            got = swap(send, axis, step=1 - step)
    down_grad = (own + got.astype(F32)).transpose(1, 0, 2).reshape(24, D)

    got_y, got_z = swap(ys, "core"), swap(zs, "core")
    y2 = halve(yk.astype(F32), got_y, "y")
    z2 = halve(zk.astype(F32), got_z, "z")

    ok, os, dq, dk, dv, vec_c = whole(
        attention_back_kernel,
        [shape(384, D), shape(384, D), shape(LEN, D), shape(ROWS, D), shape(ROWS, D), shape(8, D, dtype=F32)],
        5_000_000_000, scratch=[pltpu.VMEM((LEN, D), B16)], smem=1,
    )(lengths, dx1, o, qkv, wo, pz, lane_z)
    got_o = swap(os, "core")
    qkk, qks, vk, vs = whole(
        qkv_grad_kernel,
        [shape(384, 2 * D), shape(384, 2 * D), shape(384, D), shape(384, D)],
        3_000_000_000,
    )(a1, dq, dk, dv, lane_y, lane_z)
    got_qk, got_v = swap(qks, "core"), swap(vs, "core")
    token_grad, ek, es = whole(
        input_grad_kernel,
        [shape(ROWS, D, dtype=F32), shape(384, 128), shape(384, 128)],
        4_000_000_000, scratch=[pltpu.VMEM((ROWS, D), F32)],
    )(dq, dk, dv, wqk, wv, py, pz, lane_y, spread, x, dx1, par, vec_b, vec_c, ubg)
    got_e = swap(es, "core")

    wide = lambda *parts: jnp.concatenate(parts, axis=1)
    y1 = halve(wide(qkk, ek).astype(F32), wide(got_qk, got_e), "y")
    z1 = halve(wide(vk, ok).astype(F32), wide(got_v, got_o), "z")

    own, got = halve(wide(y2[0], y1[0]), wide(y2[1], y1[1]), "z")
    own, got = halve(own, got, "x")
    y_sum = own + got.astype(F32)
    own, got = halve(wide(z2[0], z1[0]), wide(z2[1], z1[1]), "x")
    own, got = halve(own, got, "y")
    z_sum = own + got.astype(F32)

    up_grad = wide(y_sum[:, :1536], z_sum[:, :1536])
    up_grad = up_grad.reshape(6, 3, PAD).transpose(0, 2, 1).reshape(6, FF)
    qkv_grad = wide(y_sum[:, 1536:3072], z_sum[:, 1536:2304])
    out_grad = z_sum[:, 2304:]
    small = y_sum[:, 3072:]
    gains_grad, biases_grad = small[:, 0:2].T, small[:, 2:8].T
    up_bias_grad = small[0, 8:32].reshape(3, 8).T.reshape(24)
    return (
        mixed.reshape(2, LEN, D), token_grad.reshape(2, LEN, D), qkv_grad, out_grad, up_grad, down_grad,
        gains_grad, biases_grad, up_bias_grad,
    )


def solution(mesh):
    fine = Mesh(mesh.devices.reshape(SIZES), ALL)
    rows = lambda n: P(ALL, *([None] * (n - 1)))
    cols = P(None, ALL)
    in_specs = (rows(3), rows(1), rows(2), rows(3), rows(2), rows(2), rows(2), rows(2), cols, cols, rows(1))
    out_specs = (rows(3), rows(3), rows(2), rows(2), rows(2), rows(2), cols, cols, rows(1))
    return jax.shard_map(local, mesh=fine, in_specs=in_specs, out_specs=out_specs, check_vma=False)
```

```python
import functools

import jax
import jax.numpy as jnp
import numpy as np
from jax import lax
from jax.experimental import pallas as pl
from jax.experimental.pallas import tpu as pltpu
from jax.sharding import Mesh, PartitionSpec as P

B16 = jnp.bfloat16
F32 = jnp.float32
HEADS = 12
HEAD_DIM = 64
D = 768
FF = 3072
LEN = 256
HALF = 128
ROWS = 512
PIECE = 192
FIRST = 384
Y1, Y2, Z1, Z2 = 1280, 1792, 1920, 1280
QKV = 1152
CHUNKS = ((0, 0, 896), (0, 896, 896), (1, 0, 640), (1, 640, 640))
SCALE = HEAD_DIM**-0.5
ALL = ("x", "core", "y", "z")
SIZES = (4, 2, 4, 4)
RSQRT2 = 0.5**0.5
RSQRT2PI = (2.0 * np.pi) ** -0.5


def dot(a, b, ca=1, cb=0):
    return lax.dot_general(a, b, (((ca,), (cb,)), ((), ())), preferred_element_type=F32)


def pick(a, p):
    return dot(a, p).astype(B16)


def put_back(a, p):
    high = a.astype(B16)
    rest = (a - high.astype(F32)).astype(B16)
    return dot(high, p, 1, 1) + dot(rest, p, 1, 1)


def norm_stats(v):
    centered = v - jnp.mean(v, axis=-1, keepdims=True)
    variance = jnp.mean(centered * centered, axis=-1, keepdims=True)
    scale = lax.rsqrt(variance + 1e-05)
    return centered * scale, scale


def norm_back(grad, hat, scale, gain):
    g = grad * gain
    mean_g = jnp.mean(g, axis=-1, keepdims=True)
    mean_gh = jnp.mean(g * hat, axis=-1, keepdims=True)
    return scale * (g - mean_g - hat * mean_gh)


def row_sum(v):
    return jnp.sum(v, axis=0, keepdims=True)


def softmax_of(q_one, k_two, valid):
    s = jnp.where(valid, dot(q_one, k_two, 1, 1), -1000000000.0)
    e = jnp.exp(s - jnp.max(s, axis=-1, keepdims=True))
    return e / jnp.sum(e, axis=-1, keepdims=True)


class Copies:
    def __init__(self, sems):
        self.sems, self.used = sems, 0

    def start(self, src, dst):
        copy = pltpu.make_async_copy(src, dst, self.sems.at[self.used])
        self.used += 1
        copy.start()
        return copy


def wait(copies):
    for copy in copies:
        copy.wait()


def load_rows(copies, pieces, dst, cols):
    return [
        copies.start(p.at[:, cols], dst.at[pl.ds(i * PIECE, PIECE), :]) for i, p in enumerate(pieces)
    ]


def pack_kernel(qkv_ref, out_ref, up_ref, down_ref, gains_ref, biases_ref, ub_ref, yz_ref, deal_ref):
    vecs = jnp.concatenate([gains_ref[...], biases_ref[...]], axis=0)
    eye = lax.broadcasted_iota(jnp.int32, (8, 128), 0) == lax.broadcasted_iota(jnp.int32, (8, 128), 1)
    ext = dot(vecs, eye.astype(F32).astype(B16), 0, 0)
    wide = jnp.broadcast_to(ub_ref[...].astype(F32), (6, 24)).astype(B16)
    unit = lax.broadcasted_iota(jnp.int32, (6, 24), 1)
    mine = unit // 4 == lax.broadcasted_iota(jnp.int32, (6, 24), 0)
    shift = lax.broadcasted_iota(jnp.int32, (24, 128), 0) % 4 + 8
    shift = shift == lax.broadcasted_iota(jnp.int32, (24, 128), 1)
    ub = dot(jnp.where(mine, wide, 0), shift.astype(F32).astype(B16))
    at = 0
    for part in (
        qkv_ref[:, :QKV], (ext + ub).astype(B16), up_ref[:, :Y2],
        qkv_ref[:, QKV:], out_ref[...], up_ref[:, Y2:],
    ):
        yz_ref[:, at : at + part.shape[1]] = part
        at += part.shape[1]
    for i in range(16):
        deal_ref[i] = down_ref[...]


def by_fours():
    row = lax.broadcasted_iota(jnp.int32, (512, 512), 0)
    col = lax.broadcasted_iota(jnp.int32, (512, 512), 1)
    return (row == col % 128 * 4 + col // 128).astype(F32).astype(B16)


def one_hot_of(nat):
    row = lax.broadcasted_iota(jnp.int32, (D, D), 0)
    return (row == nat).astype(F32).astype(B16)


def attend(lens_ref, cell, qkv_ref, rows, o_ref, out_rows):
    head_lane = lax.broadcasted_iota(jnp.int32, (LEN, 128), 1) < HEAD_DIM
    valid = lax.broadcasted_iota(jnp.int32, (1, LEN), 1) < lens_ref[cell]
    group = 3
    for start in range(0, HEADS // 2, group):
        scores, probs = [], []
        for pair in range(start, start + group):
            at = pair * 128
            q = qkv_ref[rows, at : at + 128] * SCALE
            k = qkv_ref[rows, D + at : D + at + 128]
            both = jnp.concatenate([jnp.where(head_lane, q, 0), jnp.where(head_lane, 0, q)], axis=0)
            scores.append(dot(both, k, 1, 1))
        for s in scores:
            s = jnp.where(valid, s, -1000000000.0)
            e = jnp.exp(s - jnp.max(s, axis=-1, keepdims=True))
            probs.append((e * (1.0 / jnp.sum(e, axis=-1, keepdims=True))).astype(B16))
        for i, pair in enumerate(range(start, start + group)):
            at = pair * 128
            o = dot(probs[i], qkv_ref[rows, 2 * D + at : 2 * D + at + 128])
            o_ref[out_rows, at : at + 128] = jnp.where(head_lane, o[:LEN], o[LEN:]).astype(B16)


def first_attention_kernel(lens_ref, x_ref, nat_ref, y0, y1, y2, y3, z0, z1, z2, z3, *refs):
    a1y_ref, a1z_ref, qkv_ref, o_ref, par_ref, ub_ref, py_hbm, pz_hbm, wy_hbm, wz_hbm, wo_hbm = refs[-16:-5]
    wy, wz, py, pz, sems = refs[-5:]
    copies = Copies(sems)
    first = []
    for i, p in enumerate((y0, y1, y2, y3)):
        first.append(copies.start(p, wy.at[pl.ds(i * PIECE, PIECE), :]))
    second = []
    for i, p in enumerate((z0, z1, z2, z3)):
        second.append(copies.start(p, wz.at[pl.ds(i * PIECE, PIECE), :]))
    py[...] = one_hot_of(nat_ref[0:1])
    pz[...] = one_hot_of(nat_ref[1:2])
    outs = [copies.start(py, py_hbm), copies.start(pz, pz_hbm)]
    hat, _ = norm_stats(x_ref[...].astype(F32))
    wait(first)
    outs.append(copies.start(wy.at[:, pl.ds(0, QKV)], wy_hbm))
    par = dot(wy[:, QKV:Y1], py[...], 0, 1)
    par_ref[...] = par[:8]
    units = [jnp.concatenate([par[8 + q : 9 + q, g * 128 : (g + 1) * 128] for q in range(4)], axis=1) for g in range(6)]
    units = dot(jnp.concatenate(units + units[:2], axis=0).astype(B16), by_fours(), 1, 1)
    for g in range(6):
        ub_ref[:, g * 512 : (g + 1) * 512] = units[g : g + 1]
    a1 = (hat * par[0:1] + par[2:3]).astype(B16)
    a1y = pick(a1, py[...])
    a1y_ref[...] = a1y
    qk = dot(a1y, wy[:, :QKV])
    qkv_ref[:, :D] = (qk[:, :D] + par[3:4]).astype(B16)
    qkv_ref[:, D:QKV] = qk[:, D:].astype(B16)
    wait(second)
    outs.append(copies.start(wz.at[:, pl.ds(0, QKV)], wz_hbm))
    outs.append(copies.start(wz.at[:, pl.ds(QKV, D)], wo_hbm))
    a1z = pick(a1, pz[...])
    a1z_ref[...] = a1z
    kv = dot(a1z, wz[:, :QKV])
    qkv_ref[:, QKV : 2 * D] = kv[:, :384].astype(B16)
    qkv_ref[:, 2 * D :] = (kv[:, 384:] + par[4:5]).astype(B16)
    attend(lens_ref, 0, qkv_ref, slice(0, LEN), o_ref, slice(0, LEN))
    wait(outs)


def second_attention_kernel(
    lens_ref, x_ref, qkv_hbm, o0_ref, par_ref, pz_hbm, wo_hbm, *refs
):
    oz_ref, x1_ref, a2_ref, qkv, o, pz, wo, sems = refs[-8:]
    copies = Copies(sems)
    first = copies.start(qkv_hbm.at[pl.ds(LEN, LEN), :], qkv)
    second = [copies.start(pz_hbm, pz), copies.start(wo_hbm, wo)]
    o[:LEN, :] = o0_ref[...]
    first.wait()
    attend(lens_ref, 1, qkv, slice(0, LEN), o, slice(LEN, ROWS))
    wait(second)
    par = par_ref[...]
    oz = pick(o[...], pz[...])
    oz_ref[:HALF, :] = oz[:HALF]
    oz_ref[HALF:, :] = oz[LEN : LEN + HALF]
    x1 = x_ref[...].astype(F32) + dot(oz, wo[...]) + par[5:6]
    hat, _ = norm_stats(x1)
    a2 = (hat * par[1:2] + par[6:7]).astype(B16)
    for cell in range(2):
        for half in range(2):
            src = slice(cell * LEN + half * HALF, cell * LEN + (half + 1) * HALF)
            dst = slice(half * LEN + cell * HALF, half * LEN + (cell + 1) * HALF)
            x1_ref[dst, :] = x1[src]
            a2_ref[dst, :] = a2[src]


def ffn_kernel(
    offs_ref, a2_ref, x1_ref, oz_ref, pos_ref, cot_ref, par_ref, ub_ref, py_hbm, pz_hbm,
    y0, y1, y2, y3, z0, z1, z2, z3, d0, d1, d2, d3, wo_hbm,
    mixed_ref, dx1_ref, do_ref, vec_ref, left_ref, dz_ref, db_ref, ys_hbm, zs_hbm, ds_hbm, du_all, g_all,
    wy, wz, wd, wo, py, pz, gy, gz, gd, acc, sems,
):
    copies = Copies(sems)
    first = [copies.start(py_hbm, py)]
    first += load_rows(copies, (y0, y1, y2, y3), wy, pl.ds(0, Y2))
    third = []
    for i, p in enumerate((d0, d1, d2, d3)):
        for j in range(2):
            at = pl.multiple_of(offs_ref[2 * i + j] * FIRST, FIRST)
            third.append(copies.start(p.at[pl.ds(j * FIRST, FIRST), :], wd.at[pl.ds(at, FIRST), :]))
    second = [copies.start(pz_hbm, pz)]
    second += load_rows(copies, (z0, z1, z2, z3), wz, pl.ds(0, Z2))
    fourth = [copies.start(wo_hbm, wo)]
    row = lax.broadcasted_iota(jnp.int32, (HALF, 64), 0)
    dy = []
    for cell in range(2):
        hot = (row == pos_ref[cell : cell + 1, :]).astype(F32).astype(B16)
        dy.append(dot(hot, cot_ref[cell]))
    dy = jnp.concatenate(dy, axis=0)
    dz = dy.astype(B16)
    dz_ref[...] = dz
    a2 = a2_ref[...]
    wait(first)
    a2y = pick(a2, py[...])
    wait(third)
    outs, unit_sums = [], []
    da2, a2f, at = None, None, 0
    for lane, start, width in CHUNKS:
        if start == 0:
            if lane == 0:
                a2f, w, p, grad_ref = a2y, wy, py, gy
            else:
                wait(second)
                a2f, w, p, grad_ref = pick(a2, pz[...]), wz, pz, gz
            left_ref[lane] = a2f[:LEN, :FIRST]
            send = a2f[:LEN, FIRST:]
            part = None
        cols = slice(start, start + width)
        ff = slice(at, at + width)
        at += width
        u = dot(a2f, w[:, cols]) + ub_ref[:, ff]
        phi = 0.5 + 0.5 * lax.erf(u * RSQRT2)
        g = (u * phi).astype(B16)
        g_all[:, ff] = g[:LEN]
        y = dot(g, wd[ff, :])
        if lane == 0 and start == 0:
            acc[...] = y
        else:
            acc[...] += y
        top = u[:LEN]
        slope = phi[:LEN] + top * (jnp.exp(-0.5 * top * top) * RSQRT2PI)
        du = (dot(dz, wd[ff, :], 1, 1) * slope).astype(B16)
        back = dot(du, w[:, cols], 1, 1)
        part = back if part is None else part + back
        unit_sums.append(row_sum(du.astype(F32)))
        du_all[:, ff] = du
        grad_ref[:, cols] = dot(send, du, 0, 0).astype(B16)
        if start > 0:
            back = put_back(part, p[...])
            da2 = back if da2 is None else da2 + back
            if lane == 0:
                outs.append(copies.start(gy, ys_hbm))
    for i in range(4):
        cols = pl.ds(pl.multiple_of(offs_ref[4 + i] * FIRST, FIRST), FIRST)
        gd[i * FIRST : (i + 1) * FIRST, :] = dot(g_all[:, cols], dz, 0, 0).astype(B16)
    outs.append(copies.start(gd, ds_hbm))
    x1 = x1_ref[...]
    hat, scale = norm_stats(x1[:LEN])
    dx1 = dy + norm_back(da2, hat, scale, par_ref[1:2])
    dx1_ref[...] = dx1
    db = dx1.astype(B16)
    db_ref[...] = db
    left_ref[2] = oz_ref[:, :FIRST]
    gz[:, Z2:] = dot(oz_ref[:, FIRST:], db, 0, 0).astype(B16)
    outs.append(copies.start(gz, zs_hbm))
    wait(fourth)
    do_ref[...] = dot(dot(db, wo[...], 1, 1).astype(B16), pz[...], 1, 1).astype(B16)
    mixed = (x1 + acc[...] + par_ref[7:8]).astype(B16)
    for cell in range(2):
        for half in range(2):
            dst = slice(cell * LEN + half * HALF, cell * LEN + (half + 1) * HALF)
            src = slice(half * LEN + cell * HALF, half * LEN + (cell + 1) * HALF)
            mixed_ref[dst, :] = mixed[src]
    sums = jnp.concatenate(unit_sums, axis=1)
    sums = jnp.concatenate([sums[:, g * 512 : (g + 1) * 512] for g in range(6)] + [jnp.zeros((2, 512), F32)], axis=0)
    sums = dot(sums.astype(B16), by_fours())
    vec_ref[:8, :] = par_ref[...]
    vec_ref[8:9, :] = row_sum(da2 * hat)
    vec_ref[9:10, :] = row_sum(da2)
    vec_ref[10:11, :] = row_sum(dz.astype(F32))
    vec_ref[11:12, :] = row_sum(db.astype(F32))
    for q in range(4):
        vec_ref[12 + q : 13 + q, :] = jnp.concatenate(
            [sums[g : g + 1, q * 128 : (q + 1) * 128] for g in range(6)], axis=1
        )
    wait(outs)


def attention_back_kernel(lens_ref, do_ref, qkv_hbm, dq_ref, dk_ref, dv_ref, vec_ref, qkv_ref, sems):
    copies = Copies(sems)
    loads = [copies.start(qkv_hbm.at[pl.ds(c * LEN, LEN), :], qkv_ref.at[pl.ds(c * LEN, LEN), :]) for c in range(2)]
    head_lane = lax.broadcasted_iota(jnp.int32, (HALF, 128), 1) < HEAD_DIM
    key = lax.broadcasted_iota(jnp.int32, (LEN, 1), 0)
    group = 2
    for cell in range(2):
        valid = key < lens_ref[cell]
        loads[cell].wait()
        rows = slice(cell * LEN, (cell + 1) * LEN)
        firsts = slice(cell * LEN, cell * LEN + HALF)
        grads = slice(cell * HALF, (cell + 1) * HALF)
        for start in range(0, HEADS // 2, group):
            held = []
            for pair in range(start, start + group):
                at = pair * 128
                q = qkv_ref[firsts, at : at + 128] * SCALE
                k = qkv_ref[rows, D + at : D + at + 128]
                v = qkv_ref[rows, 2 * D + at : 2 * D + at + 128]
                do = do_ref[grads, at : at + 128]
                q2 = jnp.concatenate([jnp.where(head_lane, q, 0), jnp.where(head_lane, 0, q)], axis=0)
                do2 = jnp.concatenate([jnp.where(head_lane, do, 0), jnp.where(head_lane, 0, do)], axis=0)
                held.append((q2, do2, k, dot(k, q2, 1, 1), dot(v, do2, 1, 1)))
            soft = []
            for q2, do2, k, s, dp in held:
                s = jnp.where(valid, s, -1000000000.0)
                e = jnp.exp(s - jnp.max(s, axis=0, keepdims=True))
                p = e * (1.0 / jnp.sum(e, axis=0, keepdims=True))
                ds = p * (dp - jnp.sum(dp * p, axis=0, keepdims=True))
                soft.append((p.astype(B16), ds.astype(B16)))
            for i, pair in enumerate(range(start, start + group)):
                at = pair * 128
                q2, do2, k, _, _ = held[i]
                p, ds = soft[i]
                dv_ref[rows, at : at + 128] = dot(p, do2).astype(B16)
                dk_ref[rows, at : at + 128] = dot(ds, q2).astype(B16)
                dq = dot(ds, k, 0, 0) * SCALE
                dq_ref[grads, at : at + 128] = jnp.where(head_lane, dq[:HALF], dq[HALF:]).astype(B16)
    vec_ref[0:1, :] = row_sum(dq_ref[...].astype(F32))
    vec_ref[1:2, :] = row_sum(dv_ref[...].astype(F32))
    vec_ref[2:, :] = jnp.zeros((6, D), F32)


def down_other_kernel(offs_ref, g_ref, dz_ref, got_ref, keep_ref, send_ref):
    for i in range(4):
        cols = pl.ds(pl.multiple_of(offs_ref[i] * FIRST, FIRST), FIRST)
        got = got_ref[i * FIRST : (i + 1) * FIRST, :].astype(F32)
        grad = (dot(g_ref[:, cols], dz_ref[...], 0, 0) + got).astype(B16)
        out = (keep_ref, send_ref)[i // 2]
        out[i % 2 * FIRST : (i % 2 + 1) * FIRST, :] = grad


def qkv_grads(a1y_ref, a1z_ref, dq_ref, dk_ref, dv_ref, rows):
    a1y, a1z = a1y_ref[:, rows], a1z_ref[:, rows]
    a1q = jnp.concatenate([a1y[:HALF], a1y[LEN : LEN + HALF]], axis=0)
    yield 0, 0, dot(a1q, dq_ref[...], 0, 0)
    yield 0, D, dot(a1y, dk_ref[:, :384], 0, 0)
    yield 1, 0, dot(a1z, dk_ref[:, 384:], 0, 0)
    yield 1, 384, dot(a1z, dv_ref[...], 0, 0)


def qkv_grad_kernel(a1y_ref, a1z_ref, dq_ref, dk_ref, dv_ref, *refs):
    outs = refs[-2:]
    for lane, at, grad in qkv_grads(a1y_ref, a1z_ref, dq_ref, dk_ref, dv_ref, slice(FIRST, D)):
        outs[lane][:, at : at + grad.shape[1]] = grad.astype(B16)


def add_halves(outs, at, grad, got):
    grad = (grad + got.astype(F32)).astype(B16)
    cols = slice(at, at + grad.shape[1])
    outs[0][:, cols] = grad[:PIECE]
    outs[1][:, cols] = grad[PIECE:]


def other_half_kernel(
    left_ref, db_ref, du_ref, gy_ref, gz_ref, a1y_ref, a1z_ref, dq_ref, dk_ref, dv_ref, gy1_ref, gz1_ref,
    *refs,
):
    outs = refs[-4:-2], refs[-2:]
    add_halves(outs[0], 0, dot(left_ref[0], du_ref[:, :Y2], 0, 0), gy_ref[...])
    add_halves(outs[1], 0, dot(left_ref[1], du_ref[:, Y2:], 0, 0), gz_ref[:, :Z2])
    add_halves(outs[1], Z2, dot(left_ref[2], db_ref[...], 0, 0), gz_ref[:, Z2:])
    for lane, at, grad in qkv_grads(a1y_ref, a1z_ref, dq_ref, dk_ref, dv_ref, slice(0, FIRST)):
        got = (gy1_ref, gz1_ref)[lane][:, at : at + grad.shape[1]]
        add_halves(outs[lane], (Y2, Z2 + D)[lane] + at, grad, got)


def norm_grad_kernel(dq_ref, dk_ref, dv_ref, py_ref, pz_ref, wy_ref, wz_ref, *refs):
    da_ref = refs[-1]
    dz = dot(dk_ref[:, 384:], wz_ref[:, :384], 1, 1) + dot(dv_ref[...], wz_ref[:, 384:], 1, 1)
    da_ref[...] = put_back(dz, pz_ref[...])
    from_q = dot(dq_ref[...], wy_ref[:, :D], 1, 1)
    dy = dot(dk_ref[:, :384], wy_ref[:, D:], 1, 1)
    zero = jnp.zeros((HALF, D), F32)
    dy += jnp.concatenate([from_q[:HALF], zero, from_q[HALF:], zero], axis=0)
    da_ref[...] += put_back(dy, py_ref[...])


def input_grad_kernel(da_ref, x_ref, dx1_ref, vec_b_ref, vec_c_ref, py_ref, *refs):
    out_ref, ek_ref, es_ref = refs[-3:]
    hat, scale = norm_stats(x_ref[...].astype(F32))
    da = da_ref[...]
    grad = norm_back(da, hat, scale, vec_b_ref[0:1])
    for cell in range(2):
        at = cell * LEN
        out_ref[at : at + HALF, :] = grad[at : at + HALF] + dx1_ref[cell * HALF : (cell + 1) * HALF]
        out_ref[at + HALF : at + LEN, :] = grad[at + HALF : at + LEN]
    lines = [
        row_sum(da * hat), vec_b_ref[8:9], row_sum(da), vec_c_ref[0:1],
        vec_c_ref[1:2], vec_b_ref[11:12], vec_b_ref[9:10], vec_b_ref[10:11],
        vec_b_ref[12:16], jnp.zeros((116, D), F32),
    ]
    ext = dot(py_ref[...], jnp.concatenate(lines, axis=0).astype(B16), 0, 1).astype(B16)
    ek_ref[...] = ext[:FIRST]
    es_ref[...] = ext[FIRST:]


def unpack_kernel(k_ref, g1_ref, g2_ref, g3_ref, qkv_ref, out_ref, up_ref, gains_ref, biases_ref, ub_ref):
    total = k_ref[...] + g1_ref[...].astype(F32) + g2_ref[...].astype(F32) + g3_ref[...].astype(F32)
    y, z = total[:, : Y1 + Y2], total[:, Y1 + Y2 :]
    up_ref[:, :Y2] = y[:, :Y2]
    up_ref[:, Y2:] = z[:, :Z2]
    out_ref[...] = z[:, Z2 : Z2 + D]
    qkv_ref[:, :QKV] = y[:, Y2 : Y2 + QKV]
    qkv_ref[:, QKV:] = z[:, Z2 + D :]
    small = y[:, Y2 + QKV :]
    turned = small.T
    gains_ref[...] = turned[0:2]
    biases_ref[...] = turned[2:8]
    ub_ref[...] = small[:, 8:12]


def whole(kernel, outs, mib, flops, scratch=(), smem=0, hbm=(), hbm_outs=()):
    def call(*args):
        in_hbm = pl.BlockSpec(memory_space=pltpu.HBM)
        in_vmem = pl.BlockSpec(memory_space=pltpu.VMEM)
        specs = [pl.BlockSpec(memory_space=pltpu.SMEM)] * smem
        specs += [in_hbm if i in hbm else in_vmem for i in range(smem, len(args))]
        return pl.pallas_call(
            kernel,
            out_shape=outs,
            in_specs=specs,
            out_specs=[in_hbm if i in hbm_outs else in_vmem for i in range(len(outs))],
            scratch_shapes=scratch,
            compiler_params=pltpu.CompilerParams(vmem_limit_bytes=mib * 1024 * 1024),
            cost_estimate=pl.CostEstimate(flops=flops, bytes_accessed=1024, transcendentals=0),
        )(*args)

    return call


def shape(*dims, dtype=B16):
    return jax.ShapeDtypeStruct(dims, dtype)


def swap(v, axis, masks):
    pairs = []
    for flat in range(128):
        at = list(np.unravel_index(flat, SIZES))
        at[ALL.index(axis)] ^= masks[at[1]]
        pairs.append((flat, int(np.ravel_multi_index(at, SIZES))))
    return lax.ppermute(v, ALL, pairs)


NEAR, FAR, OPPOSITE, CORES = (1, 3), (3, 1), (2, 2), (1, 1)


def relative(core, own):
    even = jnp.array([0, 1, 3, 2], jnp.int32)
    odd = jnp.array([0, 3, 1, 2], jnp.int32)
    return own ^ jnp.where(core == 0, even, odd)


def positions_of(at, order):
    weight = {"x": 32, "core": 16, "y": 4, "z": 1}
    core = jnp.stack([at["core"], 1 - at["core"]])
    total = core.reshape(2, 1, 1, 1, 1) * weight["core"] * 6
    for i, axis in enumerate(order):
        dims = [2, 1, 1, 1, 1]
        dims[1 + i] = 4
        rel = jnp.stack([relative(at["core"], at[axis]), relative(1 - at["core"], at[axis])])
        total = total + rel.reshape(dims) * weight[axis] * 6
    total = total + jnp.arange(6, dtype=jnp.int32)
    return total.reshape(D)


def under(*parts):
    return jnp.concatenate(parts, axis=0)


def beside(*parts):
    return jnp.concatenate(parts, axis=1)


def quadruple(own, axis):
    return under(own, swap(own, axis, NEAR), swap(own, axis, FAR), swap(own, axis, OPPOSITE))


def tie(*arrays):
    return lax.optimization_barrier(arrays)


def doubled(own, axis):
    return under(own, swap(own, axis, NEAR))


def both_cores(near, far):
    return near, far, swap(near, "core", CORES), swap(far, "core", CORES)


def deal(parts, plane):
    return lax.all_to_all(parts, plane, 0, 0)


def plus(own, got):
    return own + got.astype(F32)


def total_of(own, got):
    return own.astype(F32) + got.astype(F32)


def halves(pairs):
    n = pairs[0][0].shape[0] // 2
    keep = beside(*[total_of(own[:n], got[:n]) for own, got in pairs])
    send = beside(*[total_of(own[n:], got[n:]).astype(B16) for own, got in pairs])
    return keep, send


def quarters(total, axis):
    n = total.shape[0] // 4
    sends = [total[i * n : (i + 1) * n].astype(B16) for i in (1, 2, 3)]
    return total[:n], [swap(v, axis, m) for v, m in zip(sends, (NEAR, FAR, OPPOSITE))]


def local(
    tokens, lengths, positions, cotangent, qkv_weight, out_weight, up_weight, down_weight,
    norm_gains, biases, up_bias,
):
    at = {a: lax.axis_index(a) for a in ALL}
    nat = jnp.stack([positions_of(at, ("y", "z", "x")), positions_of(at, ("z", "y", "x"))])
    offs = jnp.concatenate([relative(core, at["x"]) * 2 + core for core in (at["core"], 1 - at["core"])])

    yz, down = whole(pack_kernel, [shape(6, Y1 + Y2 + Z1 + Z2), shape(16, 24, D)], 60, 1_000)(
        qkv_weight, out_weight, up_weight, down_weight, norm_gains, biases, up_bias.reshape(1, 24)
    )
    yz = quadruple(yz, "x")
    down = deal(down, ("y", "z")).reshape(FIRST, D)
    y = quadruple(yz[:, : Y1 + Y2], "z")
    z = quadruple(yz[:, Y1 + Y2 :], "y")
    y1, z1, y2, z2 = y[:, :Y1], z[:, :Z1], y[:, Y1:], z[:, Z1:]
    down, _, _ = tie(down, y1, z1)
    near_y, near_z = doubled(y1, "y"), doubled(z1, "z")
    far_y, far_z = swap(near_y, "y", FAR), swap(near_z, "z", FAR)
    near_x = doubled(down, "x")
    near_x, _, _ = tie(near_x, near_y, near_z)
    far_x = swap(near_x, "x", FAR)
    got_y2, got_z2 = swap(y2, "y", NEAR), swap(z2, "z", NEAR)
    yg1, zg1 = both_cores(near_y, far_y), both_cores(near_z, far_z)
    got_y2, got_z2, _, _, _ = tie(got_y2, got_z2, near_y, near_z, near_x)
    near_y2, near_z2 = under(y2, got_y2), under(z2, got_z2)
    far_y2, far_z2 = swap(near_y2, "y", FAR), swap(near_z2, "z", FAR)

    x = tokens.reshape(ROWS, D)
    dma = pltpu.SemaphoreType.DMA
    a1y, a1z, qkv, o0, par, ub, py, pz, wy, wz, wo = whole(
        first_attention_kernel,
        [shape(ROWS, D), shape(ROWS, D), shape(ROWS, 3 * D), shape(LEN, D), shape(8, D, dtype=F32),
         shape(1, FF, dtype=F32), shape(D, D), shape(D, D), shape(D, QKV), shape(D, QKV), shape(D, D)],
        60, 1_000, smem=1, hbm=range(3, 14), hbm_outs=range(6, 11),
        scratch=[pltpu.VMEM((D, Y1), B16), pltpu.VMEM((D, Z1), B16), pltpu.VMEM((D, D), B16),
                 pltpu.VMEM((D, D), B16), dma((13,))],
    )(lengths, x, nat, *yg1, *zg1, near_y2, near_z2, near_x)
    far_x, o0 = tie(far_x, o0)
    down = both_cores(near_x, far_x)
    oz, x1, a2 = whole(
        second_attention_kernel,
        [shape(LEN, D), shape(ROWS, D, dtype=F32), shape(ROWS, D)],
        60, 1_000, smem=1, hbm=(2, 5, 6),
        scratch=[pltpu.VMEM((LEN, 3 * D), B16), pltpu.VMEM((ROWS, D), B16), pltpu.VMEM((D, D), B16),
                 pltpu.VMEM((D, D), B16), dma((3,))],
    )(lengths, x, qkv, o0, par, pz, wo)
    far_y2, far_z2, a2 = tie(far_y2, far_z2, a2)
    yg2, zg2 = both_cores(near_y2, far_y2), both_cores(near_z2, far_z2)

    mixed, dx1, do, vec_b, left, dz, db, ys2, zs2, xs2, du, g = whole(
        ffn_kernel,
        [shape(ROWS, D), shape(LEN, D, dtype=F32), shape(LEN, D), shape(16, D, dtype=F32),
         shape(3, LEN, FIRST), shape(LEN, D), shape(LEN, D),
         shape(FIRST, Y2), shape(FIRST, Z2 + D), shape(1536, D), shape(LEN, FF), shape(LEN, FF)],
        60, 1_000, smem=1, hbm=range(8, 23), hbm_outs=range(7, 10),
        scratch=[pltpu.VMEM((D, Y2), B16), pltpu.VMEM((D, Z2), B16), pltpu.VMEM((FF, D), B16), pltpu.VMEM((D, D), B16),
                 pltpu.VMEM((D, D), B16), pltpu.VMEM((D, D), B16), pltpu.VMEM((FIRST, Y2), B16),
                 pltpu.VMEM((FIRST, Z2 + D), B16), pltpu.VMEM((1536, D), B16), pltpu.VMEM((ROWS, D), F32), dma((28,))],
    )(offs, a2, x1, oz, positions, cotangent, par, ub, py, pz, *yg2, *zg2, *down, wo)

    got_x, got_y, got_z = swap(xs2, "core", CORES), swap(ys2, "core", CORES), swap(zs2, "core", CORES)
    dq, dk, dv, vec_c = whole(
        attention_back_kernel,
        [shape(LEN, D), shape(ROWS, D), shape(ROWS, D), shape(8, D, dtype=F32)],
        20, 1_000, smem=1, hbm=(2,), scratch=[pltpu.VMEM((ROWS, 3 * D), B16), dma((2,))],
    )(lengths, do, qkv)
    ys1, zs1 = whole(qkv_grad_kernel, [shape(FIRST, QKV), shape(FIRST, QKV)], 14, 1_000)(a1y, a1z, dq, dk, dv)
    got_y1, got_z1 = swap(ys1, "core", CORES), swap(zs1, "core", CORES)
    xk, xs = whole(down_other_kernel, [shape(D, D), shape(D, D)], 14, 1_000, smem=1)(offs, g, dz, got_x)
    got_x = swap(xs, "x", FAR)
    yk, ys, zk, zs = whole(
        other_half_kernel,
        [shape(PIECE, QKV + Y2), shape(PIECE, QKV + Y2), shape(PIECE, Z1 + Z2), shape(PIECE, Z1 + Z2)],
        24, 1_000, hbm=(12,),
    )(left, db, du, got_y, got_z, a1y, a1z, dq, dk, dv, got_y1, got_z1, xs)
    got_y, got_z = swap(ys, "y", FAR), swap(zs, "z", FAR)
    (da,) = whole(norm_grad_kernel, [shape(ROWS, D, dtype=F32)], 28, 1_000, hbm=(7, 8))(
        dq, dk, dv, py, pz, wy, wz, ys, zs
    )
    da, got_y, got_z = tie(da, got_y, got_z)
    token_grad, ek, es = whole(
        input_grad_kernel,
        [shape(ROWS, D, dtype=F32), shape(FIRST, 128), shape(FIRST, 128)],
        24, 1_000,
    )(da, x, dx1, vec_b, vec_c, py)
    ek, es = halves([(ek, swap(es, "core", CORES))])
    got_e = swap(es, "y", FAR)

    zk, zs = halves([(zk, got_z)])
    got_z = swap(zs, "z", NEAR)
    yk, ys = halves([(yk, got_y)])
    got_y = swap(ys, "y", NEAR)
    xk, xs = halves([(xk, got_x)])
    got_x = swap(xs, "x", NEAR)
    ek, es = halves([(ek, got_e)])
    got_e = swap(es, "y", NEAR)
    down = deal(total_of(xk, got_x).astype(B16).reshape(16, 24, D), ("y", "z"))
    down_grad = jnp.sum(down.astype(F32), axis=0)
    zk, gots_z = quarters(total_of(zk, got_z), "y")
    yk, gots_y = quarters(beside(total_of(yk, got_y), total_of(ek, got_e)), "z")
    total = beside(sum([v.astype(F32) for v in gots_y], yk), sum([v.astype(F32) for v in gots_z], zk))
    keep, gots = quarters(total, "x")
    qkv_grad, out_grad, up_grad, gains_grad, biases_grad, ub_grad = whole(
        unpack_kernel,
        [shape(6, 3 * D, dtype=F32), shape(6, D, dtype=F32), shape(6, FF, dtype=F32), shape(2, 6, dtype=F32),
         shape(6, 6, dtype=F32), shape(6, 4, dtype=F32)],
        8, 1_000,
    )(keep, *gots)
    return (
        mixed.reshape(2, LEN, D), token_grad.reshape(2, LEN, D), qkv_grad, out_grad, up_grad, down_grad,
        gains_grad, biases_grad, ub_grad.reshape(24),
    )


def solution(mesh):
    fine = Mesh(mesh.devices.reshape(SIZES), ALL)
    rows = lambda n: P(ALL, *([None] * (n - 1)))
    cols = P(None, ALL)
    in_specs = (rows(3), rows(1), rows(2), rows(3), rows(2), rows(2), rows(2), rows(2), cols, cols, rows(1))
    out_specs = (rows(3), rows(3), rows(2), rows(2), rows(2), rows(2), cols, cols, rows(1))
    return jax.shard_map(local, mesh=fine, in_specs=in_specs, out_specs=out_specs, check_vma=False)
```

```python
import functools

import jax
import jax.numpy as jnp
import numpy as np
from jax import lax
from jax.experimental import pallas as pl
from jax.experimental.pallas import tpu as pltpu
from jax.sharding import Mesh, PartitionSpec as P

B16 = jnp.bfloat16
F32 = jnp.float32
HEADS = 12
HEAD_DIM = 64
D = 768
FF = 3072
LEN = 256
HALF = 128
ROWS = 512
PIECE = 192
FIRST = 384
Y1, Y2, Z1, Z2 = 1280, 1792, 1920, 1280
QKV = 1152
ORDER_Y, ORDER_Z = ((2, 4), (3, 1), (0, 32)), ((3, 1), (2, 4), (0, 32))
CHUNKS = ((0, 0, 896), (0, 896, 896), (1, 0, 640), (1, 640, 640))
SCALE = HEAD_DIM**-0.5
ALL = ("x", "core", "y", "z")
SIZES = (4, 2, 4, 4)
RSQRT2 = 0.5**0.5
RSQRT2PI = (2.0 * np.pi) ** -0.5


def dot(a, b, ca=1, cb=0):
    return lax.dot_general(a, b, (((ca,), (cb,)), ((), ())), preferred_element_type=F32)


def pick(a, p):
    return dot(a, p).astype(B16)


def put_back(a, p):
    return dot(a.astype(B16), p, 1, 1)


def norm_stats(v):
    centered = v - jnp.mean(v, axis=-1, keepdims=True)
    variance = jnp.mean(centered * centered, axis=-1, keepdims=True)
    scale = lax.rsqrt(variance + 1e-05)
    return centered * scale, scale


def norm_back(grad, hat, scale, gain):
    g = grad * gain
    mean_g = jnp.mean(g, axis=-1, keepdims=True)
    mean_gh = jnp.mean(g * hat, axis=-1, keepdims=True)
    return scale * (g - mean_g - hat * mean_gh)


def row_sum(v):
    return jnp.sum(v, axis=0, keepdims=True)


def softmax_of(q_one, k_two, valid):
    s = jnp.where(valid, dot(q_one, k_two, 1, 1), -1000000000.0)
    e = jnp.exp(s - jnp.max(s, axis=-1, keepdims=True))
    return e / jnp.sum(e, axis=-1, keepdims=True)


class Copies:
    def __init__(self, sems):
        self.sems, self.used = sems, 0

    def start(self, src, dst):
        copy = pltpu.make_async_copy(src, dst, self.sems.at[self.used])
        self.used += 1
        copy.start()
        return copy


def wait(copies):
    for copy in copies:
        copy.wait()


def load_rows(copies, pieces, dst, cols):
    return [
        copies.start(p.at[:, cols], dst.at[pl.ds(i * PIECE, PIECE), :]) for i, p in enumerate(pieces)
    ]


def pack_kernel(qkv_ref, out_ref, up_ref, down_ref, gains_ref, biases_ref, ub_ref, yz_ref, deal_ref):
    vecs = jnp.concatenate([gains_ref[...], biases_ref[...]], axis=0)
    eye = lax.broadcasted_iota(jnp.int32, (8, 128), 0) == lax.broadcasted_iota(jnp.int32, (8, 128), 1)
    ext = dot(vecs, eye.astype(F32).astype(B16), 0, 0)
    wide = jnp.broadcast_to(ub_ref[...].astype(F32), (6, 24)).astype(B16)
    unit = lax.broadcasted_iota(jnp.int32, (6, 24), 1)
    mine = unit // 4 == lax.broadcasted_iota(jnp.int32, (6, 24), 0)
    shift = lax.broadcasted_iota(jnp.int32, (24, 128), 0) % 4 + 8
    shift = shift == lax.broadcasted_iota(jnp.int32, (24, 128), 1)
    ub = dot(jnp.where(mine, wide, 0), shift.astype(F32).astype(B16))
    at = 0
    for part in (
        qkv_ref[:, :QKV], (ext + ub).astype(B16), up_ref[:, :Y2],
        qkv_ref[:, QKV:], out_ref[...], up_ref[:, Y2:],
    ):
        yz_ref[:, at : at + part.shape[1]] = part
        at += part.shape[1]
    for i in range(16):
        deal_ref[i] = down_ref[...]


def by_fours():
    row = lax.broadcasted_iota(jnp.int32, (512, 512), 0)
    col = lax.broadcasted_iota(jnp.int32, (512, 512), 1)
    return (row == col % 128 * 4 + col // 128).astype(F32).astype(B16)


def turned(step, core):
    gray = step ^ (step >> 1)
    return gray ^ ((gray & 1) * 2 * core)


def one_hot_of(at_ref, order):
    position = lax.broadcasted_iota(jnp.int32, (1, D), 1)
    device = (position * 10923) >> 16
    core = at_ref[1] ^ (device >> 6)
    total = core * 16
    for i, (axis, weight) in enumerate(order):
        total += (at_ref[axis] ^ turned((device >> (4 - 2 * i)) & 3, core)) * weight
    row = lax.broadcasted_iota(jnp.int32, (D, D), 0)
    return (row == total * 6 + position - device * 6).astype(F32).astype(B16)


def block_of(at_ref, half, i):
    core = at_ref[1] ^ half
    return (at_ref[0] ^ turned(i, core)) * 2 + core


def attend(lens_ref, cell, q_ref, kv_ref, o_ref):
    head_lane = lax.broadcasted_iota(jnp.int32, (LEN, 128), 1) < HEAD_DIM
    valid = lax.broadcasted_iota(jnp.int32, (1, LEN), 1) < lens_ref[cell]
    rows = slice(cell * LEN, (cell + 1) * LEN)
    group = 3
    for start in range(0, HEADS // 2, group):
        scores, probs = [], []
        for pair in range(start, start + group):
            at = pair * 128
            q = q_ref[rows, at : at + 128] * SCALE
            both = jnp.concatenate([jnp.where(head_lane, q, 0), jnp.where(head_lane, 0, q)], axis=0)
            scores.append(dot(both, kv_ref[rows, at : at + 128], 1, 1))
        for s in scores:
            s = jnp.where(valid, s, -1000000000.0)
            e = jnp.exp(s - jnp.max(s, axis=-1, keepdims=True))
            probs.append((e * (1.0 / jnp.sum(e, axis=-1, keepdims=True))).astype(B16))
        for i, pair in enumerate(range(start, start + group)):
            at = pair * 128
            o = dot(probs[i], kv_ref[rows, D + at : D + at + 128])
            o_ref[rows, at : at + 128] = jnp.where(head_lane, o[:LEN], o[LEN:]).astype(B16)


def half_rows(v, half):
    at = half * HALF
    return jnp.concatenate([v[at : at + HALF], v[LEN + at : LEN + at + HALF]], axis=0)


def attention_kernel(lens_ref, at_ref, x_ref, y0, y1, y2, y3, z0, z1, z2, z3, *refs):
    (a1y_hbm, a1z_hbm, kv_hbm, q_out, oz_ref, x1_ref, a2_ref, par_ref, ub_ref,
     py_hbm, pz_hbm, wy_hbm, wz_hbm, wo_hbm) = refs[-24:-10]
    wy, wz, py, pz, a1y_ref, a1z_ref, kv_ref, q_ref, o_ref, sems = refs[-10:]
    copies = Copies(sems)
    first = []
    for i, p in enumerate((y0, y1, y2, y3)):
        first.append(copies.start(p, wy.at[pl.ds(i * PIECE, PIECE), :]))
    second = []
    for i, p in enumerate((z0, z1, z2, z3)):
        second.append(copies.start(p, wz.at[pl.ds(i * PIECE, PIECE), :]))
    py[...] = one_hot_of(at_ref, ORDER_Y)
    pz[...] = one_hot_of(at_ref, ORDER_Z)
    outs = [copies.start(py, py_hbm), copies.start(pz, pz_hbm)]
    x = x_ref[...].astype(F32)
    hat, _ = norm_stats(x)
    wait(first)
    outs.append(copies.start(wy.at[:, pl.ds(0, QKV)], wy_hbm))
    par = dot(wy[:, QKV:Y1], py[...], 0, 1)
    par_ref[...] = par[:8]
    units = [jnp.concatenate([par[8 + q : 9 + q, g * 128 : (g + 1) * 128] for q in range(4)], axis=1) for g in range(6)]
    units = dot(jnp.concatenate(units + units[:2], axis=0).astype(B16), by_fours(), 1, 1)
    for g in range(6):
        ub_ref[:, g * 512 : (g + 1) * 512] = units[g : g + 1]
    a1 = (hat * par[0:1] + par[2:3]).astype(B16)
    a1y = pick(a1, py[...])
    a1y_ref[...] = a1y
    outs.append(copies.start(a1y_ref, a1y_hbm))
    qk = dot(a1y, wy[:, :QKV])
    q = (qk[:, :D] + par[3:4]).astype(B16)
    q_ref[...] = q
    q_out[...] = half_rows(q, 0)
    kv_ref[:, :384] = qk[:, D:].astype(B16)
    wait(second)
    outs.append(copies.start(wz.at[:, pl.ds(0, QKV)], wz_hbm))
    outs.append(copies.start(wz.at[:, pl.ds(QKV, D)], wo_hbm))
    a1z = pick(a1, pz[...])
    a1z_ref[...] = a1z
    outs.append(copies.start(a1z_ref, a1z_hbm))
    kv = dot(a1z, wz[:, :QKV])
    kv_ref[:, 384:D] = kv[:, :384].astype(B16)
    kv_ref[:, D:] = (kv[:, 384:] + par[4:5]).astype(B16)
    outs.append(copies.start(kv_ref, kv_hbm))
    attend(lens_ref, 0, q_ref, kv_ref, o_ref)
    attend(lens_ref, 1, q_ref, kv_ref, o_ref)
    oz = pick(o_ref[...], pz[...])
    oz_ref[...] = half_rows(oz, 0)
    x1 = x + dot(oz, wz[:, QKV:Z1]) + par[5:6]
    hat, _ = norm_stats(x1)
    a2 = (hat * par[1:2] + par[6:7]).astype(B16)
    for half in range(2):
        rows = slice(half * LEN, (half + 1) * LEN)
        x1_ref[rows, :] = half_rows(x1, half)
        a2_ref[rows, :] = half_rows(a2, half)
    wait(outs)


def load_down(copies, at_ref, pieces, wd):
    started = []
    for i, p in enumerate(pieces):
        for j in range(2):
            at = pl.multiple_of(block_of(at_ref, i // 2, 2 * (i % 2) + j) * FIRST, FIRST)
            started.append(copies.start(p.at[pl.ds(j * FIRST, FIRST), :], wd.at[pl.ds(at, FIRST), :]))
    return started


def ffn_kernel(
    at_ref, a2_ref, x1_hbm, oz_hbm, pos_ref, cot_ref, par_ref, ub_ref, py_hbm, pz_hbm,
    y0, y1, y2, y3, z0, z1, z2, z3, d0, d1, d2, d3, wo_hbm,
    mixed_ref, dx1_ref, do_ref, vec_ref, left_ref, dz_ref, db_ref, ys_hbm, zs_hbm, ds_hbm, du_hbm, g_hbm,
    wy, wz, wd, wo, py, pz, gy, gz, gd, du_all, g_all, x1_ref, oz_ref, sems,
):
    copies = Copies(sems)
    first = [copies.start(py_hbm, py)]
    first += load_rows(copies, (y0, y1, y2, y3), wy, pl.ds(0, Y2))
    second = [copies.start(pz_hbm, pz)]
    second += load_rows(copies, (z0, z1, z2, z3), wz, pl.ds(0, Z2))
    third = load_down(copies, at_ref, (d0, d1, d2, d3), wd)
    fourth = [copies.start(a, b) for a, b in ((x1_hbm, x1_ref), (oz_hbm, oz_ref), (wo_hbm, wo))]
    row = lax.broadcasted_iota(jnp.int32, (HALF, 64), 0)
    dy = []
    for cell in range(2):
        hot = (row == pos_ref[cell : cell + 1, :]).astype(F32).astype(B16)
        dy.append(dot(hot, cot_ref[cell]))
    dy = jnp.concatenate(dy, axis=0)
    dz = dy.astype(B16)
    dz_ref[...] = dz
    outs, unit_sums, lanes, slopes, at = [], [], [], [], 0
    for lane, start, width in CHUNKS:
        if start == 0:
            wait((first, second)[lane])
            a2 = pick(a2_ref[...], (py, pz)[lane][...])
            left_ref[lane] = a2[:LEN, :FIRST]
            lanes.append(a2[:LEN, FIRST:])
        ff = slice(at, at + width)
        at += width
        u = dot(a2, (wy, wz)[lane][:, start : start + width]) + ub_ref[:, ff]
        phi = 0.5 + 0.5 * lax.erf(u * RSQRT2)
        g_all[:, ff] = (u * phi).astype(B16)
        u = u[:LEN]
        slopes.append(phi[:LEN] + u * (jnp.exp(-0.5 * u * u) * RSQRT2PI))
    outs.append(copies.start(g_all.at[pl.ds(0, LEN), :], g_hbm))
    wait(third)
    for i in range(4):
        cols = pl.ds(pl.multiple_of(block_of(at_ref, 1, i) * FIRST, FIRST), FIRST)
        gd[i * FIRST : (i + 1) * FIRST, :] = dot(g_all[:LEN, cols], dz, 0, 0).astype(B16)
    outs.append(copies.start(gd, ds_hbm))
    da2, part, at = None, None, 0
    for (lane, start, width), slope in zip(CHUNKS, slopes):
        ff = slice(at, at + width)
        cols = slice(start, start + width)
        at += width
        du = (dot(dz, wd[ff, :], 1, 1) * slope).astype(B16)
        du_all[:, ff] = du
        back = dot(du, (wy, wz)[lane][:, cols], 1, 1)
        part = back if start == 0 else part + back
        unit_sums.append(row_sum(du.astype(F32)))
        (gy, gz)[lane][:, cols] = dot(lanes[lane], du, 0, 0).astype(B16)
        if start > 0:
            back = put_back(part, (py, pz)[lane][...])
            da2 = back if lane == 0 else da2 + back
            if lane == 0:
                outs.append(copies.start(gy, ys_hbm))
    outs.append(copies.start(du_all, du_hbm))
    wait(fourth)
    hat, scale = norm_stats(x1_ref[:LEN, :])
    dx1 = dy + norm_back(da2, hat, scale, par_ref[1:2])
    dx1_ref[...] = dx1
    db = dx1.astype(B16)
    db_ref[...] = db
    left_ref[2] = oz_ref[:, :FIRST]
    gz[:, Z2:] = dot(oz_ref[:, FIRST:], db, 0, 0).astype(B16)
    outs.append(copies.start(gz, zs_hbm))
    do_ref[...] = dot(dot(db, wo[...], 1, 1).astype(B16), pz[...], 1, 1).astype(B16)
    y = dot(g_all[...], wd[...]) + par_ref[7:8]
    for half in range(2):
        rows = slice(half * LEN, (half + 1) * LEN)
        mixed = (x1_ref[rows, :] + y[rows]).astype(B16)
        for cell in range(2):
            to = cell * LEN + half * HALF
            mixed_ref[to : to + HALF, :] = mixed[cell * HALF : (cell + 1) * HALF]
    sums = jnp.concatenate(unit_sums, axis=1)
    sums = jnp.concatenate([sums[:, g * 512 : (g + 1) * 512] for g in range(6)] + [jnp.zeros((2, 512), F32)], axis=0)
    sums = dot(sums.astype(B16), by_fours())
    vec_ref[:8, :] = par_ref[...]
    vec_ref[8:9, :] = row_sum(da2 * hat)
    vec_ref[9:10, :] = row_sum(da2)
    vec_ref[10:11, :] = row_sum(dz.astype(F32))
    vec_ref[11:12, :] = row_sum(db.astype(F32))
    for q in range(4):
        vec_ref[12 + q : 13 + q, :] = jnp.concatenate(
            [sums[g : g + 1, q * 128 : (q + 1) * 128] for g in range(6)], axis=1
        )
    wait(outs)


def attention_back_kernel(lens_ref, do_ref, q_ref, kv_hbm, dq_ref, dk_ref, dv_ref, vec_ref, kv_ref, sems):
    copies = Copies(sems)
    loads = [copies.start(kv_hbm.at[pl.ds(c * LEN, LEN), :], kv_ref.at[pl.ds(c * LEN, LEN), :]) for c in range(2)]
    head_lane = lax.broadcasted_iota(jnp.int32, (HALF, 128), 1) < HEAD_DIM
    key = lax.broadcasted_iota(jnp.int32, (LEN, 1), 0)
    group = 2
    for cell in range(2):
        valid = key < lens_ref[cell]
        loads[cell].wait()
        rows = slice(cell * LEN, (cell + 1) * LEN)
        grads = slice(cell * HALF, (cell + 1) * HALF)
        for start in range(0, HEADS // 2, group):
            held = []
            for pair in range(start, start + group):
                at = pair * 128
                q = q_ref[grads, at : at + 128] * SCALE
                k = kv_ref[rows, at : at + 128]
                v = kv_ref[rows, D + at : D + at + 128]
                do = do_ref[grads, at : at + 128]
                q2 = jnp.concatenate([jnp.where(head_lane, q, 0), jnp.where(head_lane, 0, q)], axis=0)
                do2 = jnp.concatenate([jnp.where(head_lane, do, 0), jnp.where(head_lane, 0, do)], axis=0)
                held.append((q2, do2, k, dot(k, q2, 1, 1), dot(v, do2, 1, 1)))
            soft = []
            for q2, do2, k, s, dp in held:
                s = jnp.where(valid, s, -1000000000.0)
                e = jnp.exp(s - jnp.max(s, axis=0, keepdims=True))
                p = e * (1.0 / jnp.sum(e, axis=0, keepdims=True))
                ds = p * (dp - jnp.sum(dp * p, axis=0, keepdims=True))
                soft.append((p.astype(B16), ds.astype(B16)))
            for i, pair in enumerate(range(start, start + group)):
                at = pair * 128
                q2, do2, k, _, _ = held[i]
                p, ds = soft[i]
                dv_ref[rows, at : at + 128] = dot(p, do2).astype(B16)
                dk_ref[rows, at : at + 128] = dot(ds, q2).astype(B16)
                dq = dot(ds, k, 0, 0) * SCALE
                dq_ref[grads, at : at + 128] = jnp.where(head_lane, dq[:HALF], dq[HALF:]).astype(B16)
    vec_ref[0:1, :] = row_sum(dq_ref[...].astype(F32))
    vec_ref[1:2, :] = row_sum(dv_ref[...].astype(F32))
    vec_ref[2:, :] = jnp.zeros((6, D), F32)


def down_other_kernel(at_ref, g_ref, dz_ref, got_ref, keep_ref, send_ref):
    for i in range(4):
        cols = pl.ds(pl.multiple_of(block_of(at_ref, 0, i) * FIRST, FIRST), FIRST)
        got = got_ref[i * FIRST : (i + 1) * FIRST, :].astype(F32)
        grad = (dot(g_ref[:, cols], dz_ref[...], 0, 0) + got).astype(B16)
        out = (keep_ref, send_ref)[i // 2]
        out[i % 2 * FIRST : (i % 2 + 1) * FIRST, :] = grad


def qkv_grads(a1y_ref, a1z_ref, dq_ref, dk_ref, dv_ref, rows):
    a1y, a1z = a1y_ref[:, rows], a1z_ref[:, rows]
    a1q = jnp.concatenate([a1y[:HALF], a1y[LEN : LEN + HALF]], axis=0)
    yield 0, 0, dot(a1q, dq_ref[...], 0, 0)
    yield 0, D, dot(a1y, dk_ref[:, :384], 0, 0)
    yield 1, 0, dot(a1z, dk_ref[:, 384:], 0, 0)
    yield 1, 384, dot(a1z, dv_ref[...], 0, 0)


def qkv_grad_kernel(a1y_ref, a1z_ref, dq_ref, dk_ref, dv_ref, *refs):
    outs = refs[-2:]
    for lane, at, grad in qkv_grads(a1y_ref, a1z_ref, dq_ref, dk_ref, dv_ref, slice(FIRST, D)):
        outs[lane][:, at : at + grad.shape[1]] = grad.astype(B16)


def add_halves(outs, at, grad, got):
    grad = (grad + got.astype(F32)).astype(B16)
    cols = slice(at, at + grad.shape[1])
    outs[0][:, cols] = grad[:PIECE]
    outs[1][:, cols] = grad[PIECE:]


def other_half_kernel(
    left_ref, db_ref, du_ref, gy_ref, gz_ref, a1y_ref, a1z_ref, dq_ref, dk_ref, dv_ref, gy1_ref, gz1_ref,
    *refs,
):
    outs = refs[-4:-2], refs[-2:]
    add_halves(outs[0], 0, dot(left_ref[0], du_ref[:, :Y2], 0, 0), gy_ref[...])
    add_halves(outs[1], 0, dot(left_ref[1], du_ref[:, Y2:], 0, 0), gz_ref[:, :Z2])
    add_halves(outs[1], Z2, dot(left_ref[2], db_ref[...], 0, 0), gz_ref[:, Z2:])
    for lane, at, grad in qkv_grads(a1y_ref, a1z_ref, dq_ref, dk_ref, dv_ref, slice(0, FIRST)):
        got = (gy1_ref, gz1_ref)[lane][:, at : at + grad.shape[1]]
        add_halves(outs[lane], (Y2, Z2 + D)[lane] + at, grad, got)


def input_grad_kernel(
    dq_ref, dk_ref, dv_ref, vec_b_ref, vec_c_ref, x_ref, dx1_ref, py, pz, wy, wz, *refs
):
    out_ref, ek_ref, es_ref, da_ref = refs[-4:]
    dz = dot(dk_ref[:, 384:], wz[:, :384], 1, 1) + dot(dv_ref[...], wz[:, 384:], 1, 1)
    da_ref[...] = put_back(dz, pz[...])
    from_q = dot(dq_ref[...], wy[:, :D], 1, 1)
    dy = dot(dk_ref[:, :384], wy[:, D:], 1, 1)
    zero = jnp.zeros((HALF, D), F32)
    dy += jnp.concatenate([from_q[:HALF], zero, from_q[HALF:], zero], axis=0)
    da = da_ref[...] + put_back(dy, py[...])
    hat, scale = norm_stats(x_ref[...].astype(F32))
    grad = norm_back(da, hat, scale, vec_b_ref[0:1])
    for cell in range(2):
        at = cell * LEN
        out_ref[at : at + HALF, :] = grad[at : at + HALF] + dx1_ref[cell * HALF : (cell + 1) * HALF]
        out_ref[at + HALF : at + LEN, :] = grad[at + HALF : at + LEN]
    lines = [
        row_sum(da * hat), vec_b_ref[8:9], row_sum(da), vec_c_ref[0:1],
        vec_c_ref[1:2], vec_b_ref[11:12], vec_b_ref[9:10], vec_b_ref[10:11],
        vec_b_ref[12:16], jnp.zeros((116, D), F32),
    ]
    ext = dot(py[...], jnp.concatenate(lines, axis=0).astype(B16), 0, 1).astype(B16)
    ek_ref[...] = ext[:FIRST]
    es_ref[...] = ext[FIRST:]


def unpack_kernel(k_ref, g1_ref, g2_ref, g3_ref, qkv_ref, out_ref, up_ref, gains_ref, biases_ref, ub_ref):
    total = k_ref[...] + g1_ref[...].astype(F32) + g2_ref[...].astype(F32) + g3_ref[...].astype(F32)
    y, z = total[:, : Y1 + Y2], total[:, Y1 + Y2 :]
    up_ref[:, :Y2] = y[:, :Y2]
    up_ref[:, Y2:] = z[:, :Z2]
    out_ref[...] = z[:, Z2 : Z2 + D]
    qkv_ref[:, :QKV] = y[:, Y2 : Y2 + QKV]
    qkv_ref[:, QKV:] = z[:, Z2 + D :]
    small = y[:, Y2 + QKV :]
    turned = small.T
    gains_ref[...] = turned[0:2]
    biases_ref[...] = turned[2:8]
    ub_ref[...] = small[:, 8:12]


def whole(kernel, outs, mib, flops, scratch=(), smem=0, hbm=(), hbm_outs=()):
    def call(*args):
        in_hbm = pl.BlockSpec(memory_space=pltpu.HBM)
        in_vmem = pl.BlockSpec(memory_space=pltpu.VMEM)
        specs = [pl.BlockSpec(memory_space=pltpu.SMEM)] * smem
        specs += [in_hbm if i in hbm else in_vmem for i in range(smem, len(args))]
        return pl.pallas_call(
            kernel,
            out_shape=outs,
            in_specs=specs,
            out_specs=[in_hbm if i in hbm_outs else in_vmem for i in range(len(outs))],
            scratch_shapes=scratch,
            compiler_params=pltpu.CompilerParams(vmem_limit_bytes=mib * 1024 * 1024),
            cost_estimate=pl.CostEstimate(flops=flops, bytes_accessed=1024, transcendentals=0),
        )(*args)

    return call


def shape(*dims, dtype=B16):
    return jax.ShapeDtypeStruct(dims, dtype)


def swap(v, axis, masks):
    pairs = []
    for flat in range(128):
        at = list(np.unravel_index(flat, SIZES))
        at[ALL.index(axis)] ^= masks[at[1]]
        pairs.append((flat, int(np.ravel_multi_index(at, SIZES))))
    return lax.ppermute(v, ALL, pairs)


NEAR, FAR, OPPOSITE, CORES = (1, 3), (3, 1), (2, 2), (1, 1)


def under(*parts):
    return jnp.concatenate(parts, axis=0)


def beside(*parts):
    return jnp.concatenate(parts, axis=1)


def quadruple(own, axis):
    return under(own, swap(own, axis, NEAR), swap(own, axis, FAR), swap(own, axis, OPPOSITE))


def tie(*arrays):
    return lax.optimization_barrier(arrays)


def doubled(own, axis):
    return under(own, swap(own, axis, NEAR))


def both_cores(near, far):
    return near, far, swap(near, "core", CORES), swap(far, "core", CORES)


def deal(parts, plane):
    return lax.all_to_all(parts, plane, 0, 0)


def plus(own, got):
    return own + got.astype(F32)


def total_of(own, got):
    return own.astype(F32) + got.astype(F32)


def halves(pairs):
    n = pairs[0][0].shape[0] // 2
    keep = beside(*[total_of(own[:n], got[:n]) for own, got in pairs])
    send = beside(*[total_of(own[n:], got[n:]).astype(B16) for own, got in pairs])
    return keep, send


def quarters(total):
    n = total.shape[0] // 4
    return total[:n], [total[i * n : (i + 1) * n].astype(B16) for i in (1, 2, 3)]


def exchange(sends, axis):
    return [swap(v, axis, m) for v, m in zip(sends, (NEAR, FAR, OPPOSITE))]


def local(
    tokens, lengths, positions, cotangent, qkv_weight, out_weight, up_weight, down_weight,
    norm_gains, biases, up_bias,
):
    at = jnp.stack([lax.axis_index(a) for a in ALL])

    yz, down = whole(pack_kernel, [shape(6, Y1 + Y2 + Z1 + Z2), shape(16, 24, D)], 60, 1_000)(
        qkv_weight, out_weight, up_weight, down_weight, norm_gains, biases, up_bias.reshape(1, 24)
    )
    yz = quadruple(yz, "x")
    down = deal(down, ("y", "z")).reshape(FIRST, D)
    y = quadruple(yz[:, : Y1 + Y2], "z")
    z = quadruple(yz[:, Y1 + Y2 :], "y")
    y1, z1, y2, z2 = y[:, :Y1], z[:, :Z1], y[:, Y1:], z[:, Z1:]
    down, _, _ = tie(down, y1, z1)
    near_y, near_z = doubled(y1, "y"), doubled(z1, "z")
    far_y, far_z = swap(near_y, "y", FAR), swap(near_z, "z", FAR)
    near_x = doubled(down, "x")
    near_x, _, _ = tie(near_x, near_y, near_z)
    far_x = swap(near_x, "x", FAR)
    got_y2, got_z2 = swap(y2, "y", NEAR), swap(z2, "z", NEAR)
    yg1, zg1 = both_cores(near_y, far_y), both_cores(near_z, far_z)
    other_x = swap(near_x, "core", CORES)
    got_y2, got_z2, _, _, _ = tie(got_y2, got_z2, far_y, far_z, near_x)
    near_y2, near_z2 = under(y2, got_y2), under(z2, got_z2)
    far_y2, far_z2 = swap(near_y2, "y", FAR), swap(near_z2, "z", FAR)
    other_y2 = swap(near_y2, "core", CORES)

    x = tokens.reshape(ROWS, D)
    dma = pltpu.SemaphoreType.DMA
    a1y, a1z, kv, q, oz, x1, a2, par, ub, py, pz, wy, wz, wo = whole(
        attention_kernel,
        [shape(ROWS, D), shape(ROWS, D), shape(ROWS, 2 * D), shape(LEN, D), shape(LEN, D), shape(ROWS, D, dtype=F32),
         shape(ROWS, D), shape(8, D, dtype=F32), shape(1, FF, dtype=F32),
         shape(D, D), shape(D, D), shape(D, QKV), shape(D, QKV), shape(D, D)],
        60, 1_000, smem=2, hbm=range(3, 16), hbm_outs=(0, 1, 2, 9, 10, 11, 12, 13),
        scratch=[pltpu.VMEM((D, Y1), B16), pltpu.VMEM((D, Z1), B16), pltpu.VMEM((D, D), B16),
                 pltpu.VMEM((D, D), B16), pltpu.VMEM((ROWS, D), B16), pltpu.VMEM((ROWS, D), B16),
                 pltpu.VMEM((ROWS, 2 * D), B16), pltpu.VMEM((ROWS, D), B16), pltpu.VMEM((ROWS, D), B16), dma((16,))],
    )(lengths, at, x, *yg1, *zg1, near_y2, near_z2, near_x, other_x, other_y2)
    far_x, far_y2, far_z2, a2 = tie(far_x, far_y2, far_z2, a2)
    down = (near_x, far_x, other_x, swap(far_x, "core", CORES))
    yg2 = (near_y2, far_y2, other_y2, swap(far_y2, "core", CORES))
    zg2 = both_cores(near_z2, far_z2)

    mixed, dx1, do, vec_b, left, dz, db, ys2, zs2, xs2, du, g = whole(
        ffn_kernel,
        [shape(ROWS, D), shape(LEN, D, dtype=F32), shape(LEN, D), shape(16, D, dtype=F32),
         shape(3, LEN, FIRST), shape(LEN, D), shape(LEN, D),
         shape(FIRST, Y2), shape(FIRST, Z2 + D), shape(1536, D), shape(LEN, FF), shape(LEN, FF)],
        60, 1_000, smem=1, hbm=(2, 3, *range(8, 23)), hbm_outs=range(7, 12),
        scratch=[pltpu.VMEM((D, Y2), B16), pltpu.VMEM((D, Z2), B16), pltpu.VMEM((FF, D), B16), pltpu.VMEM((D, D), B16),
                 pltpu.VMEM((D, D), B16), pltpu.VMEM((D, D), B16), pltpu.VMEM((FIRST, Y2), B16),
                 pltpu.VMEM((FIRST, Z2 + D), B16), pltpu.VMEM((1536, D), B16), pltpu.VMEM((LEN, FF), B16),
                 pltpu.VMEM((ROWS, FF), B16), pltpu.VMEM((ROWS, D), F32), pltpu.VMEM((LEN, D), B16), dma((32,))],
    )(at, a2, x1, oz, positions, cotangent, par, ub, py, pz, *yg2, *zg2, *down, wo)

    got_x, got_y, got_z = swap(xs2, "core", CORES), swap(ys2, "core", CORES), swap(zs2, "core", CORES)
    dq, dk, dv, vec_c = whole(
        attention_back_kernel,
        [shape(LEN, D), shape(ROWS, D), shape(ROWS, D), shape(8, D, dtype=F32)],
        20, 1_000, smem=1, hbm=(3,), scratch=[pltpu.VMEM((ROWS, 2 * D), B16), dma((2,))],
    )(lengths, do, q, kv)
    ys1, zs1 = whole(qkv_grad_kernel, [shape(FIRST, QKV), shape(FIRST, QKV)], 14, 1_000)(a1y, a1z, dq, dk, dv)
    got_y1, got_z1 = swap(ys1, "core", CORES), swap(zs1, "core", CORES)
    xk, xs = whole(down_other_kernel, [shape(D, D), shape(D, D)], 14, 1_000, smem=1)(at, g, dz, got_x)
    got_x = swap(xs, "x", FAR)
    yk, ys, zk, zs = whole(
        other_half_kernel,
        [shape(PIECE, QKV + Y2), shape(PIECE, QKV + Y2), shape(PIECE, Z1 + Z2), shape(PIECE, Z1 + Z2)],
        24, 1_000, hbm=(12,),
    )(left, db, du, got_y, got_z, a1y, a1z, dq, dk, dv, got_y1, got_z1, xs)
    got_y, got_z = swap(ys, "y", FAR), swap(zs, "z", FAR)
    token_grad, ek, es = whole(
        input_grad_kernel,
        [shape(ROWS, D, dtype=F32), shape(FIRST, 128), shape(FIRST, 128)],
        30, 1_000, hbm=(11, 12), scratch=[pltpu.VMEM((ROWS, D), F32)],
    )(dq, dk, dv, vec_b, vec_c, x, dx1, py, pz, wy, wz, ys, zs)
    es, got_y, got_z = tie(es, got_y, got_z)
    zk, zs = halves([(zk, got_z)])
    yk, ys = halves([(yk, got_y)])
    got_z, got_y = swap(zs, "z", NEAR), swap(ys, "y", NEAR)
    got_e, got_x, _, _ = tie(swap(es, "core", CORES), got_x, ys, zs)
    ek, es = halves([(ek, got_e)])
    got_e = swap(es, "y", FAR)
    xk, xs = halves([(xk, got_x)])
    got_x = swap(xs, "x", NEAR)
    ek, es = halves([(ek, got_e)])
    got_e = swap(es, "y", NEAR)
    zk, z_sends = quarters(total_of(zk, got_z))
    yk, y_sends = quarters(beside(total_of(yk, got_y), total_of(ek, got_e)))
    gots_z, gots_y = exchange(z_sends, "y"), exchange(y_sends, "z")
    got_x, gots_z[0], gots_y[0] = tie(got_x, gots_z[0], gots_y[0])
    down = deal(total_of(xk, got_x).astype(B16).reshape(16, 24, D), ("y", "z"))
    total = beside(sum([v.astype(F32) for v in gots_y], yk), sum([v.astype(F32) for v in gots_z], zk))
    keep, sends = quarters(total)
    down_grad = jnp.sum(down.astype(F32), axis=0)
    gots = exchange(sends, "x")
    qkv_grad, out_grad, up_grad, gains_grad, biases_grad, ub_grad = whole(
        unpack_kernel,
        [shape(6, 3 * D, dtype=F32), shape(6, D, dtype=F32), shape(6, FF, dtype=F32), shape(2, 6, dtype=F32),
         shape(6, 6, dtype=F32), shape(6, 4, dtype=F32)],
        8, 1_000,
    )(keep, *gots)
    return (
        mixed.reshape(2, LEN, D), token_grad.reshape(2, LEN, D), qkv_grad, out_grad, up_grad, down_grad,
        gains_grad, biases_grad, ub_grad.reshape(24),
    )


def solution(mesh):
    fine = Mesh(mesh.devices.reshape(SIZES), ALL)
    rows = lambda n: P(ALL, *([None] * (n - 1)))
    cols = P(None, ALL)
    in_specs = (rows(3), rows(1), rows(2), rows(3), rows(2), rows(2), rows(2), rows(2), cols, cols, rows(1))
    out_specs = (rows(3), rows(3), rows(2), rows(2), rows(2), rows(2), cols, cols, rows(1))
    return jax.shard_map(local, mesh=fine, in_specs=in_specs, out_specs=out_specs, check_vma=False)
```

```python
import functools

import jax
import jax.numpy as jnp
import numpy as np
from jax import lax
from jax.experimental import pallas as pl
from jax.experimental.pallas import tpu as pltpu
from jax.sharding import Mesh, PartitionSpec as P

B16 = jnp.bfloat16
F32 = jnp.float32
HEADS = 12
HEAD_DIM = 64
D = 768
FF = 3072
LEN = 256
HALF = 128
ROWS = 512
PIECE = 192
FIRST = 384
Y1, Y2, Z1, Z2 = 1280, 1792, 1920, 1280
QKV = 1152
ORDER_Y, ORDER_Z = ((2, 4), (3, 1), (0, 32)), ((3, 1), (2, 4), (0, 32))
CHUNKS = ((0, 0, 896), (0, 896, 896), (1, 0, 640), (1, 640, 640))
SCALE = HEAD_DIM**-0.5
ALL = ("x", "core", "y", "z")
SIZES = (4, 2, 4, 4)
RSQRT2 = 0.5**0.5
RSQRT2PI = (2.0 * np.pi) ** -0.5


def dot(a, b, ca=1, cb=0):
    return lax.dot_general(a, b, (((ca,), (cb,)), ((), ())), preferred_element_type=F32)


def pick(a, p):
    return dot(a, p).astype(B16)


def put_back(a, p):
    return dot(a.astype(B16), p, 1, 1)


def norm_stats(v):
    centered = v - jnp.mean(v, axis=-1, keepdims=True)
    variance = jnp.mean(centered * centered, axis=-1, keepdims=True)
    scale = lax.rsqrt(variance + 1e-05)
    return centered * scale, scale


def norm_back(grad, hat, scale, gain):
    g = grad * gain
    mean_g = jnp.mean(g, axis=-1, keepdims=True)
    mean_gh = jnp.mean(g * hat, axis=-1, keepdims=True)
    return scale * (g - mean_g - hat * mean_gh)


def row_sum(v):
    return jnp.sum(v, axis=0, keepdims=True)


def softmax_of(q_one, k_two, valid):
    s = jnp.where(valid, dot(q_one, k_two, 1, 1), -1000000000.0)
    e = jnp.exp(s - jnp.max(s, axis=-1, keepdims=True))
    return e / jnp.sum(e, axis=-1, keepdims=True)


class Copies:
    def __init__(self, sems):
        self.sems, self.used = sems, 0

    def start(self, src, dst):
        copy = pltpu.make_async_copy(src, dst, self.sems.at[self.used])
        self.used += 1
        copy.start()
        return copy


def wait(copies):
    for copy in copies:
        copy.wait()


def load_rows(copies, pieces, dst, cols):
    return [
        copies.start(p.at[:, cols], dst.at[pl.ds(i * PIECE, PIECE), :]) for i, p in enumerate(pieces)
    ]


def pack_kernel(qkv_ref, out_ref, up_ref, down_ref, gains_ref, biases_ref, ub_ref, yz_ref, deal_ref):
    vecs = jnp.concatenate([gains_ref[...], biases_ref[...]], axis=0)
    eye = lax.broadcasted_iota(jnp.int32, (8, 128), 0) == lax.broadcasted_iota(jnp.int32, (8, 128), 1)
    ext = dot(vecs, eye.astype(F32).astype(B16), 0, 0)
    wide = jnp.broadcast_to(ub_ref[...].astype(F32), (6, 24)).astype(B16)
    unit = lax.broadcasted_iota(jnp.int32, (6, 24), 1)
    mine = unit // 4 == lax.broadcasted_iota(jnp.int32, (6, 24), 0)
    shift = lax.broadcasted_iota(jnp.int32, (24, 128), 0) % 4 + 8
    shift = shift == lax.broadcasted_iota(jnp.int32, (24, 128), 1)
    ub = dot(jnp.where(mine, wide, 0), shift.astype(F32).astype(B16))
    at = 0
    for part in (
        qkv_ref[:, :QKV], (ext + ub).astype(B16), up_ref[:, :Y2],
        qkv_ref[:, QKV:], out_ref[...], up_ref[:, Y2:],
    ):
        yz_ref[:, at : at + part.shape[1]] = part
        at += part.shape[1]
    for i in range(16):
        deal_ref[i] = down_ref[...]


def by_fours():
    row = lax.broadcasted_iota(jnp.int32, (512, 512), 0)
    col = lax.broadcasted_iota(jnp.int32, (512, 512), 1)
    return (row == col % 128 * 4 + col // 128).astype(F32).astype(B16)


def turned(step, core):
    gray = step ^ (step >> 1)
    return gray ^ ((gray & 1) * 2 * core)


def one_hot_of(at_ref, order):
    position = lax.broadcasted_iota(jnp.int32, (1, D), 1)
    device = (position * 10923) >> 16
    core = at_ref[1] ^ (device >> 6)
    total = core * 16
    for i, (axis, weight) in enumerate(order):
        total += (at_ref[axis] ^ turned((device >> (4 - 2 * i)) & 3, core)) * weight
    row = lax.broadcasted_iota(jnp.int32, (D, D), 0)
    return (row == total * 6 + position - device * 6).astype(F32).astype(B16)


def block_of(at_ref, half, i):
    core = at_ref[1] ^ half
    return (at_ref[0] ^ turned(i, core)) * 2 + core


def attend(lens_ref, cell, q_ref, kv_ref, o_ref):
    head_lane = lax.broadcasted_iota(jnp.int32, (LEN, 128), 1) < HEAD_DIM
    valid = lax.broadcasted_iota(jnp.int32, (1, LEN), 1) < lens_ref[cell]
    rows = slice(cell * LEN, (cell + 1) * LEN)
    group = 3
    for start in range(0, HEADS // 2, group):
        scores, probs = [], []
        for pair in range(start, start + group):
            at = pair * 128
            q = q_ref[rows, at : at + 128] * SCALE
            both = jnp.concatenate([jnp.where(head_lane, q, 0), jnp.where(head_lane, 0, q)], axis=0)
            scores.append(dot(both, kv_ref[rows, at : at + 128], 1, 1))
        for s in scores:
            s = jnp.where(valid, s, -1000000000.0)
            e = jnp.exp(s - jnp.max(s, axis=-1, keepdims=True))
            probs.append((e * (1.0 / jnp.sum(e, axis=-1, keepdims=True))).astype(B16))
        for i, pair in enumerate(range(start, start + group)):
            at = pair * 128
            o = dot(probs[i], kv_ref[rows, D + at : D + at + 128])
            o_ref[rows, at : at + 128] = jnp.where(head_lane, o[:LEN], o[LEN:]).astype(B16)


def half_rows(v, half):
    at = half * HALF
    return jnp.concatenate([v[at : at + HALF], v[LEN + at : LEN + at + HALF]], axis=0)


def attention_kernel(lens_ref, at_ref, x_ref, y0, y1, y2, y3, z0, z1, z2, z3, *refs):
    (a1y_hbm, a1z_hbm, kv_hbm, q_out, oz_ref, x1_ref, a2_ref, par_ref, ub_ref,
     py_hbm, pz_hbm, wy_hbm, wz_hbm, wo_hbm) = refs[-24:-10]
    wy, wz, py, pz, a1y_ref, a1z_ref, kv_ref, q_ref, o_ref, sems = refs[-10:]
    copies = Copies(sems)
    first = []
    for i, p in enumerate((y0, y1, y2, y3)):
        first.append(copies.start(p, wy.at[pl.ds(i * PIECE, PIECE), :]))
    second = []
    for i, p in enumerate((z0, z1, z2, z3)):
        second.append(copies.start(p, wz.at[pl.ds(i * PIECE, PIECE), :]))
    py[...] = one_hot_of(at_ref, ORDER_Y)
    pz[...] = one_hot_of(at_ref, ORDER_Z)
    outs = [copies.start(py, py_hbm), copies.start(pz, pz_hbm)]
    x = x_ref[...].astype(F32)
    hat, _ = norm_stats(x)
    wait(first)
    outs.append(copies.start(wy.at[:, pl.ds(0, QKV)], wy_hbm))
    par = dot(wy[:, QKV:Y1], py[...], 0, 1)
    par_ref[...] = par[:8]
    units = [jnp.concatenate([par[8 + q : 9 + q, g * 128 : (g + 1) * 128] for q in range(4)], axis=1) for g in range(6)]
    units = dot(jnp.concatenate(units + units[:2], axis=0).astype(B16), by_fours(), 1, 1)
    for g in range(6):
        ub_ref[:, g * 512 : (g + 1) * 512] = units[g : g + 1]
    a1 = (hat * par[0:1] + par[2:3]).astype(B16)
    a1y = pick(a1, py[...])
    a1y_ref[...] = a1y
    outs.append(copies.start(a1y_ref, a1y_hbm))
    qk = dot(a1y, wy[:, :QKV])
    q = (qk[:, :D] + par[3:4]).astype(B16)
    q_ref[...] = q
    q_out[...] = half_rows(q, 0)
    kv_ref[:, :384] = qk[:, D:].astype(B16)
    wait(second)
    outs.append(copies.start(wz.at[:, pl.ds(0, QKV)], wz_hbm))
    outs.append(copies.start(wz.at[:, pl.ds(QKV, D)], wo_hbm))
    a1z = pick(a1, pz[...])
    a1z_ref[...] = a1z
    outs.append(copies.start(a1z_ref, a1z_hbm))
    kv = dot(a1z, wz[:, :QKV])
    kv_ref[:, 384:D] = kv[:, :384].astype(B16)
    kv_ref[:, D:] = (kv[:, 384:] + par[4:5]).astype(B16)
    outs.append(copies.start(kv_ref, kv_hbm))
    attend(lens_ref, 0, q_ref, kv_ref, o_ref)
    attend(lens_ref, 1, q_ref, kv_ref, o_ref)
    oz = pick(o_ref[...], pz[...])
    oz_ref[...] = half_rows(oz, 0)
    x1 = x + dot(oz, wz[:, QKV:Z1]) + par[5:6]
    hat, _ = norm_stats(x1)
    a2 = (hat * par[1:2] + par[6:7]).astype(B16)
    for half in range(2):
        rows = slice(half * LEN, (half + 1) * LEN)
        x1_ref[rows, :] = half_rows(x1, half)
        a2_ref[rows, :] = half_rows(a2, half)
    wait(outs)


def load_down(copies, at_ref, pieces, wd):
    started = []
    for i, p in enumerate(pieces):
        for j in range(2):
            at = pl.multiple_of(block_of(at_ref, i // 2, 2 * (i % 2) + j) * FIRST, FIRST)
            started.append(copies.start(p.at[pl.ds(j * FIRST, FIRST), :], wd.at[pl.ds(at, FIRST), :]))
    return started


def ffn_kernel(
    at_ref, a2_ref, x1_hbm, oz_hbm, pos_ref, cot_ref, par_ref, ub_ref, py_hbm, pz_hbm,
    y0, y1, y2, y3, z0, z1, z2, z3, d0, d1, d2, d3, wo_hbm,
    dx1_ref, do_ref, vec_ref, left_ref, dz_ref, db_ref, ys_hbm, zs_hbm, ds_hbm, du_hbm, g_hbm, wd_hbm,
    wy, wz, wd, wo, py, pz, gy, gz, gd, du_all, g_all, x1_ref, oz_ref, sems,
):
    copies = Copies(sems)
    first = [copies.start(py_hbm, py)]
    first += load_rows(copies, (y0, y1, y2, y3), wy, pl.ds(0, Y2))
    second = [copies.start(pz_hbm, pz)]
    second += load_rows(copies, (z0, z1, z2, z3), wz, pl.ds(0, Z2))
    third = load_down(copies, at_ref, (d0, d1, d2, d3), wd)
    fourth = [copies.start(a, b) for a, b in ((x1_hbm.at[pl.ds(0, LEN), :], x1_ref), (oz_hbm, oz_ref), (wo_hbm, wo))]
    row = lax.broadcasted_iota(jnp.int32, (HALF, 64), 0)
    dy = []
    for cell in range(2):
        hot = (row == pos_ref[cell : cell + 1, :]).astype(F32).astype(B16)
        dy.append(dot(hot, cot_ref[cell]))
    dy = jnp.concatenate(dy, axis=0)
    dz = dy.astype(B16)
    dz_ref[...] = dz
    outs, unit_sums, lanes, slopes, at = [], [], [], [], 0
    for lane, start, width in CHUNKS:
        if start == 0:
            wait((first, second)[lane])
            a2 = pick(a2_ref[...], (py, pz)[lane][...])
            left_ref[lane] = a2[:LEN, :FIRST]
            lanes.append(a2[:LEN, FIRST:])
        ff = slice(at, at + width)
        at += width
        u = dot(a2, (wy, wz)[lane][:, start : start + width]) + ub_ref[:, ff]
        phi = 0.5 + 0.5 * lax.erf(u * RSQRT2)
        g_all[:, ff] = (u * phi).astype(B16)
        u = u[:LEN]
        slopes.append(phi[:LEN] + u * (jnp.exp(-0.5 * u * u) * RSQRT2PI))
    outs.append(copies.start(g_all, g_hbm))
    wait(third)
    outs.append(copies.start(wd, wd_hbm))
    for i in range(4):
        cols = pl.ds(pl.multiple_of(block_of(at_ref, 1, i) * FIRST, FIRST), FIRST)
        gd[i * FIRST : (i + 1) * FIRST, :] = dot(g_all[:LEN, cols], dz, 0, 0).astype(B16)
    outs.append(copies.start(gd, ds_hbm))
    da2, part, at = None, None, 0
    for (lane, start, width), slope in zip(CHUNKS, slopes):
        ff = slice(at, at + width)
        cols = slice(start, start + width)
        at += width
        du = (dot(dz, wd[ff, :], 1, 1) * slope).astype(B16)
        du_all[:, ff] = du
        back = dot(du, (wy, wz)[lane][:, cols], 1, 1)
        part = back if start == 0 else part + back
        unit_sums.append(row_sum(du.astype(F32)))
        (gy, gz)[lane][:, cols] = dot(lanes[lane], du, 0, 0).astype(B16)
        if start > 0:
            back = put_back(part, (py, pz)[lane][...])
            da2 = back if lane == 0 else da2 + back
            if lane == 0:
                outs.append(copies.start(gy, ys_hbm))
    outs.append(copies.start(du_all, du_hbm))
    wait(fourth)
    hat, scale = norm_stats(x1_ref[...])
    dx1 = dy + norm_back(da2, hat, scale, par_ref[1:2])
    dx1_ref[...] = dx1
    db = dx1.astype(B16)
    db_ref[...] = db
    left_ref[2] = oz_ref[:, :FIRST]
    gz[:, Z2:] = dot(oz_ref[:, FIRST:], db, 0, 0).astype(B16)
    outs.append(copies.start(gz, zs_hbm))
    do_ref[...] = dot(dot(db, wo[...], 1, 1).astype(B16), pz[...], 1, 1).astype(B16)
    sums = jnp.concatenate(unit_sums, axis=1)
    sums = jnp.concatenate([sums[:, g * 512 : (g + 1) * 512] for g in range(6)] + [jnp.zeros((2, 512), F32)], axis=0)
    sums = dot(sums.astype(B16), by_fours())
    vec_ref[:8, :] = par_ref[...]
    vec_ref[8:9, :] = row_sum(da2 * hat)
    vec_ref[9:10, :] = row_sum(da2)
    vec_ref[10:11, :] = row_sum(dz.astype(F32))
    vec_ref[11:12, :] = row_sum(db.astype(F32))
    for q in range(4):
        vec_ref[12 + q : 13 + q, :] = jnp.concatenate(
            [sums[g : g + 1, q * 128 : (q + 1) * 128] for g in range(6)], axis=1
        )
    wait(outs)


def output_kernel(g_ref, wd_ref, x1_ref, vec_ref, mixed_ref):
    y = dot(g_ref[...], wd_ref[...]) + vec_ref[7:8]
    for half in range(2):
        rows = slice(half * LEN, (half + 1) * LEN)
        mixed = (x1_ref[rows, :] + y[rows]).astype(B16)
        for cell in range(2):
            to = cell * LEN + half * HALF
            mixed_ref[to : to + HALF, :] = mixed[cell * HALF : (cell + 1) * HALF]


def attention_back_kernel(lens_ref, do_ref, q_ref, kv_hbm, dq_ref, dk_ref, dv_ref, vec_ref, kv_ref, sems):
    copies = Copies(sems)
    loads = [copies.start(kv_hbm.at[pl.ds(c * LEN, LEN), :], kv_ref.at[pl.ds(c * LEN, LEN), :]) for c in range(2)]
    head_lane = lax.broadcasted_iota(jnp.int32, (HALF, 128), 1) < HEAD_DIM
    key = lax.broadcasted_iota(jnp.int32, (LEN, 1), 0)
    group = 2
    for cell in range(2):
        valid = key < lens_ref[cell]
        loads[cell].wait()
        rows = slice(cell * LEN, (cell + 1) * LEN)
        grads = slice(cell * HALF, (cell + 1) * HALF)
        for start in range(0, HEADS // 2, group):
            held = []
            for pair in range(start, start + group):
                at = pair * 128
                q = q_ref[grads, at : at + 128] * SCALE
                k = kv_ref[rows, at : at + 128]
                v = kv_ref[rows, D + at : D + at + 128]
                do = do_ref[grads, at : at + 128]
                q2 = jnp.concatenate([jnp.where(head_lane, q, 0), jnp.where(head_lane, 0, q)], axis=0)
                do2 = jnp.concatenate([jnp.where(head_lane, do, 0), jnp.where(head_lane, 0, do)], axis=0)
                held.append((q2, do2, k, dot(k, q2, 1, 1), dot(v, do2, 1, 1)))
            soft = []
            for q2, do2, k, s, dp in held:
                s = jnp.where(valid, s, -1000000000.0)
                e = jnp.exp(s - jnp.max(s, axis=0, keepdims=True))
                p = e * (1.0 / jnp.sum(e, axis=0, keepdims=True))
                ds = p * (dp - jnp.sum(dp * p, axis=0, keepdims=True))
                soft.append((p.astype(B16), ds.astype(B16)))
            for i, pair in enumerate(range(start, start + group)):
                at = pair * 128
                q2, do2, k, _, _ = held[i]
                p, ds = soft[i]
                dv_ref[rows, at : at + 128] = dot(p, do2).astype(B16)
                dk_ref[rows, at : at + 128] = dot(ds, q2).astype(B16)
                dq = dot(ds, k, 0, 0) * SCALE
                dq_ref[grads, at : at + 128] = jnp.where(head_lane, dq[:HALF], dq[HALF:]).astype(B16)
    vec_ref[0:1, :] = row_sum(dq_ref[...].astype(F32))
    vec_ref[1:2, :] = row_sum(dv_ref[...].astype(F32))
    vec_ref[2:, :] = jnp.zeros((6, D), F32)


def down_other_kernel(at_ref, g_ref, dz_ref, got_ref, keep_ref, send_ref):
    for i in range(4):
        cols = pl.ds(pl.multiple_of(block_of(at_ref, 0, i) * FIRST, FIRST), FIRST)
        got = got_ref[i * FIRST : (i + 1) * FIRST, :].astype(F32)
        grad = (dot(g_ref[:LEN, cols], dz_ref[...], 0, 0) + got).astype(B16)
        out = (keep_ref, send_ref)[i // 2]
        out[i % 2 * FIRST : (i % 2 + 1) * FIRST, :] = grad


def qkv_grads(a1y_ref, a1z_ref, dq_ref, dk_ref, dv_ref, rows):
    a1y, a1z = a1y_ref[:, rows], a1z_ref[:, rows]
    a1q = jnp.concatenate([a1y[:HALF], a1y[LEN : LEN + HALF]], axis=0)
    yield 0, 0, dot(a1q, dq_ref[...], 0, 0)
    yield 0, D, dot(a1y, dk_ref[:, :384], 0, 0)
    yield 1, 0, dot(a1z, dk_ref[:, 384:], 0, 0)
    yield 1, 384, dot(a1z, dv_ref[...], 0, 0)


def qkv_grad_kernel(a1y_ref, a1z_ref, dq_ref, dk_ref, dv_ref, *refs):
    outs = refs[-2:]
    for lane, at, grad in qkv_grads(a1y_ref, a1z_ref, dq_ref, dk_ref, dv_ref, slice(FIRST, D)):
        outs[lane][:, at : at + grad.shape[1]] = grad.astype(B16)


def add_halves(outs, at, grad, got):
    grad = (grad + got.astype(F32)).astype(B16)
    cols = slice(at, at + grad.shape[1])
    outs[0][:, cols] = grad[:PIECE]
    outs[1][:, cols] = grad[PIECE:]


def other_half_kernel(
    left_ref, db_ref, du_ref, gy_ref, gz_ref, a1y_ref, a1z_ref, dq_ref, dk_ref, dv_ref, gy1_ref, gz1_ref,
    *refs,
):
    outs = refs[-4:-2], refs[-2:]
    add_halves(outs[0], 0, dot(left_ref[0], du_ref[:, :Y2], 0, 0), gy_ref[...])
    add_halves(outs[1], 0, dot(left_ref[1], du_ref[:, Y2:], 0, 0), gz_ref[:, :Z2])
    add_halves(outs[1], Z2, dot(left_ref[2], db_ref[...], 0, 0), gz_ref[:, Z2:])
    for lane, at, grad in qkv_grads(a1y_ref, a1z_ref, dq_ref, dk_ref, dv_ref, slice(0, FIRST)):
        got = (gy1_ref, gz1_ref)[lane][:, at : at + grad.shape[1]]
        add_halves(outs[lane], (Y2, Z2 + D)[lane] + at, grad, got)


def input_grad_kernel(
    dq_ref, dk_ref, dv_ref, vec_b_ref, vec_c_ref, x_ref, dx1_ref, py, pz, wy, wz, *refs
):
    out_ref, ek_ref, es_ref, da_ref = refs[-4:]
    dz = dot(dk_ref[:, 384:], wz[:, :384], 1, 1) + dot(dv_ref[...], wz[:, 384:], 1, 1)
    da_ref[...] = put_back(dz, pz[...])
    from_q = dot(dq_ref[...], wy[:, :D], 1, 1)
    dy = dot(dk_ref[:, :384], wy[:, D:], 1, 1)
    zero = jnp.zeros((HALF, D), F32)
    dy += jnp.concatenate([from_q[:HALF], zero, from_q[HALF:], zero], axis=0)
    da = da_ref[...] + put_back(dy, py[...])
    hat, scale = norm_stats(x_ref[...].astype(F32))
    grad = norm_back(da, hat, scale, vec_b_ref[0:1])
    for cell in range(2):
        at = cell * LEN
        out_ref[at : at + HALF, :] = grad[at : at + HALF] + dx1_ref[cell * HALF : (cell + 1) * HALF]
        out_ref[at + HALF : at + LEN, :] = grad[at + HALF : at + LEN]
    lines = [
        row_sum(da * hat), vec_b_ref[8:9], row_sum(da), vec_c_ref[0:1],
        vec_c_ref[1:2], vec_b_ref[11:12], vec_b_ref[9:10], vec_b_ref[10:11],
        vec_b_ref[12:16], jnp.zeros((116, D), F32),
    ]
    ext = dot(py[...], jnp.concatenate(lines, axis=0).astype(B16), 0, 1).astype(B16)
    ek_ref[...] = ext[:FIRST]
    es_ref[...] = ext[FIRST:]


def unpack_kernel(k_ref, g1_ref, g2_ref, g3_ref, qkv_ref, out_ref, up_ref, gains_ref, biases_ref, ub_ref):
    total = k_ref[...] + g1_ref[...].astype(F32) + g2_ref[...].astype(F32) + g3_ref[...].astype(F32)
    y, z = total[:, : Y1 + Y2], total[:, Y1 + Y2 :]
    up_ref[:, :Y2] = y[:, :Y2]
    up_ref[:, Y2:] = z[:, :Z2]
    out_ref[...] = z[:, Z2 : Z2 + D]
    qkv_ref[:, :QKV] = y[:, Y2 : Y2 + QKV]
    qkv_ref[:, QKV:] = z[:, Z2 + D :]
    small = y[:, Y2 + QKV :]
    turned = small.T
    gains_ref[...] = turned[0:2]
    biases_ref[...] = turned[2:8]
    line = jnp.concatenate([small[:, 8:12]] * 6, axis=1)
    mine = lax.broadcasted_iota(jnp.int32, (6, 24), 1) // 4 == lax.broadcasted_iota(jnp.int32, (6, 24), 0)
    ub_ref[...] = row_sum(jnp.where(mine, line, 0.0))


def whole(kernel, outs, mib, flops, scratch=(), smem=0, hbm=(), hbm_outs=()):
    def call(*args):
        in_hbm = pl.BlockSpec(memory_space=pltpu.HBM)
        in_vmem = pl.BlockSpec(memory_space=pltpu.VMEM)
        specs = [pl.BlockSpec(memory_space=pltpu.SMEM)] * smem
        specs += [in_hbm if i in hbm else in_vmem for i in range(smem, len(args))]
        return pl.pallas_call(
            kernel,
            out_shape=outs,
            in_specs=specs,
            out_specs=[in_hbm if i in hbm_outs else in_vmem for i in range(len(outs))],
            scratch_shapes=scratch,
            compiler_params=pltpu.CompilerParams(vmem_limit_bytes=mib * 1024 * 1024),
            cost_estimate=pl.CostEstimate(flops=flops, bytes_accessed=1024, transcendentals=0),
        )(*args)

    return call


def shape(*dims, dtype=B16):
    return jax.ShapeDtypeStruct(dims, dtype)


def swap(v, axis, masks):
    pairs = []
    for flat in range(128):
        at = list(np.unravel_index(flat, SIZES))
        at[ALL.index(axis)] ^= masks[at[1]]
        pairs.append((flat, int(np.ravel_multi_index(at, SIZES))))
    return lax.ppermute(v, ALL, pairs)


NEAR, FAR, OPPOSITE, CORES = (1, 3), (3, 1), (2, 2), (1, 1)


def under(*parts):
    return jnp.concatenate(parts, axis=0)


def beside(*parts):
    return jnp.concatenate(parts, axis=1)


def quadruple(own, axis):
    return under(own, swap(own, axis, NEAR), swap(own, axis, FAR), swap(own, axis, OPPOSITE))


def tie(*arrays):
    return lax.optimization_barrier(arrays)


def doubled(own, axis):
    return under(own, swap(own, axis, NEAR))


def both_cores(near, far):
    return near, far, swap(near, "core", CORES), swap(far, "core", CORES)


def deal(parts, plane):
    return lax.all_to_all(parts, plane, 0, 0)


def plus(own, got):
    return own + got.astype(F32)


def total_of(own, got):
    return own.astype(F32) + got.astype(F32)


def halves(pairs):
    n = pairs[0][0].shape[0] // 2
    keep = beside(*[total_of(own[:n], got[:n]) for own, got in pairs])
    send = beside(*[total_of(own[n:], got[n:]).astype(B16) for own, got in pairs])
    return keep, send


def quarters(total):
    n = total.shape[0] // 4
    return total[:n], [total[i * n : (i + 1) * n].astype(B16) for i in (1, 2, 3)]


def exchange(sends, axis):
    return [swap(v, axis, m) for v, m in zip(sends, (NEAR, FAR, OPPOSITE))]


def local(
    tokens, lengths, positions, cotangent, qkv_weight, out_weight, up_weight, down_weight,
    norm_gains, biases, up_bias,
):
    at = jnp.stack([lax.axis_index(a) for a in ALL])

    yz, down = whole(pack_kernel, [shape(6, Y1 + Y2 + Z1 + Z2), shape(16, 24, D)], 60, 1_000)(
        qkv_weight, out_weight, up_weight, down_weight, norm_gains, biases, up_bias.reshape(1, 24)
    )
    yz = quadruple(yz, "x")
    down = deal(down, ("y", "z")).reshape(FIRST, D)
    y = quadruple(yz[:, : Y1 + Y2], "z")
    z = quadruple(yz[:, Y1 + Y2 :], "y")
    y1, z1, y2, z2 = y[:, :Y1], z[:, :Z1], y[:, Y1:], z[:, Z1:]
    down, at, _, _ = tie(down, at, y1, z1)
    near_y, near_z = doubled(y1, "y"), doubled(z1, "z")
    far_y, far_z = swap(near_y, "y", FAR), swap(near_z, "z", FAR)
    near_x = doubled(down, "x")
    near_x, _, _ = tie(near_x, near_y, near_z)
    far_x = swap(near_x, "x", FAR)
    got_y2, got_z2 = swap(y2, "y", NEAR), swap(z2, "z", NEAR)
    yg1, zg1 = both_cores(near_y, far_y), both_cores(near_z, far_z)
    other_x = swap(near_x, "core", CORES)
    got_y2, got_z2, _, _, _ = tie(got_y2, got_z2, near_y, near_z, near_x)
    near_y2, near_z2 = under(y2, got_y2), under(z2, got_z2)
    far_y2, far_z2 = swap(near_y2, "y", FAR), swap(near_z2, "z", FAR)
    other_y2 = swap(near_y2, "core", CORES)

    x = tokens.reshape(ROWS, D)
    dma = pltpu.SemaphoreType.DMA
    a1y, a1z, kv, q, oz, x1, a2, par, ub, py, pz, wy, wz, wo = whole(
        attention_kernel,
        [shape(ROWS, D), shape(ROWS, D), shape(ROWS, 2 * D), shape(LEN, D), shape(LEN, D), shape(ROWS, D, dtype=F32),
         shape(ROWS, D), shape(8, D, dtype=F32), shape(1, FF, dtype=F32),
         shape(D, D), shape(D, D), shape(D, QKV), shape(D, QKV), shape(D, D)],
        60, 1_000, smem=2, hbm=range(3, 14), hbm_outs=(0, 1, 2, 9, 10, 11, 12, 13),
        scratch=[pltpu.VMEM((D, Y1), B16), pltpu.VMEM((D, Z1), B16), pltpu.VMEM((D, D), B16),
                 pltpu.VMEM((D, D), B16), pltpu.VMEM((ROWS, D), B16), pltpu.VMEM((ROWS, D), B16),
                 pltpu.VMEM((ROWS, 2 * D), B16), pltpu.VMEM((ROWS, D), B16), pltpu.VMEM((ROWS, D), B16), dma((16,))],
    )(lengths, at, x, *yg1, *zg1, near_y2, near_z2, near_x)
    far_x, far_y2, far_z2, a2 = tie(far_x, far_y2, far_z2, a2)
    down = (near_x, far_x, other_x, swap(far_x, "core", CORES))
    yg2 = (near_y2, far_y2, other_y2, swap(far_y2, "core", CORES))
    zg2 = both_cores(near_z2, far_z2)

    dx1, do, vec_b, left, dz, db, ys2, zs2, xs2, du, g, wd = whole(
        ffn_kernel,
        [shape(LEN, D, dtype=F32), shape(LEN, D), shape(16, D, dtype=F32),
         shape(3, LEN, FIRST), shape(LEN, D), shape(LEN, D),
         shape(FIRST, Y2), shape(FIRST, Z2 + D), shape(1536, D), shape(LEN, FF), shape(ROWS, FF), shape(FF, D)],
        60, 1_000, smem=1, hbm=(2, 3, *range(8, 23)), hbm_outs=range(6, 12),
        scratch=[pltpu.VMEM((D, Y2), B16), pltpu.VMEM((D, Z2), B16), pltpu.VMEM((FF, D), B16), pltpu.VMEM((D, D), B16),
                 pltpu.VMEM((D, D), B16), pltpu.VMEM((D, D), B16), pltpu.VMEM((FIRST, Y2), B16),
                 pltpu.VMEM((FIRST, Z2 + D), B16), pltpu.VMEM((1536, D), B16), pltpu.VMEM((LEN, FF), B16),
                 pltpu.VMEM((ROWS, FF), B16), pltpu.VMEM((LEN, D), F32), pltpu.VMEM((LEN, D), B16), dma((32,))],
    )(at, a2, x1, oz, positions, cotangent, par, ub, py, pz, *yg2, *zg2, *down, wo)

    got_x, got_y, got_z = swap(xs2, "core", CORES), swap(ys2, "core", CORES), swap(zs2, "core", CORES)
    dq, dk, dv, vec_c = whole(
        attention_back_kernel,
        [shape(LEN, D), shape(ROWS, D), shape(ROWS, D), shape(8, D, dtype=F32)],
        20, 1_000, smem=1, hbm=(3,), scratch=[pltpu.VMEM((ROWS, 2 * D), B16), dma((2,))],
    )(lengths, do, q, kv)
    ys1, zs1 = whole(qkv_grad_kernel, [shape(FIRST, QKV), shape(FIRST, QKV)], 14, 1_000)(a1y, a1z, dq, dk, dv)
    got_y1, got_z1 = swap(ys1, "core", CORES), swap(zs1, "core", CORES)
    xk, xs = whole(down_other_kernel, [shape(D, D), shape(D, D)], 14, 1_000, smem=1)(at, g, dz, got_x)
    got_x = swap(xs, "x", FAR)
    yk, ys, zk, zs = whole(
        other_half_kernel,
        [shape(PIECE, QKV + Y2), shape(PIECE, QKV + Y2), shape(PIECE, Z1 + Z2), shape(PIECE, Z1 + Z2)],
        24, 1_000, hbm=(12,),
    )(left, db, du, got_y, got_z, a1y, a1z, dq, dk, dv, got_y1, got_z1, xs)
    got_y, got_z = swap(ys, "y", FAR), swap(zs, "z", FAR)
    token_grad, ek, es = whole(
        input_grad_kernel,
        [shape(ROWS, D, dtype=F32), shape(FIRST, 128), shape(FIRST, 128)],
        30, 1_000, hbm=(11, 12), scratch=[pltpu.VMEM((ROWS, D), F32)],
    )(dq, dk, dv, vec_b, vec_c, x, dx1, py, pz, wy, wz, ys, zs)
    wd, es = tie(wd, es)
    (mixed,) = whole(output_kernel, [shape(ROWS, D)], 14, 1_000)(g, wd, x1, vec_b)
    es, mixed, got_y, got_z = tie(es, mixed, got_y, got_z)
    zk, zs = halves([(zk, got_z)])
    yk, ys = halves([(yk, got_y)])
    got_z, got_y = swap(zs, "z", NEAR), swap(ys, "y", NEAR)
    got_e, got_x, _, _ = tie(swap(es, "core", CORES), got_x, ys, zs)
    ek, es = halves([(ek, got_e)])
    got_e = swap(es, "y", FAR)
    xk, xs = halves([(xk, got_x)])
    got_x = swap(xs, "x", NEAR)
    ek, es = halves([(ek, got_e)])
    got_e = swap(es, "y", NEAR)
    zk, z_sends = quarters(total_of(zk, got_z))
    yk, y_sends = quarters(beside(total_of(yk, got_y), total_of(ek, got_e)))
    gots_z, gots_y = exchange(z_sends, "y"), exchange(y_sends, "z")
    got_x, gots_z[0], gots_y[0] = tie(got_x, gots_z[0], gots_y[0])
    down = deal(total_of(xk, got_x).astype(B16).reshape(16, 24, D), ("y", "z"))
    total = beside(sum([v.astype(F32) for v in gots_y], yk), sum([v.astype(F32) for v in gots_z], zk))
    keep, sends = quarters(total)
    down_grad = jnp.sum(down.astype(F32), axis=0)
    gots = exchange(sends, "x")
    qkv_grad, out_grad, up_grad, gains_grad, biases_grad, ub_grad = whole(
        unpack_kernel,
        [shape(6, 3 * D, dtype=F32), shape(6, D, dtype=F32), shape(6, FF, dtype=F32), shape(2, 6, dtype=F32),
         shape(6, 6, dtype=F32), shape(1, 24, dtype=F32)],
        8, 1_000,
    )(keep, *gots)
    return (
        mixed.reshape(2, LEN, D), token_grad.reshape(2, LEN, D), qkv_grad, out_grad, up_grad, down_grad,
        gains_grad, biases_grad, ub_grad.reshape(24),
    )


def solution(mesh):
    fine = Mesh(mesh.devices.reshape(SIZES), ALL)
    rows = lambda n: P(ALL, *([None] * (n - 1)))
    cols = P(None, ALL)
    in_specs = (rows(3), rows(1), rows(2), rows(3), rows(2), rows(2), rows(2), rows(2), cols, cols, rows(1))
    out_specs = (rows(3), rows(3), rows(2), rows(2), rows(2), rows(2), cols, cols, rows(1))
    return jax.shard_map(local, mesh=fine, in_specs=in_specs, out_specs=out_specs, check_vma=False)
```

```python
import functools

import jax
import jax.numpy as jnp
import numpy as np
from jax import lax
from jax.experimental import pallas as pl
from jax.experimental.pallas import tpu as pltpu
from jax.sharding import Mesh, PartitionSpec as P

B16 = jnp.bfloat16
F32 = jnp.float32
HEADS = 12
HEAD_DIM = 64
D = 768
FF = 3072
LEN = 256
HALF = 128
ROWS = 512
PIECE = 192
FIRST = 384
Y1, Y2, Z1, Z2 = 1280, 1792, 1920, 1280
QKV = 1152
ORDER_Y, ORDER_Z = ((2, 4), (3, 1), (0, 32)), ((3, 1), (2, 4), (0, 32))
CHUNKS = ((0, 0, 896), (0, 896, 896), (1, 0, 640), (1, 640, 640))
SCALE = HEAD_DIM**-0.5
ALL = ("x", "core", "y", "z")
SIZES = (4, 2, 4, 4)
RSQRT2 = 0.5**0.5
RSQRT2PI = (2.0 * np.pi) ** -0.5


def dot(a, b, ca=1, cb=0):
    return lax.dot_general(a, b, (((ca,), (cb,)), ((), ())), preferred_element_type=F32)


def pick(a, p):
    return dot(a, p).astype(B16)


def put_back(a, p):
    return dot(a.astype(B16), p, 1, 1)


def norm_stats(v):
    centered = v - jnp.mean(v, axis=-1, keepdims=True)
    variance = jnp.mean(centered * centered, axis=-1, keepdims=True)
    scale = lax.rsqrt(variance + 1e-05)
    return centered * scale, scale


def norm_back(grad, hat, scale, gain):
    g = grad * gain
    mean_g = jnp.mean(g, axis=-1, keepdims=True)
    mean_gh = jnp.mean(g * hat, axis=-1, keepdims=True)
    return scale * (g - mean_g - hat * mean_gh)


def row_sum(v):
    return jnp.sum(v, axis=0, keepdims=True)


def softmax_of(q_one, k_two, valid):
    s = jnp.where(valid, dot(q_one, k_two, 1, 1), -1000000000.0)
    e = jnp.exp(s - jnp.max(s, axis=-1, keepdims=True))
    return e / jnp.sum(e, axis=-1, keepdims=True)


class Copies:
    def __init__(self, sems):
        self.sems, self.used = sems, 0

    def start(self, src, dst):
        copy = pltpu.make_async_copy(src, dst, self.sems.at[self.used])
        self.used += 1
        copy.start()
        return copy


def wait(copies):
    for copy in copies:
        copy.wait()


def load_rows(copies, pieces, dst, cols):
    return [
        copies.start(p.at[:, cols], dst.at[pl.ds(i * PIECE, PIECE), :]) for i, p in enumerate(pieces)
    ]


def pack_kernel(qkv_ref, out_ref, up_ref, down_ref, gains_ref, biases_ref, ub_ref, yz_ref, deal_ref):
    vecs = jnp.concatenate([gains_ref[...], biases_ref[...]], axis=0)
    eye = lax.broadcasted_iota(jnp.int32, (8, 128), 0) == lax.broadcasted_iota(jnp.int32, (8, 128), 1)
    ext = dot(vecs, eye.astype(F32).astype(B16), 0, 0)
    wide = jnp.broadcast_to(ub_ref[...].astype(F32), (6, 24)).astype(B16)
    unit = lax.broadcasted_iota(jnp.int32, (6, 24), 1)
    mine = unit // 4 == lax.broadcasted_iota(jnp.int32, (6, 24), 0)
    shift = lax.broadcasted_iota(jnp.int32, (24, 128), 0) % 4 + 8
    shift = shift == lax.broadcasted_iota(jnp.int32, (24, 128), 1)
    ub = dot(jnp.where(mine, wide, 0), shift.astype(F32).astype(B16))
    at = 0
    for part in (
        qkv_ref[:, :QKV], (ext + ub).astype(B16), up_ref[:, :Y2],
        qkv_ref[:, QKV:], out_ref[...], up_ref[:, Y2:],
    ):
        yz_ref[:, at : at + part.shape[1]] = part
        at += part.shape[1]
    for i in range(16):
        deal_ref[i] = down_ref[...]


def by_fours():
    row = lax.broadcasted_iota(jnp.int32, (512, 512), 0)
    col = lax.broadcasted_iota(jnp.int32, (512, 512), 1)
    return (row == col % 128 * 4 + col // 128).astype(F32).astype(B16)


def turned(step, core):
    gray = step ^ (step >> 1)
    return gray ^ ((gray & 1) * 2 * core)


def one_hot_of(at_ref, order):
    position = lax.broadcasted_iota(jnp.int32, (1, D), 1)
    device = (position * 10923) >> 16
    core = at_ref[1] ^ (device >> 6)
    total = core * 16
    for i, (axis, weight) in enumerate(order):
        total += (at_ref[axis] ^ turned((device >> (4 - 2 * i)) & 3, core)) * weight
    row = lax.broadcasted_iota(jnp.int32, (D, D), 0)
    return (row == total * 6 + position - device * 6).astype(F32).astype(B16)


def block_of(at_ref, half, i):
    core = at_ref[1] ^ half
    return (at_ref[0] ^ turned(i, core)) * 2 + core


def attend(at_ref, cell, q_ref, kv_ref, o_ref):
    head_lane = lax.broadcasted_iota(jnp.int32, (HALF, 128), 1) < HEAD_DIM
    valid = lax.broadcasted_iota(jnp.int32, (1, LEN), 1) < at_ref[4 + cell]
    rows = slice(cell * HALF, (cell + 1) * HALF)
    keys = slice(cell * LEN, (cell + 1) * LEN)
    group = 3
    for start in range(0, HEADS // 2, group):
        scores, probs = [], []
        for pair in range(start, start + group):
            at = pair * 128
            q = q_ref[rows, at : at + 128] * SCALE
            both = jnp.concatenate([jnp.where(head_lane, q, 0), jnp.where(head_lane, 0, q)], axis=0)
            scores.append(dot(both, kv_ref[keys, at : at + 128], 1, 1))
        for s in scores:
            s = jnp.where(valid, s, -1000000000.0)
            e = jnp.exp(s - jnp.max(s, axis=-1, keepdims=True))
            probs.append((e * (1.0 / jnp.sum(e, axis=-1, keepdims=True))).astype(B16))
        for i, pair in enumerate(range(start, start + group)):
            at = pair * 128
            o = dot(probs[i], kv_ref[keys, D + at : D + at + 128])
            o_ref[rows, at : at + 128] = jnp.where(head_lane, o[:HALF], o[HALF:]).astype(B16)


def half_rows(v, half):
    at = half * HALF
    return jnp.concatenate([v[at : at + HALF], v[LEN + at : LEN + at + HALF]], axis=0)


def attention_kernel(at_ref, x_ref, y0, y1, y2, y3, z0, z1, z2, z3, *refs):
    (a1y_hbm, a1z_hbm, kv_hbm, q_ref, oz_ref, x1_ref, a2_ref, par_ref, ub_ref,
     py_hbm, pz_hbm, wy_hbm, wz_hbm, wo_hbm) = refs[-23:-9]
    wy, wz, py, pz, a1y_ref, a1z_ref, kv_ref, o_ref, sems = refs[-9:]
    copies = Copies(sems)
    first = []
    for i, p in enumerate((y0, y1, y2, y3)):
        first.append(copies.start(p, wy.at[pl.ds(i * PIECE, PIECE), :]))
    second = []
    for i, p in enumerate((z0, z1, z2, z3)):
        second.append(copies.start(p, wz.at[pl.ds(i * PIECE, PIECE), :]))
    py[...] = one_hot_of(at_ref, ORDER_Y)
    pz[...] = one_hot_of(at_ref, ORDER_Z)
    outs = [copies.start(py, py_hbm), copies.start(pz, pz_hbm)]
    x = x_ref[...].astype(F32)
    hat, _ = norm_stats(x)
    wait(first)
    outs.append(copies.start(wy.at[:, pl.ds(0, QKV)], wy_hbm))
    par = dot(wy[:, QKV:Y1], py[...], 0, 1)
    par_ref[...] = par[:8]
    units = [jnp.concatenate([par[8 + q : 9 + q, g * 128 : (g + 1) * 128] for q in range(4)], axis=1) for g in range(6)]
    units = dot(jnp.concatenate(units + units[:2], axis=0).astype(B16), by_fours(), 1, 1)
    for g in range(6):
        ub_ref[:, g * 512 : (g + 1) * 512] = units[g : g + 1]
    a1 = (hat * par[0:1] + par[2:3]).astype(B16)
    a1y = pick(a1, py[...])
    a1y_ref[...] = a1y
    outs.append(copies.start(a1y_ref, a1y_hbm))
    q_ref[...] = (dot(half_rows(a1y, 0), wy[:, :D]) + par[3:4]).astype(B16)
    kv_ref[:, :384] = dot(a1y, wy[:, D:QKV]).astype(B16)
    wait(second)
    outs.append(copies.start(wz.at[:, pl.ds(0, QKV)], wz_hbm))
    outs.append(copies.start(wz.at[:, pl.ds(QKV, D)], wo_hbm))
    a1z = pick(a1, pz[...])
    a1z_ref[...] = a1z
    outs.append(copies.start(a1z_ref, a1z_hbm))
    kv = dot(a1z, wz[:, :QKV])
    kv_ref[:, 384:D] = kv[:, :384].astype(B16)
    kv_ref[:, D:] = (kv[:, 384:] + par[4:5]).astype(B16)
    outs.append(copies.start(kv_ref, kv_hbm))
    attend(at_ref, 0, q_ref, kv_ref, o_ref)
    attend(at_ref, 1, q_ref, kv_ref, o_ref)
    oz = pick(o_ref[...], pz[...])
    oz_ref[...] = oz
    x1 = half_rows(x, 0) + dot(oz, wz[:, QKV:Z1]) + par[5:6]
    hat, _ = norm_stats(x1)
    x1_ref[...] = x1
    a2 = (hat * par[1:2] + par[6:7]).astype(B16)
    a2_ref[0] = pick(a2, py[...])
    a2_ref[1] = pick(a2, pz[...])
    wait(outs)


def later_attention_kernel(at_ref, x_ref, vec_ref, a1y_ref, kv_ref, pz_ref, wy_ref, wo_ref, *refs):
    x1_ref, a2_ref, q, o = refs[-4:]
    q[...] = (dot(half_rows(a1y_ref, 1), wy_ref[:, :D]) + vec_ref[3:4]).astype(B16)
    attend(at_ref, 0, q, kv_ref, o)
    attend(at_ref, 1, q, kv_ref, o)
    x1 = half_rows(x_ref, 1).astype(F32) + dot(pick(o[...], pz_ref[...]), wo_ref[...]) + vec_ref[5:6]
    hat, _ = norm_stats(x1)
    x1_ref[...] = x1
    a2_ref[...] = (hat * vec_ref[1:2] + vec_ref[6:7]).astype(B16)


def load_down(copies, at_ref, pieces, wd):
    started = []
    for i, p in enumerate(pieces):
        for j in range(2):
            at = pl.multiple_of(block_of(at_ref, i // 2, 2 * (i % 2) + j) * FIRST, FIRST)
            started.append(copies.start(p.at[pl.ds(j * FIRST, FIRST), :], wd.at[pl.ds(at, FIRST), :]))
    return started


def ffn_kernel(
    at_ref, a2_ref, x1_hbm, oz_hbm, pos_ref, cot_ref, par_ref, ub_ref, py_hbm, pz_hbm,
    y0, y1, y2, y3, z0, z1, z2, z3, d0, d1, d2, d3, wo_hbm, q_hbm,
    dx1_ref, pair_ref, vec_ref, left_ref, dz_ref, db_ref, ys_hbm, zs_hbm, ds_hbm, du_hbm, g_hbm, wd_hbm,
    wy, wz, wd, wo, py, pz, gy, gz, gd, du_all, g_all, x1_ref, oz_ref, sems,
):
    copies = Copies(sems)
    first = load_rows(copies, (y0, y1, y2, y3), wy, pl.ds(0, Y2))
    second = load_rows(copies, (z0, z1, z2, z3), wz, pl.ds(0, Z2))
    third = load_down(copies, at_ref, (d0, d1, d2, d3), wd)
    turns = [copies.start(py_hbm, py), copies.start(pz_hbm, pz)]
    fourth = [
        copies.start(a, b)
        for a, b in ((x1_hbm, x1_ref), (oz_hbm, oz_ref), (wo_hbm, wo), (q_hbm, pair_ref.at[0]))
    ]
    row = lax.broadcasted_iota(jnp.int32, (HALF, 64), 0)
    dy = []
    for cell in range(2):
        hot = (row == pos_ref[cell : cell + 1, :]).astype(F32).astype(B16)
        dy.append(dot(hot, cot_ref[cell]))
    dy = jnp.concatenate(dy, axis=0)
    dz = dy.astype(B16)
    dz_ref[...] = dz
    outs, unit_sums, lanes, slopes, at = [], [], [], [], 0
    for lane, start, width in CHUNKS:
        if start == 0:
            wait((first, second)[lane])
            a2 = a2_ref[lane]
            left_ref[lane] = a2[:, :FIRST]
            lanes.append(a2[:, FIRST:])
        ff = slice(at, at + width)
        at += width
        u = dot(a2, (wy, wz)[lane][:, start : start + width]) + ub_ref[:, ff]
        phi = 0.5 + 0.5 * lax.erf(u * RSQRT2)
        g_all[:, ff] = (u * phi).astype(B16)
        slopes.append(phi + u * (jnp.exp(-0.5 * u * u) * RSQRT2PI))
    outs.append(copies.start(g_all, g_hbm))
    wait(third)
    outs.append(copies.start(wd, wd_hbm))
    for i in range(4):
        cols = pl.ds(pl.multiple_of(block_of(at_ref, 1, i) * FIRST, FIRST), FIRST)
        gd[i * FIRST : (i + 1) * FIRST, :] = dot(g_all[:, cols], dz, 0, 0).astype(B16)
    outs.append(copies.start(gd, ds_hbm))
    wait(turns)
    da2, part, at = None, None, 0
    for (lane, start, width), slope in zip(CHUNKS, slopes):
        ff = slice(at, at + width)
        cols = slice(start, start + width)
        at += width
        du = (dot(dz, wd[ff, :], 1, 1) * slope).astype(B16)
        du_all[:, ff] = du
        back = dot(du, (wy, wz)[lane][:, cols], 1, 1)
        part = back if start == 0 else part + back
        unit_sums.append(row_sum(du.astype(F32)))
        (gy, gz)[lane][:, cols] = dot(lanes[lane], du, 0, 0).astype(B16)
        if start > 0:
            back = put_back(part, (py, pz)[lane][...])
            da2 = back if lane == 0 else da2 + back
            if lane == 0:
                outs.append(copies.start(gy, ys_hbm))
    outs.append(copies.start(du_all, du_hbm))
    wait(fourth)
    hat, scale = norm_stats(x1_ref[...])
    dx1 = dy + norm_back(da2, hat, scale, par_ref[1:2])
    dx1_ref[...] = dx1
    db = dx1.astype(B16)
    db_ref[...] = db
    left_ref[2] = oz_ref[:, :FIRST]
    gz[:, Z2:] = dot(oz_ref[:, FIRST:], db, 0, 0).astype(B16)
    outs.append(copies.start(gz, zs_hbm))
    pair_ref[1] = dot(dot(db, wo[...], 1, 1).astype(B16), pz[...], 1, 1).astype(B16)
    sums = jnp.concatenate(unit_sums, axis=1)
    sums = jnp.concatenate([sums[:, g * 512 : (g + 1) * 512] for g in range(6)] + [jnp.zeros((2, 512), F32)], axis=0)
    sums = dot(sums.astype(B16), by_fours())
    vec_ref[:8, :] = par_ref[...]
    vec_ref[8:9, :] = row_sum(da2 * hat)
    vec_ref[9:10, :] = row_sum(da2)
    vec_ref[10:11, :] = row_sum(dz.astype(F32))
    vec_ref[11:12, :] = row_sum(db.astype(F32))
    for q in range(4):
        vec_ref[12 + q : 13 + q, :] = jnp.concatenate(
            [sums[g : g + 1, q * 128 : (q + 1) * 128] for g in range(6)], axis=1
        )
    wait(outs)


def later_hidden_kernel(a2_ref, ub_ref, py_ref, pz_ref, y0, y1, y2, y3, z0, z1, z2, z3, *refs):
    g_ref, wy, wz = refs[-3:]
    for w, pieces in ((wy, (y0, y1, y2, y3)), (wz, (z0, z1, z2, z3))):
        for i, p in enumerate(pieces):
            w[i * PIECE : (i + 1) * PIECE, :] = p[...]
    at = 0
    for lane, start, width in CHUNKS:
        if start == 0:
            a2 = pick(a2_ref[...], (py_ref, pz_ref)[lane][...])
        ff = slice(at, at + width)
        at += width
        u = dot(a2, (wy, wz)[lane][:, start : start + width]) + ub_ref[:, ff]
        g_ref[:, ff] = (u * (0.5 + 0.5 * lax.erf(u * RSQRT2))).astype(B16)


def output_kernel(g_ref, later_g_ref, wd_ref, x1_ref, later_x1_ref, vec_ref, mixed_ref):
    for half, (g, x1) in enumerate(((g_ref, x1_ref), (later_g_ref, later_x1_ref))):
        mixed = (x1[...] + (dot(g[...], wd_ref[...]) + vec_ref[7:8])).astype(B16)
        for cell in range(2):
            to = cell * LEN + half * HALF
            mixed_ref[to : to + HALF, :] = mixed[cell * HALF : (cell + 1) * HALF]


def attention_back_kernel(at_ref, pair_ref, kv_hbm, dq_ref, dk_ref, dv_ref, vec_ref, kv_ref, sems):
    copies = Copies(sems)
    loads = [copies.start(kv_hbm.at[pl.ds(c * LEN, LEN), :], kv_ref.at[pl.ds(c * LEN, LEN), :]) for c in range(2)]
    head_lane = lax.broadcasted_iota(jnp.int32, (HALF, 128), 1) < HEAD_DIM
    key = lax.broadcasted_iota(jnp.int32, (LEN, 1), 0)
    group = 2
    for cell in range(2):
        valid = key < at_ref[4 + cell]
        loads[cell].wait()
        rows = slice(cell * LEN, (cell + 1) * LEN)
        grads = slice(cell * HALF, (cell + 1) * HALF)
        for start in range(0, HEADS // 2, group):
            held = []
            for pair in range(start, start + group):
                at = pair * 128
                q = pair_ref[0, grads, at : at + 128] * SCALE
                k = kv_ref[rows, at : at + 128]
                v = kv_ref[rows, D + at : D + at + 128]
                do = pair_ref[1, grads, at : at + 128]
                q2 = jnp.concatenate([jnp.where(head_lane, q, 0), jnp.where(head_lane, 0, q)], axis=0)
                do2 = jnp.concatenate([jnp.where(head_lane, do, 0), jnp.where(head_lane, 0, do)], axis=0)
                held.append((q2, do2, k, dot(k, q2, 1, 1), dot(v, do2, 1, 1)))
            soft = []
            for q2, do2, k, s, dp in held:
                s = jnp.where(valid, s, -1000000000.0)
                e = jnp.exp(s - jnp.max(s, axis=0, keepdims=True))
                p = e * (1.0 / jnp.sum(e, axis=0, keepdims=True))
                ds = p * (dp - jnp.sum(dp * p, axis=0, keepdims=True))
                soft.append((p.astype(B16), ds.astype(B16)))
            for i, pair in enumerate(range(start, start + group)):
                at = pair * 128
                q2, do2, k, _, _ = held[i]
                p, ds = soft[i]
                dv_ref[rows, at : at + 128] = dot(p, do2).astype(B16)
                dk_ref[rows, at : at + 128] = dot(ds, q2).astype(B16)
                dq = dot(ds, k, 0, 0) * SCALE
                dq_ref[grads, at : at + 128] = jnp.where(head_lane, dq[:HALF], dq[HALF:]).astype(B16)
    vec_ref[0:1, :] = row_sum(dq_ref[...].astype(F32))
    vec_ref[1:2, :] = row_sum(dv_ref[...].astype(F32))
    vec_ref[2:, :] = jnp.zeros((6, D), F32)


def down_other_kernel(at_ref, g_ref, dz_ref, got_ref, keep_ref, send_ref):
    for i in range(4):
        cols = pl.ds(pl.multiple_of(block_of(at_ref, 0, i) * FIRST, FIRST), FIRST)
        got = got_ref[i * FIRST : (i + 1) * FIRST, :].astype(F32)
        grad = (dot(g_ref[:, cols], dz_ref[...], 0, 0) + got).astype(B16)
        out = (keep_ref, send_ref)[i // 2]
        out[i % 2 * FIRST : (i % 2 + 1) * FIRST, :] = grad


def qkv_grads(a1y_ref, a1z_ref, dq_ref, dk_ref, dv_ref, rows):
    a1y, a1z = a1y_ref[:, rows], a1z_ref[:, rows]
    a1q = jnp.concatenate([a1y[:HALF], a1y[LEN : LEN + HALF]], axis=0)
    yield 0, 0, dot(a1q, dq_ref[...], 0, 0)
    yield 0, D, dot(a1y, dk_ref[:, :384], 0, 0)
    yield 1, 0, dot(a1z, dk_ref[:, 384:], 0, 0)
    yield 1, 384, dot(a1z, dv_ref[...], 0, 0)


def qkv_grad_kernel(a1y_ref, a1z_ref, dq_ref, dk_ref, dv_ref, *refs):
    outs = refs[-2:]
    for lane, at, grad in qkv_grads(a1y_ref, a1z_ref, dq_ref, dk_ref, dv_ref, slice(FIRST, D)):
        outs[lane][:, at : at + grad.shape[1]] = grad.astype(B16)


def add_halves(outs, at, grad, got):
    grad = (grad + got.astype(F32)).astype(B16)
    cols = slice(at, at + grad.shape[1])
    outs[0][:, cols] = grad[:PIECE]
    outs[1][:, cols] = grad[PIECE:]


def other_half_kernel(
    left_ref, db_ref, du_ref, gy_ref, gz_ref, a1y_ref, a1z_ref, dq_ref, dk_ref, dv_ref, gy1_ref, gz1_ref,
    *refs,
):
    outs = refs[-4:-2], refs[-2:]
    add_halves(outs[0], 0, dot(left_ref[0], du_ref[:, :Y2], 0, 0), gy_ref[...])
    add_halves(outs[1], 0, dot(left_ref[1], du_ref[:, Y2:], 0, 0), gz_ref[:, :Z2])
    add_halves(outs[1], Z2, dot(left_ref[2], db_ref[...], 0, 0), gz_ref[:, Z2:])
    for lane, at, grad in qkv_grads(a1y_ref, a1z_ref, dq_ref, dk_ref, dv_ref, slice(0, FIRST)):
        got = (gy1_ref, gz1_ref)[lane][:, at : at + grad.shape[1]]
        add_halves(outs[lane], (Y2, Z2 + D)[lane] + at, grad, got)


def input_grad_kernel(
    dq_ref, dk_ref, dv_ref, vec_b_ref, vec_c_ref, x_ref, dx1_ref, py, pz, wy, wz, *refs
):
    out_ref, ek_ref, es_ref, da_ref = refs[-4:]
    dz = dot(dk_ref[:, 384:], wz[:, :384], 1, 1) + dot(dv_ref[...], wz[:, 384:], 1, 1)
    da_ref[...] = put_back(dz, pz[...])
    from_q = dot(dq_ref[...], wy[:, :D], 1, 1)
    dy = dot(dk_ref[:, :384], wy[:, D:], 1, 1)
    zero = jnp.zeros((HALF, D), F32)
    dy += jnp.concatenate([from_q[:HALF], zero, from_q[HALF:], zero], axis=0)
    da = da_ref[...] + put_back(dy, py[...])
    hat, scale = norm_stats(x_ref[...].astype(F32))
    grad = norm_back(da, hat, scale, vec_b_ref[0:1])
    for cell in range(2):
        at = cell * LEN
        out_ref[at : at + HALF, :] = grad[at : at + HALF] + dx1_ref[cell * HALF : (cell + 1) * HALF]
        out_ref[at + HALF : at + LEN, :] = grad[at + HALF : at + LEN]
    lines = [
        row_sum(da * hat), vec_b_ref[8:9], row_sum(da), vec_c_ref[0:1],
        vec_c_ref[1:2], vec_b_ref[11:12], vec_b_ref[9:10], vec_b_ref[10:11],
        vec_b_ref[12:16], jnp.zeros((116, D), F32),
    ]
    ext = dot(py[...], jnp.concatenate(lines, axis=0).astype(B16), 0, 1).astype(B16)
    ek_ref[...] = ext[:FIRST]
    es_ref[...] = ext[FIRST:]


def unpack_kernel(k_ref, g1_ref, g2_ref, g3_ref, qkv_ref, out_ref, up_ref, gains_ref, biases_ref, ub_ref):
    total = k_ref[...] + g1_ref[...].astype(F32) + g2_ref[...].astype(F32) + g3_ref[...].astype(F32)
    y, z = total[:, : Y1 + Y2], total[:, Y1 + Y2 :]
    up_ref[:, :Y2] = y[:, :Y2]
    up_ref[:, Y2:] = z[:, :Z2]
    out_ref[...] = z[:, Z2 : Z2 + D]
    qkv_ref[:, :QKV] = y[:, Y2 : Y2 + QKV]
    qkv_ref[:, QKV:] = z[:, Z2 + D :]
    small = y[:, Y2 + QKV :]
    turned = small.T
    gains_ref[...] = turned[0:2]
    biases_ref[...] = turned[2:8]
    line = jnp.concatenate([small[:, 8:12]] * 6, axis=1)
    mine = lax.broadcasted_iota(jnp.int32, (6, 24), 1) // 4 == lax.broadcasted_iota(jnp.int32, (6, 24), 0)
    ub_ref[...] = row_sum(jnp.where(mine, line, 0.0))


def whole(kernel, outs, mib, flops, scratch=(), smem=0, hbm=(), hbm_outs=()):
    def call(*args):
        in_hbm = pl.BlockSpec(memory_space=pltpu.HBM)
        in_vmem = pl.BlockSpec(memory_space=pltpu.VMEM)
        specs = [pl.BlockSpec(memory_space=pltpu.SMEM)] * smem
        specs += [in_hbm if i in hbm else in_vmem for i in range(smem, len(args))]
        return pl.pallas_call(
            kernel,
            out_shape=outs,
            in_specs=specs,
            out_specs=[in_hbm if i in hbm_outs else in_vmem for i in range(len(outs))],
            scratch_shapes=scratch,
            compiler_params=pltpu.CompilerParams(vmem_limit_bytes=mib * 1024 * 1024),
            cost_estimate=pl.CostEstimate(flops=flops, bytes_accessed=1024, transcendentals=0),
        )(*args)

    return call


def shape(*dims, dtype=B16):
    return jax.ShapeDtypeStruct(dims, dtype)


def swap(v, axis, masks):
    pairs = []
    for flat in range(128):
        at = list(np.unravel_index(flat, SIZES))
        at[ALL.index(axis)] ^= masks[at[1]]
        pairs.append((flat, int(np.ravel_multi_index(at, SIZES))))
    return lax.ppermute(v, ALL, pairs)


NEAR, FAR, OPPOSITE, CORES = (1, 3), (3, 1), (2, 2), (1, 1)


def under(*parts):
    return jnp.concatenate(parts, axis=0)


def beside(*parts):
    return jnp.concatenate(parts, axis=1)


def quadruple(own, axis):
    return under(own, swap(own, axis, NEAR), swap(own, axis, FAR), swap(own, axis, OPPOSITE))


def tie(*arrays):
    return lax.optimization_barrier(arrays)


def doubled(own, axis):
    return under(own, swap(own, axis, NEAR))


def both_cores(near, far):
    return near, far, swap(near, "core", CORES), swap(far, "core", CORES)


def deal(parts, plane):
    return lax.all_to_all(parts, plane, 0, 0)


def plus(own, got):
    return own + got.astype(F32)


def total_of(own, got):
    return own.astype(F32) + got.astype(F32)


def halves(pairs):
    n = pairs[0][0].shape[0] // 2
    keep = beside(*[total_of(own[:n], got[:n]) for own, got in pairs])
    send = beside(*[total_of(own[n:], got[n:]).astype(B16) for own, got in pairs])
    return keep, send


def quarters(total):
    n = total.shape[0] // 4
    return total[:n], [total[i * n : (i + 1) * n].astype(B16) for i in (1, 2, 3)]


def exchange(sends, axis):
    return [swap(v, axis, m) for v, m in zip(sends, (NEAR, FAR, OPPOSITE))]


def local(
    tokens, lengths, positions, cotangent, qkv_weight, out_weight, up_weight, down_weight,
    norm_gains, biases, up_bias,
):
    at = jnp.concatenate([jnp.stack([lax.axis_index(a) for a in ALL]), lengths])

    yz, down = whole(pack_kernel, [shape(6, Y1 + Y2 + Z1 + Z2), shape(16, 24, D)], 60, 1_000)(
        qkv_weight, out_weight, up_weight, down_weight, norm_gains, biases, up_bias.reshape(1, 24)
    )
    yz = quadruple(yz, "x")
    down = deal(down, ("y", "z")).reshape(FIRST, D)
    y = quadruple(yz[:, : Y1 + Y2], "z")
    z = quadruple(yz[:, Y1 + Y2 :], "y")
    y1, z1, y2, z2 = y[:, :Y1], z[:, :Z1], y[:, Y1:], z[:, Z1:]
    down, at, _, _ = tie(down, at, y1, z1)
    near_y, near_z = doubled(y1, "y"), doubled(z1, "z")
    far_y, far_z = swap(near_y, "y", FAR), swap(near_z, "z", FAR)
    near_x = doubled(down, "x")
    near_x, _, _ = tie(near_x, near_y, near_z)
    far_x = swap(near_x, "x", FAR)
    got_y2, got_z2 = swap(y2, "y", NEAR), swap(z2, "z", NEAR)
    yg1, zg1 = both_cores(near_y, far_y), both_cores(near_z, far_z)
    other_x = swap(near_x, "core", CORES)
    got_y2, got_z2, _, _, _ = tie(got_y2, got_z2, near_y, near_z, near_x)
    near_y2 = under(y2, got_y2)
    other_y2 = swap(near_y2, "core", CORES)
    got_z2, other_y2 = tie(got_z2, other_y2)
    near_z2 = under(z2, got_z2)
    far_y2, far_z2 = swap(near_y2, "y", FAR), swap(near_z2, "z", FAR)

    x = tokens.reshape(ROWS, D)
    dma = pltpu.SemaphoreType.DMA
    a1y, a1z, kv, q, oz, x1, a2, par, ub, py, pz, wy, wz, wo = whole(
        attention_kernel,
        [shape(ROWS, D), shape(ROWS, D), shape(ROWS, 2 * D), shape(LEN, D), shape(LEN, D), shape(LEN, D, dtype=F32),
         shape(2, LEN, D), shape(8, D, dtype=F32), shape(1, FF, dtype=F32),
         shape(D, D), shape(D, D), shape(D, QKV), shape(D, QKV), shape(D, D)],
        60, 1_000, smem=1, hbm=range(2, 13), hbm_outs=(0, 1, 2, 9, 10, 11, 12, 13),
        scratch=[pltpu.VMEM((D, Y1), B16), pltpu.VMEM((D, Z1), B16), pltpu.VMEM((D, D), B16),
                 pltpu.VMEM((D, D), B16), pltpu.VMEM((ROWS, D), B16), pltpu.VMEM((ROWS, D), B16),
                 pltpu.VMEM((ROWS, 2 * D), B16), pltpu.VMEM((LEN, D), B16), dma((16,))],
    )(at, x, *yg1, *zg1, near_y2, near_z2, near_x)
    far_x, far_y2, far_z2, a2 = tie(far_x, far_y2, far_z2, a2)
    down = (near_x, far_x, other_x, swap(far_x, "core", CORES))
    yg2 = (near_y2, far_y2, other_y2, swap(far_y2, "core", CORES))
    zg2 = both_cores(near_z2, far_z2)

    dx1, pair, vec_b, left, dz, db, ys2, zs2, xs2, du, g, wd = whole(
        ffn_kernel,
        [shape(LEN, D, dtype=F32), shape(2, LEN, D), shape(16, D, dtype=F32),
         shape(3, LEN, FIRST), shape(LEN, D), shape(LEN, D),
         shape(FIRST, Y2), shape(FIRST, Z2 + D), shape(1536, D), shape(LEN, FF), shape(LEN, FF), shape(FF, D)],
        60, 1_000, smem=1, hbm=(2, 3, *range(8, 24)), hbm_outs=range(6, 12),
        scratch=[pltpu.VMEM((D, Y2), B16), pltpu.VMEM((D, Z2), B16), pltpu.VMEM((FF, D), B16), pltpu.VMEM((D, D), B16),
                 pltpu.VMEM((D, D), B16), pltpu.VMEM((D, D), B16), pltpu.VMEM((FIRST, Y2), B16),
                 pltpu.VMEM((FIRST, Z2 + D), B16), pltpu.VMEM((1536, D), B16), pltpu.VMEM((LEN, FF), B16),
                 pltpu.VMEM((LEN, FF), B16), pltpu.VMEM((LEN, D), F32), pltpu.VMEM((LEN, D), B16), dma((32,))],
    )(at, a2, x1, oz, positions, cotangent, par, ub, py, pz, *yg2, *zg2, *down, wo, q)

    got_x, got_y, got_z = swap(xs2, "core", CORES), swap(ys2, "core", CORES), swap(zs2, "core", CORES)
    dq, dk, dv, vec_c = whole(
        attention_back_kernel,
        [shape(LEN, D), shape(ROWS, D), shape(ROWS, D), shape(8, D, dtype=F32)],
        20, 1_000, smem=1, hbm=(2,), scratch=[pltpu.VMEM((ROWS, 2 * D), B16), dma((2,))],
    )(at, pair, kv)
    ys1, zs1 = whole(qkv_grad_kernel, [shape(FIRST, QKV), shape(FIRST, QKV)], 14, 1_000)(a1y, a1z, dq, dk, dv)
    got_y1, got_z1 = swap(ys1, "core", CORES), swap(zs1, "core", CORES)
    xk, xs = whole(down_other_kernel, [shape(D, D), shape(D, D)], 14, 1_000, smem=1)(at, g, dz, got_x)
    got_x = swap(xs, "x", FAR)
    yk, ys, zk, zs = whole(
        other_half_kernel,
        [shape(PIECE, QKV + Y2), shape(PIECE, QKV + Y2), shape(PIECE, Z1 + Z2), shape(PIECE, Z1 + Z2)],
        24, 1_000, hbm=(12,),
    )(left, db, du, got_y, got_z, a1y, a1z, dq, dk, dv, got_y1, got_z1, xs)
    got_y, got_z = swap(ys, "y", FAR), swap(zs, "z", FAR)
    token_grad, ek, es = whole(
        input_grad_kernel,
        [shape(ROWS, D, dtype=F32), shape(FIRST, 128), shape(FIRST, 128)],
        30, 1_000, hbm=(11, 12), scratch=[pltpu.VMEM((ROWS, D), F32)],
    )(dq, dk, dv, vec_b, vec_c, x, dx1, py, pz, wy, wz, ys, zs)
    kv, es = tie(kv, es)
    x1b, a2b = whole(
        later_attention_kernel, [shape(LEN, D, dtype=F32), shape(LEN, D)], 20, 1_000, smem=1,
        scratch=[pltpu.VMEM((LEN, D), B16), pltpu.VMEM((LEN, D), B16)],
    )(at, x, vec_b, a1y, kv, pz, wy, wo)
    es, a2b, got_y, got_z = tie(es, a2b, got_y, got_z)
    zk, zs = halves([(zk, got_z)])
    yk, ys = halves([(yk, got_y)])
    got_z, got_y = swap(zs, "z", NEAR), swap(ys, "y", NEAR)
    got_e, got_x, _, _ = tie(swap(es, "core", CORES), got_x, ys, zs)
    ek, es = halves([(ek, got_e)])
    got_e = swap(es, "y", FAR)
    a2b, _, _, _ = tie(a2b, ys, zs, es)
    (later_g,) = whole(
        later_hidden_kernel, [shape(LEN, FF)], 22, 1_000,
        scratch=[pltpu.VMEM((D, Y2), B16), pltpu.VMEM((D, Z2), B16)],
    )(a2b, ub, py, pz, *yg2, *zg2)
    later_g, got_e = tie(later_g, got_e)
    xk, xs = halves([(xk, got_x)])
    got_x = swap(xs, "x", NEAR)
    ek, es = halves([(ek, got_e)])
    got_e = swap(es, "y", NEAR)
    later_g, _ = tie(later_g, es)
    (mixed,) = whole(output_kernel, [shape(ROWS, D)], 16, 1_000)(g, later_g, wd, x1, x1b, vec_b)
    mixed, got_y, got_z = tie(mixed, got_y, got_z)
    zk, z_sends = quarters(total_of(zk, got_z))
    yk, y_sends = quarters(beside(total_of(yk, got_y), total_of(ek, got_e)))
    gots_z, gots_y = exchange(z_sends, "y"), exchange(y_sends, "z")
    got_x, gots_z[0], gots_y[0] = tie(got_x, gots_z[0], gots_y[0])
    down = deal(total_of(xk, got_x).astype(B16).reshape(16, 24, D), ("y", "z"))
    total = beside(sum([v.astype(F32) for v in gots_y], yk), sum([v.astype(F32) for v in gots_z], zk))
    keep, sends = quarters(total)
    down_grad = jnp.sum(down.astype(F32), axis=0)
    gots = exchange(sends, "x")
    gots[2], down_grad = tie(gots[2], down_grad)
    qkv_grad, out_grad, up_grad, gains_grad, biases_grad, ub_grad = whole(
        unpack_kernel,
        [shape(6, 3 * D, dtype=F32), shape(6, D, dtype=F32), shape(6, FF, dtype=F32), shape(2, 6, dtype=F32),
         shape(6, 6, dtype=F32), shape(1, 24, dtype=F32)],
        8, 1_000,
    )(keep, *gots)
    return (
        mixed.reshape(2, LEN, D), token_grad.reshape(2, LEN, D), qkv_grad, out_grad, up_grad, down_grad,
        gains_grad, biases_grad, ub_grad.reshape(24),
    )


def solution(mesh):
    fine = Mesh(mesh.devices.reshape(SIZES), ALL)
    rows = lambda n: P(ALL, *([None] * (n - 1)))
    cols = P(None, ALL)
    in_specs = (rows(3), rows(1), rows(2), rows(3), rows(2), rows(2), rows(2), rows(2), cols, cols, rows(1))
    out_specs = (rows(3), rows(3), rows(2), rows(2), rows(2), rows(2), cols, cols, rows(1))
    return jax.shard_map(local, mesh=fine, in_specs=in_specs, out_specs=out_specs, check_vma=False)
```

```python
import functools

import jax
import jax.numpy as jnp
import numpy as np
from jax import lax
from jax.experimental import pallas as pl
from jax.experimental.pallas import tpu as pltpu
from jax.sharding import Mesh, PartitionSpec as P

B16 = jnp.bfloat16
F32 = jnp.float32
HEADS = 12
HEAD_DIM = 64
D = 768
FF = 3072
LEN = 256
HALF = 128
ROWS = 512
PIECE = 192
FIRST = 384
Y1, Y2, Z1, Z2 = 1280, 1792, 1920, 1280
QKV = 1152
ORDER_Y, ORDER_Z = ((2, 4), (3, 1), (0, 32)), ((3, 1), (2, 4), (0, 32))
CHUNKS = ((0, 0, 896), (0, 896, 896), (1, 0, 640), (1, 640, 640))
SCALE = HEAD_DIM**-0.5
ALL = ("x", "core", "y", "z")
SIZES = (4, 2, 4, 4)
RSQRT2 = 0.5**0.5
RSQRT2PI = (2.0 * np.pi) ** -0.5


def dot(a, b, ca=1, cb=0):
    return lax.dot_general(a, b, (((ca,), (cb,)), ((), ())), preferred_element_type=F32)


def pick(a, p):
    return dot(a, p).astype(B16)


def put_back(a, p):
    return dot(a.astype(B16), p, 1, 1)


def norm_stats(v):
    centered = v - jnp.mean(v, axis=-1, keepdims=True)
    variance = jnp.mean(centered * centered, axis=-1, keepdims=True)
    scale = lax.rsqrt(variance + 1e-05)
    return centered * scale, scale


def norm_back(grad, hat, scale, gain):
    g = grad * gain
    mean_g = jnp.mean(g, axis=-1, keepdims=True)
    mean_gh = jnp.mean(g * hat, axis=-1, keepdims=True)
    return scale * (g - mean_g - hat * mean_gh)


def row_sum(v):
    return jnp.sum(v, axis=0, keepdims=True)


def softmax_of(q_one, k_two, valid):
    s = jnp.where(valid, dot(q_one, k_two, 1, 1), -1000000000.0)
    e = jnp.exp(s - jnp.max(s, axis=-1, keepdims=True))
    return e / jnp.sum(e, axis=-1, keepdims=True)


class Copies:
    def __init__(self, sems):
        self.sems, self.used = sems, 0

    def start(self, src, dst):
        copy = pltpu.make_async_copy(src, dst, self.sems.at[self.used])
        self.used += 1
        copy.start()
        return copy


def wait(copies):
    for copy in copies:
        copy.wait()


def load_rows(copies, pieces, dst, cols):
    return [
        copies.start(p.at[:, cols], dst.at[pl.ds(i * PIECE, PIECE), :]) for i, p in enumerate(pieces)
    ]


def pack_kernel(qkv_ref, out_ref, up_ref, down_ref, gains_ref, biases_ref, ub_ref, yz_ref, deal_ref):
    vecs = jnp.concatenate([gains_ref[...], biases_ref[...]], axis=0)
    eye = lax.broadcasted_iota(jnp.int32, (8, 128), 0) == lax.broadcasted_iota(jnp.int32, (8, 128), 1)
    ext = dot(vecs, eye.astype(F32).astype(B16), 0, 0)
    wide = jnp.broadcast_to(ub_ref[...].astype(F32), (6, 24)).astype(B16)
    unit = lax.broadcasted_iota(jnp.int32, (6, 24), 1)
    mine = unit // 4 == lax.broadcasted_iota(jnp.int32, (6, 24), 0)
    shift = lax.broadcasted_iota(jnp.int32, (24, 128), 0) % 4 + 8
    shift = shift == lax.broadcasted_iota(jnp.int32, (24, 128), 1)
    ub = dot(jnp.where(mine, wide, 0), shift.astype(F32).astype(B16))
    at = 0
    for part in (
        qkv_ref[:, :QKV], (ext + ub).astype(B16), up_ref[:, :Y2],
        qkv_ref[:, QKV:], out_ref[...], up_ref[:, Y2:],
    ):
        yz_ref[:, at : at + part.shape[1]] = part
        at += part.shape[1]
    for i in range(16):
        deal_ref[i] = down_ref[...]


def by_fours():
    row = lax.broadcasted_iota(jnp.int32, (512, 512), 0)
    col = lax.broadcasted_iota(jnp.int32, (512, 512), 1)
    return (row == col % 128 * 4 + col // 128).astype(F32).astype(B16)


def turned(step, core):
    gray = step ^ (step >> 1)
    return gray ^ ((gray & 1) * 2 * core)


def one_hot_of(at_ref, order):
    position = lax.broadcasted_iota(jnp.int32, (1, D), 1)
    device = (position * 10923) >> 16
    core = at_ref[1] ^ (device >> 6)
    total = core * 16
    for i, (axis, weight) in enumerate(order):
        total += (at_ref[axis] ^ turned((device >> (4 - 2 * i)) & 3, core)) * weight
    row = lax.broadcasted_iota(jnp.int32, (D, D), 0)
    return (row == total * 6 + position - device * 6).astype(F32).astype(B16)


def block_of(at_ref, half, i):
    core = at_ref[1] ^ half
    return (at_ref[0] ^ turned(i, core)) * 2 + core


def attend(at_ref, cell, q_ref, kv_ref, o_ref):
    head_lane = lax.broadcasted_iota(jnp.int32, (HALF, 128), 1) < HEAD_DIM
    valid = lax.broadcasted_iota(jnp.int32, (1, LEN), 1) < at_ref[4 + cell]
    rows = slice(cell * HALF, (cell + 1) * HALF)
    keys = slice(cell * LEN, (cell + 1) * LEN)
    group = 3
    for start in range(0, HEADS // 2, group):
        scores, probs = [], []
        for pair in range(start, start + group):
            at = pair * 128
            q = q_ref[rows, at : at + 128] * SCALE
            both = jnp.concatenate([jnp.where(head_lane, q, 0), jnp.where(head_lane, 0, q)], axis=0)
            scores.append(dot(both, kv_ref[keys, at : at + 128], 1, 1))
        for s in scores:
            s = jnp.where(valid, s, -1000000000.0)
            e = jnp.exp(s - jnp.max(s, axis=-1, keepdims=True))
            probs.append((e * (1.0 / jnp.sum(e, axis=-1, keepdims=True))).astype(B16))
        for i, pair in enumerate(range(start, start + group)):
            at = pair * 128
            o = dot(probs[i], kv_ref[keys, D + at : D + at + 128])
            o_ref[rows, at : at + 128] = jnp.where(head_lane, o[:HALF], o[HALF:]).astype(B16)


def half_rows(v, half):
    at = half * HALF
    return jnp.concatenate([v[at : at + HALF], v[LEN + at : LEN + at + HALF]], axis=0)


def attention_kernel(at_ref, x_ref, y0, y1, y2, y3, z0, z1, z2, z3, *refs):
    (a1y_hbm, a1z_hbm, kv_hbm, q_ref, oz_ref, x1_ref, a2_ref, par_ref, ub_ref,
     py_hbm, pz_hbm, wy_hbm, wz_hbm, wo_hbm) = refs[-23:-9]
    wy, wz, py, pz, a1y_ref, a1z_ref, kv_ref, o_ref, sems = refs[-9:]
    copies = Copies(sems)
    first = []
    for i, p in enumerate((y0, y1, y2, y3)):
        first.append(copies.start(p, wy.at[pl.ds(i * PIECE, PIECE), :]))
    second = []
    for i, p in enumerate((z0, z1, z2, z3)):
        second.append(copies.start(p, wz.at[pl.ds(i * PIECE, PIECE), :]))
    py[...] = one_hot_of(at_ref, ORDER_Y)
    pz[...] = one_hot_of(at_ref, ORDER_Z)
    outs = [copies.start(py, py_hbm), copies.start(pz, pz_hbm)]
    x = x_ref[...].astype(F32)
    hat, _ = norm_stats(x)
    wait(first)
    outs.append(copies.start(wy.at[:, pl.ds(0, QKV)], wy_hbm))
    par = dot(wy[:, QKV:Y1], py[...], 0, 1)
    par_ref[...] = par[:8]
    units = [jnp.concatenate([par[8 + q : 9 + q, g * 128 : (g + 1) * 128] for q in range(4)], axis=1) for g in range(6)]
    units = dot(jnp.concatenate(units + units[:2], axis=0).astype(B16), by_fours(), 1, 1)
    for g in range(6):
        ub_ref[:, g * 512 : (g + 1) * 512] = units[g : g + 1]
    a1 = (hat * par[0:1] + par[2:3]).astype(B16)
    a1y = pick(a1, py[...])
    a1y_ref[...] = a1y
    outs.append(copies.start(a1y_ref, a1y_hbm))
    q_ref[...] = (dot(half_rows(a1y, 0), wy[:, :D]) + par[3:4]).astype(B16)
    kv_ref[:, :384] = dot(a1y, wy[:, D:QKV]).astype(B16)
    wait(second)
    outs.append(copies.start(wz.at[:, pl.ds(0, QKV)], wz_hbm))
    outs.append(copies.start(wz.at[:, pl.ds(QKV, D)], wo_hbm))
    a1z = pick(a1, pz[...])
    a1z_ref[...] = a1z
    outs.append(copies.start(a1z_ref, a1z_hbm))
    kv = dot(a1z, wz[:, :QKV])
    kv_ref[:, 384:D] = kv[:, :384].astype(B16)
    kv_ref[:, D:] = (kv[:, 384:] + par[4:5]).astype(B16)
    outs.append(copies.start(kv_ref, kv_hbm))
    attend(at_ref, 0, q_ref, kv_ref, o_ref)
    attend(at_ref, 1, q_ref, kv_ref, o_ref)
    oz = pick(o_ref[...], pz[...])
    oz_ref[...] = oz
    x1 = half_rows(x, 0) + dot(oz, wz[:, QKV:Z1]) + par[5:6]
    hat, _ = norm_stats(x1)
    x1_ref[...] = x1
    a2 = (hat * par[1:2] + par[6:7]).astype(B16)
    a2_ref[0] = pick(a2, py[...])
    a2_ref[1] = pick(a2, pz[...])
    wait(outs)


def later_attention_kernel(at_ref, x_ref, vec_ref, a1y_ref, kv_ref, pz_ref, wy_ref, wo_ref, *refs):
    x1_ref, a2_ref, q, o = refs[-4:]
    q[...] = (dot(half_rows(a1y_ref, 1), wy_ref[:, :D]) + vec_ref[3:4]).astype(B16)
    attend(at_ref, 0, q, kv_ref, o)
    attend(at_ref, 1, q, kv_ref, o)
    x1 = half_rows(x_ref, 1).astype(F32) + dot(pick(o[...], pz_ref[...]), wo_ref[...]) + vec_ref[5:6]
    hat, _ = norm_stats(x1)
    x1_ref[...] = x1
    a2_ref[...] = (hat * vec_ref[1:2] + vec_ref[6:7]).astype(B16)


def load_down(copies, at_ref, pieces, wd):
    started = []
    for i, p in enumerate(pieces):
        for j in range(2):
            at = pl.multiple_of(block_of(at_ref, i // 2, 2 * (i % 2) + j) * FIRST, FIRST)
            started.append(copies.start(p.at[pl.ds(j * FIRST, FIRST), :], wd.at[pl.ds(at, FIRST), :]))
    return started


def ffn_kernel(
    at_ref, a2_ref, x1_hbm, oz_hbm, pos_ref, cot_ref, par_ref, ub_ref, py_hbm, pz_hbm,
    y0, y1, y2, y3, z0, z1, z2, z3, d0, d1, d2, d3, wo_hbm, q_hbm,
    dx1_ref, pair_ref, vec_ref, left_ref, dz_ref, db_ref, ys_hbm, zs_hbm, ds_hbm, du_hbm, g_hbm, wd_hbm,
    wy, wz, wd, wo, py, pz, gy, gz, gd, du_all, g_all, x1_ref, oz_ref, sems,
):
    copies = Copies(sems)
    first = load_rows(copies, (y0, y1, y2, y3), wy, pl.ds(0, Y2))
    third = load_down(copies, at_ref, (d0, d1, d2, d3), wd)
    turns = [copies.start(py_hbm, py)]
    second = load_rows(copies, (z0, z1, z2, z3), wz, pl.ds(0, Z2))
    turns.append(copies.start(pz_hbm, pz))
    fourth = [
        copies.start(a, b)
        for a, b in ((x1_hbm, x1_ref), (oz_hbm, oz_ref), (wo_hbm, wo), (q_hbm, pair_ref.at[0]))
    ]
    row = lax.broadcasted_iota(jnp.int32, (HALF, 64), 0)
    dy = []
    for cell in range(2):
        hot = (row == pos_ref[cell : cell + 1, :]).astype(F32).astype(B16)
        dy.append(dot(hot, cot_ref[cell]))
    dy = jnp.concatenate(dy, axis=0)
    dz = dy.astype(B16)
    dz_ref[...] = dz
    outs, unit_sums, da2, at = [], [], None, 0
    for lane, w, grads in ((0, wy, gy), (1, wz, gz)):
        wait((first, second)[lane])
        a2 = a2_ref[lane]
        left_ref[lane] = a2[:, :FIRST]
        chunks, slopes, part = [], [], None
        for at_lane, start, width in CHUNKS:
            if at_lane == lane:
                chunks.append((slice(start, start + width), slice(at, at + width)))
                at += width
        for cols, ff in chunks:
            u = dot(a2, w[:, cols]) + ub_ref[:, ff]
            phi = 0.5 + 0.5 * lax.erf(u * RSQRT2)
            g_all[:, ff] = (u * phi).astype(B16)
            slopes.append(phi + u * (jnp.exp(-0.5 * u * u) * RSQRT2PI))
        if lane == 0:
            wait(third)
            outs.append(copies.start(wd, wd_hbm))
        for (cols, ff), slope in zip(chunks, slopes):
            du = (dot(dz, wd[ff, :], 1, 1) * slope).astype(B16)
            du_all[:, ff] = du
            back = dot(du, w[:, cols], 1, 1)
            part = back if part is None else part + back
            unit_sums.append(row_sum(du.astype(F32)))
            grads[:, cols] = dot(a2[:, FIRST:], du, 0, 0).astype(B16)
        turns[lane].wait()
        back = put_back(part, (py, pz)[lane][...])
        da2 = back if lane == 0 else da2 + back
        if lane == 0:
            outs.append(copies.start(gy, ys_hbm))
    outs += [copies.start(g_all, g_hbm), copies.start(du_all, du_hbm)]
    for i in range(4):
        cols = pl.ds(pl.multiple_of(block_of(at_ref, 1, i) * FIRST, FIRST), FIRST)
        gd[i * FIRST : (i + 1) * FIRST, :] = dot(g_all[:, cols], dz, 0, 0).astype(B16)
    outs.append(copies.start(gd, ds_hbm))
    wait(fourth)
    hat, scale = norm_stats(x1_ref[...])
    dx1 = dy + norm_back(da2, hat, scale, par_ref[1:2])
    dx1_ref[...] = dx1
    db = dx1.astype(B16)
    db_ref[...] = db
    left_ref[2] = oz_ref[:, :FIRST]
    gz[:, Z2:] = dot(oz_ref[:, FIRST:], db, 0, 0).astype(B16)
    outs.append(copies.start(gz, zs_hbm))
    pair_ref[1] = dot(dot(db, wo[...], 1, 1).astype(B16), pz[...], 1, 1).astype(B16)
    sums = jnp.concatenate(unit_sums, axis=1)
    sums = jnp.concatenate([sums[:, g * 512 : (g + 1) * 512] for g in range(6)] + [jnp.zeros((2, 512), F32)], axis=0)
    sums = dot(sums.astype(B16), by_fours())
    vec_ref[:8, :] = par_ref[...]
    vec_ref[8:9, :] = row_sum(da2 * hat)
    vec_ref[9:10, :] = row_sum(da2)
    vec_ref[10:11, :] = row_sum(dz.astype(F32))
    vec_ref[11:12, :] = row_sum(db.astype(F32))
    for q in range(4):
        vec_ref[12 + q : 13 + q, :] = jnp.concatenate(
            [sums[g : g + 1, q * 128 : (q + 1) * 128] for g in range(6)], axis=1
        )
    wait(outs)


def later_hidden_kernel(a2_ref, ub_ref, py_ref, pz_ref, y0, y1, y2, y3, z0, z1, z2, z3, *refs):
    g_ref, wy, wz = refs[-3:]
    for w, pieces in ((wy, (y0, y1, y2, y3)), (wz, (z0, z1, z2, z3))):
        for i, p in enumerate(pieces):
            w[i * PIECE : (i + 1) * PIECE, :] = p[...]
    at = 0
    for lane, start, width in CHUNKS:
        if start == 0:
            a2 = pick(a2_ref[...], (py_ref, pz_ref)[lane][...])
        ff = slice(at, at + width)
        at += width
        u = dot(a2, (wy, wz)[lane][:, start : start + width]) + ub_ref[:, ff]
        g_ref[:, ff] = (u * (0.5 + 0.5 * lax.erf(u * RSQRT2))).astype(B16)


def output_kernel(g_ref, later_g_ref, wd_ref, x1_ref, later_x1_ref, vec_ref, mixed_ref):
    for half, (g, x1) in enumerate(((g_ref, x1_ref), (later_g_ref, later_x1_ref))):
        mixed = (x1[...] + (dot(g[...], wd_ref[...]) + vec_ref[7:8])).astype(B16)
        for cell in range(2):
            to = cell * LEN + half * HALF
            mixed_ref[to : to + HALF, :] = mixed[cell * HALF : (cell + 1) * HALF]


def attention_back_kernel(at_ref, pair_ref, kv_hbm, dq_ref, dk_ref, dv_ref, vec_ref, kv_ref, sems):
    copies = Copies(sems)
    loads = [copies.start(kv_hbm.at[pl.ds(c * LEN, LEN), :], kv_ref.at[pl.ds(c * LEN, LEN), :]) for c in range(2)]
    head_lane = lax.broadcasted_iota(jnp.int32, (HALF, 128), 1) < HEAD_DIM
    key = lax.broadcasted_iota(jnp.int32, (LEN, 1), 0)
    group = 6
    for cell in range(2):
        valid = key < at_ref[4 + cell]
        loads[cell].wait()
        rows = slice(cell * LEN, (cell + 1) * LEN)
        grads = slice(cell * HALF, (cell + 1) * HALF)
        for start in range(0, HEADS // 2, group):
            held = []
            for pair in range(start, start + group):
                at = pair * 128
                q = pair_ref[0, grads, at : at + 128] * SCALE
                k = kv_ref[rows, at : at + 128]
                v = kv_ref[rows, D + at : D + at + 128]
                do = pair_ref[1, grads, at : at + 128]
                q2 = jnp.concatenate([jnp.where(head_lane, q, 0), jnp.where(head_lane, 0, q)], axis=0)
                do2 = jnp.concatenate([jnp.where(head_lane, do, 0), jnp.where(head_lane, 0, do)], axis=0)
                held.append((q2, do2, k, dot(k, q2, 1, 1), dot(v, do2, 1, 1)))
            soft = []
            for q2, do2, k, s, dp in held:
                s = jnp.where(valid, s, -1000000000.0)
                e = jnp.exp(s - jnp.max(s, axis=0, keepdims=True))
                p = e * (1.0 / jnp.sum(e, axis=0, keepdims=True))
                ds = p * (dp - jnp.sum(dp * p, axis=0, keepdims=True))
                soft.append((p.astype(B16), ds.astype(B16)))
            for i, pair in enumerate(range(start, start + group)):
                at = pair * 128
                q2, do2, k, _, _ = held[i]
                p, ds = soft[i]
                dv_ref[rows, at : at + 128] = dot(p, do2).astype(B16)
                dk_ref[rows, at : at + 128] = dot(ds, q2).astype(B16)
                dq = dot(ds, k, 0, 0) * SCALE
                dq_ref[grads, at : at + 128] = jnp.where(head_lane, dq[:HALF], dq[HALF:]).astype(B16)
    vec_ref[0:1, :] = row_sum(dq_ref[...].astype(F32))
    vec_ref[1:2, :] = row_sum(dv_ref[...].astype(F32))
    vec_ref[2:, :] = jnp.zeros((6, D), F32)


def down_other_kernel(at_ref, g_ref, dz_ref, got_ref, keep_ref, send_ref):
    for i in range(4):
        cols = pl.ds(pl.multiple_of(block_of(at_ref, 0, i) * FIRST, FIRST), FIRST)
        got = got_ref[i * FIRST : (i + 1) * FIRST, :].astype(F32)
        grad = (dot(g_ref[:, cols], dz_ref[...], 0, 0) + got).astype(B16)
        out = (keep_ref, send_ref)[i // 2]
        out[i % 2 * FIRST : (i % 2 + 1) * FIRST, :] = grad


def qkv_grads(a1y_ref, a1z_ref, dq_ref, dk_ref, dv_ref, rows):
    a1y, a1z = a1y_ref[:, rows], a1z_ref[:, rows]
    a1q = jnp.concatenate([a1y[:HALF], a1y[LEN : LEN + HALF]], axis=0)
    yield 0, 0, dot(a1q, dq_ref[...], 0, 0)
    yield 0, D, dot(a1y, dk_ref[:, :384], 0, 0)
    yield 1, 0, dot(a1z, dk_ref[:, 384:], 0, 0)
    yield 1, 384, dot(a1z, dv_ref[...], 0, 0)


def qkv_grad_kernel(a1y_ref, a1z_ref, dq_ref, dk_ref, dv_ref, *refs):
    outs = refs[-2:]
    for lane, at, grad in qkv_grads(a1y_ref, a1z_ref, dq_ref, dk_ref, dv_ref, slice(FIRST, D)):
        outs[lane][:, at : at + grad.shape[1]] = grad.astype(B16)


def add_halves(outs, at, grad, got):
    grad = (grad + got.astype(F32)).astype(B16)
    cols = slice(at, at + grad.shape[1])
    outs[0][:, cols] = grad[:PIECE]
    outs[1][:, cols] = grad[PIECE:]


def other_half_kernel(
    left_ref, db_ref, du_ref, gy_ref, gz_ref, a1y_ref, a1z_ref, dq_ref, dk_ref, dv_ref, gy1_ref, gz1_ref,
    *refs,
):
    outs = refs[-4:-2], refs[-2:]
    add_halves(outs[0], 0, dot(left_ref[0], du_ref[:, :Y2], 0, 0), gy_ref[...])
    add_halves(outs[1], 0, dot(left_ref[1], du_ref[:, Y2:], 0, 0), gz_ref[:, :Z2])
    add_halves(outs[1], Z2, dot(left_ref[2], db_ref[...], 0, 0), gz_ref[:, Z2:])
    for lane, at, grad in qkv_grads(a1y_ref, a1z_ref, dq_ref, dk_ref, dv_ref, slice(0, FIRST)):
        got = (gy1_ref, gz1_ref)[lane][:, at : at + grad.shape[1]]
        add_halves(outs[lane], (Y2, Z2 + D)[lane] + at, grad, got)


def input_grad_kernel(
    dq_ref, dk_ref, dv_ref, vec_b_ref, vec_c_ref, x_ref, dx1_ref, py, pz, wy, wz, *refs
):
    out_ref, ek_ref, es_ref, da_ref = refs[-4:]
    dz = dot(dk_ref[:, 384:], wz[:, :384], 1, 1) + dot(dv_ref[...], wz[:, 384:], 1, 1)
    da_ref[...] = put_back(dz, pz[...])
    from_q = dot(dq_ref[...], wy[:, :D], 1, 1)
    dy = dot(dk_ref[:, :384], wy[:, D:], 1, 1)
    zero = jnp.zeros((HALF, D), F32)
    dy += jnp.concatenate([from_q[:HALF], zero, from_q[HALF:], zero], axis=0)
    da = da_ref[...] + put_back(dy, py[...])
    hat, scale = norm_stats(x_ref[...].astype(F32))
    grad = norm_back(da, hat, scale, vec_b_ref[0:1])
    for cell in range(2):
        at = cell * LEN
        out_ref[at : at + HALF, :] = grad[at : at + HALF] + dx1_ref[cell * HALF : (cell + 1) * HALF]
        out_ref[at + HALF : at + LEN, :] = grad[at + HALF : at + LEN]
    lines = [
        row_sum(da * hat), vec_b_ref[8:9], row_sum(da), vec_c_ref[0:1],
        vec_c_ref[1:2], vec_b_ref[11:12], vec_b_ref[9:10], vec_b_ref[10:11],
        vec_b_ref[12:16], jnp.zeros((116, D), F32),
    ]
    ext = dot(py[...], jnp.concatenate(lines, axis=0).astype(B16), 0, 1).astype(B16)
    ek_ref[...] = ext[:FIRST]
    es_ref[...] = ext[FIRST:]


def unpack_kernel(k_ref, g1_ref, g2_ref, g3_ref, qkv_ref, out_ref, up_ref, gains_ref, biases_ref, ub_ref):
    total = k_ref[...] + g1_ref[...].astype(F32) + g2_ref[...].astype(F32) + g3_ref[...].astype(F32)
    y, z = total[:, : Y1 + Y2], total[:, Y1 + Y2 :]
    up_ref[:, :Y2] = y[:, :Y2]
    up_ref[:, Y2:] = z[:, :Z2]
    out_ref[...] = z[:, Z2 : Z2 + D]
    qkv_ref[:, :QKV] = y[:, Y2 : Y2 + QKV]
    qkv_ref[:, QKV:] = z[:, Z2 + D :]
    small = y[:, Y2 + QKV :]
    turned = small.T
    gains_ref[...] = turned[0:2]
    biases_ref[...] = turned[2:8]
    line = jnp.concatenate([small[:, 8:12]] * 6, axis=1)
    mine = lax.broadcasted_iota(jnp.int32, (6, 24), 1) // 4 == lax.broadcasted_iota(jnp.int32, (6, 24), 0)
    ub_ref[...] = row_sum(jnp.where(mine, line, 0.0))


def whole(kernel, outs, mib, flops, scratch=(), smem=0, hbm=(), hbm_outs=()):
    def call(*args):
        in_hbm = pl.BlockSpec(memory_space=pltpu.HBM)
        in_vmem = pl.BlockSpec(memory_space=pltpu.VMEM)
        specs = [pl.BlockSpec(memory_space=pltpu.SMEM)] * smem
        specs += [in_hbm if i in hbm else in_vmem for i in range(smem, len(args))]
        return pl.pallas_call(
            kernel,
            out_shape=outs,
            in_specs=specs,
            out_specs=[in_hbm if i in hbm_outs else in_vmem for i in range(len(outs))],
            scratch_shapes=scratch,
            compiler_params=pltpu.CompilerParams(vmem_limit_bytes=mib * 1024 * 1024),
            cost_estimate=pl.CostEstimate(flops=flops, bytes_accessed=1024, transcendentals=0),
        )(*args)

    return call


def shape(*dims, dtype=B16):
    return jax.ShapeDtypeStruct(dims, dtype)


def swap(v, axis, masks):
    pairs = []
    for flat in range(128):
        at = list(np.unravel_index(flat, SIZES))
        at[ALL.index(axis)] ^= masks[at[1]]
        pairs.append((flat, int(np.ravel_multi_index(at, SIZES))))
    return lax.ppermute(v, ALL, pairs)


NEAR, FAR, OPPOSITE, CORES = (1, 3), (3, 1), (2, 2), (1, 1)


def under(*parts):
    return jnp.concatenate(parts, axis=0)


def beside(*parts):
    return jnp.concatenate(parts, axis=1)


def quadruple(own, axis):
    return under(own, swap(own, axis, NEAR), swap(own, axis, FAR), swap(own, axis, OPPOSITE))


def tie(*arrays):
    return lax.optimization_barrier(arrays)


def doubled(own, axis):
    return under(own, swap(own, axis, NEAR))


def both_cores(near, far):
    return near, far, swap(near, "core", CORES), swap(far, "core", CORES)


def deal(parts, plane):
    return lax.all_to_all(parts, plane, 0, 0)


def plus(own, got):
    return own + got.astype(F32)


def total_of(own, got):
    return own.astype(F32) + got.astype(F32)


def halves(pairs):
    n = pairs[0][0].shape[0] // 2
    keep = beside(*[total_of(own[:n], got[:n]) for own, got in pairs])
    send = beside(*[total_of(own[n:], got[n:]).astype(B16) for own, got in pairs])
    return keep, send


def quarters(total):
    n = total.shape[0] // 4
    return total[:n], [total[i * n : (i + 1) * n].astype(B16) for i in (1, 2, 3)]


def exchange(sends, axis):
    return [swap(v, axis, m) for v, m in zip(sends, (NEAR, FAR, OPPOSITE))]


def local(
    tokens, lengths, positions, cotangent, qkv_weight, out_weight, up_weight, down_weight,
    norm_gains, biases, up_bias,
):
    at = jnp.concatenate([jnp.stack([lax.axis_index(a) for a in ALL]), lengths])

    yz, down = whole(pack_kernel, [shape(6, Y1 + Y2 + Z1 + Z2), shape(16, 24, D)], 60, 1_000)(
        qkv_weight, out_weight, up_weight, down_weight, norm_gains, biases, up_bias.reshape(1, 24)
    )
    yz = quadruple(yz, "x")
    down = deal(down, ("y", "z")).reshape(FIRST, D)
    y = quadruple(yz[:, : Y1 + Y2], "z")
    z = quadruple(yz[:, Y1 + Y2 :], "y")
    y1, z1, y2, z2 = y[:, :Y1], z[:, :Z1], y[:, Y1:], z[:, Z1:]
    down, at, _, _ = tie(down, at, y1, z1)
    near_y, near_z = doubled(y1, "y"), doubled(z1, "z")
    far_y, far_z = swap(near_y, "y", FAR), swap(near_z, "z", FAR)
    near_x = doubled(down, "x")
    near_x, _, _ = tie(near_x, near_y, near_z)
    far_x = swap(near_x, "x", FAR)
    got_y2, got_z2 = swap(y2, "y", NEAR), swap(z2, "z", NEAR)
    yg1, zg1 = both_cores(near_y, far_y), both_cores(near_z, far_z)
    other_x = swap(near_x, "core", CORES)
    got_y2, got_z2, _, _, _ = tie(got_y2, got_z2, near_y, near_z, near_x)
    near_y2 = under(y2, got_y2)
    other_y2 = swap(near_y2, "core", CORES)
    got_z2, other_y2 = tie(got_z2, other_y2)
    near_z2 = under(z2, got_z2)
    far_y2, far_z2 = swap(near_y2, "y", FAR), swap(near_z2, "z", FAR)

    x = tokens.reshape(ROWS, D)
    dma = pltpu.SemaphoreType.DMA
    a1y, a1z, kv, q, oz, x1, a2, par, ub, py, pz, wy, wz, wo = whole(
        attention_kernel,
        [shape(ROWS, D), shape(ROWS, D), shape(ROWS, 2 * D), shape(LEN, D), shape(LEN, D), shape(LEN, D, dtype=F32),
         shape(2, LEN, D), shape(8, D, dtype=F32), shape(1, FF, dtype=F32),
         shape(D, D), shape(D, D), shape(D, QKV), shape(D, QKV), shape(D, D)],
        60, 1_000, smem=1, hbm=range(2, 13), hbm_outs=(0, 1, 2, 9, 10, 11, 12, 13),
        scratch=[pltpu.VMEM((D, Y1), B16), pltpu.VMEM((D, Z1), B16), pltpu.VMEM((D, D), B16),
                 pltpu.VMEM((D, D), B16), pltpu.VMEM((ROWS, D), B16), pltpu.VMEM((ROWS, D), B16),
                 pltpu.VMEM((ROWS, 2 * D), B16), pltpu.VMEM((LEN, D), B16), dma((16,))],
    )(at, x, *yg1, *zg1, near_y2, near_z2, near_x)
    far_x, far_y2, far_z2, a2 = tie(far_x, far_y2, far_z2, a2)
    down = (near_x, far_x, other_x, swap(far_x, "core", CORES))
    yg2 = (near_y2, far_y2, other_y2, swap(far_y2, "core", CORES))
    zg2 = both_cores(near_z2, far_z2)

    dx1, pair, vec_b, left, dz, db, ys2, zs2, xs2, du, g, wd = whole(
        ffn_kernel,
        [shape(LEN, D, dtype=F32), shape(2, LEN, D), shape(16, D, dtype=F32),
         shape(3, LEN, FIRST), shape(LEN, D), shape(LEN, D),
         shape(FIRST, Y2), shape(FIRST, Z2 + D), shape(1536, D), shape(LEN, FF), shape(LEN, FF), shape(FF, D)],
        60, 1_000, smem=1, hbm=(2, 3, *range(8, 24)), hbm_outs=range(6, 12),
        scratch=[pltpu.VMEM((D, Y2), B16), pltpu.VMEM((D, Z2), B16), pltpu.VMEM((FF, D), B16), pltpu.VMEM((D, D), B16),
                 pltpu.VMEM((D, D), B16), pltpu.VMEM((D, D), B16), pltpu.VMEM((FIRST, Y2), B16),
                 pltpu.VMEM((FIRST, Z2 + D), B16), pltpu.VMEM((1536, D), B16), pltpu.VMEM((LEN, FF), B16),
                 pltpu.VMEM((LEN, FF), B16), pltpu.VMEM((LEN, D), F32), pltpu.VMEM((LEN, D), B16), dma((32,))],
    )(at, a2, x1, oz, positions, cotangent, par, ub, py, pz, *yg2, *zg2, *down, wo, q)

    got_x, got_y, got_z = swap(xs2, "core", CORES), swap(ys2, "core", CORES), swap(zs2, "core", CORES)
    dq, dk, dv, vec_c = whole(
        attention_back_kernel,
        [shape(LEN, D), shape(ROWS, D), shape(ROWS, D), shape(8, D, dtype=F32)],
        20, 1_000, smem=1, hbm=(2,), scratch=[pltpu.VMEM((ROWS, 2 * D), B16), dma((2,))],
    )(at, pair, kv)
    ys1, zs1 = whole(qkv_grad_kernel, [shape(FIRST, QKV), shape(FIRST, QKV)], 14, 1_000)(a1y, a1z, dq, dk, dv)
    got_y1, got_z1 = swap(ys1, "core", CORES), swap(zs1, "core", CORES)
    xk, xs = whole(down_other_kernel, [shape(D, D), shape(D, D)], 14, 1_000, smem=1)(at, g, dz, got_x)
    got_x = swap(xs, "x", FAR)
    yk, ys, zk, zs = whole(
        other_half_kernel,
        [shape(PIECE, QKV + Y2), shape(PIECE, QKV + Y2), shape(PIECE, Z1 + Z2), shape(PIECE, Z1 + Z2)],
        24, 1_000, hbm=(12,),
    )(left, db, du, got_y, got_z, a1y, a1z, dq, dk, dv, got_y1, got_z1, xs)
    got_y, got_z = swap(ys, "y", FAR), swap(zs, "z", FAR)
    token_grad, ek, es = whole(
        input_grad_kernel,
        [shape(ROWS, D, dtype=F32), shape(FIRST, 128), shape(FIRST, 128)],
        30, 1_000, hbm=(11, 12), scratch=[pltpu.VMEM((ROWS, D), F32)],
    )(dq, dk, dv, vec_b, vec_c, x, dx1, py, pz, wy, wz, ys, zs)
    kv, es = tie(kv, es)
    x1b, a2b = whole(
        later_attention_kernel, [shape(LEN, D, dtype=F32), shape(LEN, D)], 20, 1_000, smem=1,
        scratch=[pltpu.VMEM((LEN, D), B16), pltpu.VMEM((LEN, D), B16)],
    )(at, x, vec_b, a1y, kv, pz, wy, wo)
    es, a2b, got_y, got_z = tie(es, a2b, got_y, got_z)
    zk, zs = halves([(zk, got_z)])
    yk, ys = halves([(yk, got_y)])
    got_z, got_y = swap(zs, "z", NEAR), swap(ys, "y", NEAR)
    got_e, got_x, _, _ = tie(swap(es, "core", CORES), got_x, ys, zs)
    ek, es = halves([(ek, got_e)])
    got_e = swap(es, "y", FAR)
    a2b, _, _, _ = tie(a2b, ys, zs, es)
    (later_g,) = whole(
        later_hidden_kernel, [shape(LEN, FF)], 22, 1_000,
        scratch=[pltpu.VMEM((D, Y2), B16), pltpu.VMEM((D, Z2), B16)],
    )(a2b, ub, py, pz, *yg2, *zg2)
    later_g, got_e = tie(later_g, got_e)
    xk, xs = halves([(xk, got_x)])
    got_x = swap(xs, "x", NEAR)
    ek, es = halves([(ek, got_e)])
    got_e = swap(es, "y", NEAR)
    later_g, _ = tie(later_g, es)
    (mixed,) = whole(output_kernel, [shape(ROWS, D)], 16, 1_000)(g, later_g, wd, x1, x1b, vec_b)
    mixed, got_y, got_z = tie(mixed, got_y, got_z)
    zk, z_sends = quarters(total_of(zk, got_z))
    yk, y_sends = quarters(beside(total_of(yk, got_y), total_of(ek, got_e)))
    gots_z, gots_y = exchange(z_sends, "y"), exchange(y_sends, "z")
    got_x, gots_z[0], gots_y[0] = tie(got_x, gots_z[0], gots_y[0])
    down = deal(total_of(xk, got_x).astype(B16).reshape(16, 24, D), ("y", "z"))
    total = beside(sum([v.astype(F32) for v in gots_y], yk), sum([v.astype(F32) for v in gots_z], zk))
    keep, sends = quarters(total)
    down_grad = jnp.sum(down.astype(F32), axis=0)
    gots = exchange(sends, "x")
    gots[2], down_grad = tie(gots[2], down_grad)
    qkv_grad, out_grad, up_grad, gains_grad, biases_grad, ub_grad = whole(
        unpack_kernel,
        [shape(6, 3 * D, dtype=F32), shape(6, D, dtype=F32), shape(6, FF, dtype=F32), shape(2, 6, dtype=F32),
         shape(6, 6, dtype=F32), shape(1, 24, dtype=F32)],
        8, 1_000,
    )(keep, *gots)
    return (
        mixed.reshape(2, LEN, D), token_grad.reshape(2, LEN, D), qkv_grad, out_grad, up_grad, down_grad,
        gains_grad, biases_grad, ub_grad.reshape(24),
    )


def solution(mesh):
    fine = Mesh(mesh.devices.reshape(SIZES), ALL)
    rows = lambda n: P(ALL, *([None] * (n - 1)))
    cols = P(None, ALL)
    in_specs = (rows(3), rows(1), rows(2), rows(3), rows(2), rows(2), rows(2), rows(2), cols, cols, rows(1))
    out_specs = (rows(3), rows(3), rows(2), rows(2), rows(2), rows(2), cols, cols, rows(1))
    return jax.shard_map(local, mesh=fine, in_specs=in_specs, out_specs=out_specs, check_vma=False)
```

```python
import functools

import jax
import jax.numpy as jnp
import numpy as np
from jax import lax
from jax.experimental import pallas as pl
from jax.experimental.pallas import tpu as pltpu
from jax.sharding import Mesh, PartitionSpec as P

B16 = jnp.bfloat16
F32 = jnp.float32
HEADS = 12
HEAD_DIM = 64
D = 768
FF = 3072
LEN = 256
HALF = 128
ROWS = 512
PIECE = 192
FIRST = 384
Y1, Y2, Z1, Z2 = 1280, 1792, 1920, 1280
QKV = 1152
ORDER_Y, ORDER_Z = ((2, 4), (3, 1), (0, 32)), ((3, 1), (2, 4), (0, 32))
CHUNKS = ((0, 0, 896), (0, 896, 896), (1, 0, 640), (1, 640, 640))
SCALE = HEAD_DIM**-0.5
ALL = ("x", "core", "y", "z")
SIZES = (4, 2, 4, 4)
RSQRT2 = 0.5**0.5
RSQRT2PI = (2.0 * np.pi) ** -0.5


def dot(a, b, ca=1, cb=0):
    return lax.dot_general(a, b, (((ca,), (cb,)), ((), ())), preferred_element_type=F32)


def pick(a, p):
    return dot(a, p).astype(B16)


def put_back(a, p):
    return dot(a.astype(B16), p, 1, 1)


def norm_stats(v):
    centered = v - jnp.mean(v, axis=-1, keepdims=True)
    variance = jnp.mean(centered * centered, axis=-1, keepdims=True)
    scale = lax.rsqrt(variance + 1e-05)
    return centered * scale, scale


def norm_back(grad, hat, scale, gain):
    g = grad * gain
    mean_g = jnp.mean(g, axis=-1, keepdims=True)
    mean_gh = jnp.mean(g * hat, axis=-1, keepdims=True)
    return scale * (g - mean_g - hat * mean_gh)


def row_sum(v):
    return jnp.sum(v, axis=0, keepdims=True)


def softmax_of(q_one, k_two, valid):
    s = jnp.where(valid, dot(q_one, k_two, 1, 1), -1000000000.0)
    e = jnp.exp(s - jnp.max(s, axis=-1, keepdims=True))
    return e / jnp.sum(e, axis=-1, keepdims=True)


class Copies:
    def __init__(self, sems):
        self.sems, self.used = sems, 0

    def start(self, src, dst):
        copy = pltpu.make_async_copy(src, dst, self.sems.at[self.used])
        self.used += 1
        copy.start()
        return copy


def wait(copies):
    for copy in copies:
        copy.wait()


def load_rows(copies, pieces, dst, cols):
    return [
        copies.start(p.at[:, cols], dst.at[pl.ds(i * PIECE, PIECE), :]) for i, p in enumerate(pieces)
    ]


def pack_kernel(qkv_ref, out_ref, up_ref, down_ref, gains_ref, biases_ref, ub_ref, yz_ref, deal_ref):
    vecs = jnp.concatenate([gains_ref[...], biases_ref[...]], axis=0)
    eye = lax.broadcasted_iota(jnp.int32, (8, 128), 0) == lax.broadcasted_iota(jnp.int32, (8, 128), 1)
    ext = dot(vecs, eye.astype(F32).astype(B16), 0, 0)
    wide = jnp.broadcast_to(ub_ref[...].astype(F32), (6, 24)).astype(B16)
    unit = lax.broadcasted_iota(jnp.int32, (6, 24), 1)
    mine = unit // 4 == lax.broadcasted_iota(jnp.int32, (6, 24), 0)
    shift = lax.broadcasted_iota(jnp.int32, (24, 128), 0) % 4 + 8
    shift = shift == lax.broadcasted_iota(jnp.int32, (24, 128), 1)
    ub = dot(jnp.where(mine, wide, 0), shift.astype(F32).astype(B16))
    at = 0
    for part in (
        qkv_ref[:, :QKV], (ext + ub).astype(B16), up_ref[:, :Y2],
        qkv_ref[:, QKV:], out_ref[...], up_ref[:, Y2:],
    ):
        yz_ref[:, at : at + part.shape[1]] = part
        at += part.shape[1]
    for i in range(16):
        deal_ref[i] = down_ref[...]


def by_fours():
    row = lax.broadcasted_iota(jnp.int32, (512, 512), 0)
    col = lax.broadcasted_iota(jnp.int32, (512, 512), 1)
    return (row == col % 128 * 4 + col // 128).astype(F32).astype(B16)


def turned(step, core):
    gray = step ^ (step >> 1)
    return gray ^ ((gray & 1) * 2 * core)


def one_hot_of(at_ref, order):
    position = lax.broadcasted_iota(jnp.int32, (1, D), 1)
    device = (position * 10923) >> 16
    core = at_ref[1] ^ (device >> 6)
    total = core * 16
    for i, (axis, weight) in enumerate(order):
        total += (at_ref[axis] ^ turned((device >> (4 - 2 * i)) & 3, core)) * weight
    row = lax.broadcasted_iota(jnp.int32, (D, D), 0)
    return (row == total * 6 + position - device * 6).astype(F32).astype(B16)


def block_of(at_ref, half, i):
    core = at_ref[1] ^ half
    return (at_ref[0] ^ turned(i, core)) * 2 + core


def attend(at_ref, cell, q_ref, kv_ref, o_ref):
    head_lane = lax.broadcasted_iota(jnp.int32, (HALF, 128), 1) < HEAD_DIM
    valid = lax.broadcasted_iota(jnp.int32, (1, LEN), 1) < at_ref[4 + cell]
    rows = slice(cell * HALF, (cell + 1) * HALF)
    keys = slice(cell * LEN, (cell + 1) * LEN)
    group = 6
    for start in range(0, HEADS // 2, group):
        scores, probs = [], []
        for pair in range(start, start + group):
            at = pair * 128
            q = q_ref[rows, at : at + 128] * SCALE
            both = jnp.concatenate([jnp.where(head_lane, q, 0), jnp.where(head_lane, 0, q)], axis=0)
            scores.append(dot(both, kv_ref[keys, at : at + 128], 1, 1))
        for s in scores:
            s = jnp.where(valid, s, -1000000000.0)
            e = jnp.exp(s - jnp.max(s, axis=-1, keepdims=True))
            probs.append((e * (1.0 / jnp.sum(e, axis=-1, keepdims=True))).astype(B16))
        for i, pair in enumerate(range(start, start + group)):
            at = pair * 128
            o = dot(probs[i], kv_ref[keys, D + at : D + at + 128])
            o_ref[rows, at : at + 128] = jnp.where(head_lane, o[:HALF], o[HALF:]).astype(B16)


def half_rows(v, half):
    at = half * HALF
    return jnp.concatenate([v[at : at + HALF], v[LEN + at : LEN + at + HALF]], axis=0)


def attention_kernel(at_ref, x_ref, y0, y1, y2, y3, z0, z1, z2, z3, *refs):
    (a1y_hbm, a1z_hbm, kv_hbm, q_ref, oz_ref, x1_ref, a2_ref, par_ref, ub_ref,
     py_hbm, pz_hbm, wy_hbm, wz_hbm, wo_hbm) = refs[-23:-9]
    wy, wz, py, pz, a1y_ref, a1z_ref, kv_ref, o_ref, sems = refs[-9:]
    copies = Copies(sems)
    first = []
    for i, p in enumerate((y0, y1, y2, y3)):
        first.append(copies.start(p, wy.at[pl.ds(i * PIECE, PIECE), :]))
    second = []
    for i, p in enumerate((z0, z1, z2, z3)):
        second.append(copies.start(p, wz.at[pl.ds(i * PIECE, PIECE), :]))
    py[...] = one_hot_of(at_ref, ORDER_Y)
    outs = [copies.start(py, py_hbm)]
    x = x_ref[...].astype(F32)
    hat, _ = norm_stats(x)
    wait(first)
    outs.append(copies.start(wy.at[:, pl.ds(0, QKV)], wy_hbm))
    par = dot(wy[:, QKV:Y1], py[...], 0, 1)
    par_ref[...] = par[:8]
    a1 = (hat * par[0:1] + par[2:3]).astype(B16)
    a1y = pick(a1, py[...])
    a1y_ref[...] = a1y
    outs.append(copies.start(a1y_ref, a1y_hbm))
    q_ref[...] = (dot(half_rows(a1y, 0), wy[:, :D]) + par[3:4]).astype(B16)
    kv_ref[:, :384] = dot(a1y, wy[:, D:QKV]).astype(B16)
    pz[...] = one_hot_of(at_ref, ORDER_Z)
    outs.append(copies.start(pz, pz_hbm))
    wait(second)
    outs.append(copies.start(wz.at[:, pl.ds(0, QKV)], wz_hbm))
    outs.append(copies.start(wz.at[:, pl.ds(QKV, D)], wo_hbm))
    a1z = pick(a1, pz[...])
    a1z_ref[...] = a1z
    outs.append(copies.start(a1z_ref, a1z_hbm))
    kv = dot(a1z, wz[:, :QKV])
    kv_ref[:, 384:D] = kv[:, :384].astype(B16)
    kv_ref[:, D:] = (kv[:, 384:] + par[4:5]).astype(B16)
    outs.append(copies.start(kv_ref, kv_hbm))
    units = [jnp.concatenate([par[8 + q : 9 + q, g * 128 : (g + 1) * 128] for q in range(4)], axis=1) for g in range(6)]
    units = dot(jnp.concatenate(units + units[:2], axis=0).astype(B16), by_fours(), 1, 1)
    for g in range(6):
        ub_ref[:, g * 512 : (g + 1) * 512] = units[g : g + 1]
    attend(at_ref, 0, q_ref, kv_ref, o_ref)
    attend(at_ref, 1, q_ref, kv_ref, o_ref)
    oz = pick(o_ref[...], pz[...])
    oz_ref[...] = oz
    x1 = half_rows(x, 0) + dot(oz, wz[:, QKV:Z1]) + par[5:6]
    hat, _ = norm_stats(x1)
    x1_ref[...] = x1
    a2 = (hat * par[1:2] + par[6:7]).astype(B16)
    a2_ref[0] = pick(a2, py[...])
    a2_ref[1] = pick(a2, pz[...])
    wait(outs)


def later_attention_kernel(at_ref, x_ref, vec_ref, a1y_ref, kv_ref, pz_ref, wy_ref, wo_ref, *refs):
    x1_ref, a2_ref, q, o = refs[-4:]
    q[...] = (dot(half_rows(a1y_ref, 1), wy_ref[:, :D]) + vec_ref[3:4]).astype(B16)
    attend(at_ref, 0, q, kv_ref, o)
    attend(at_ref, 1, q, kv_ref, o)
    x1 = half_rows(x_ref, 1).astype(F32) + dot(pick(o[...], pz_ref[...]), wo_ref[...]) + vec_ref[5:6]
    hat, _ = norm_stats(x1)
    x1_ref[...] = x1
    a2_ref[...] = (hat * vec_ref[1:2] + vec_ref[6:7]).astype(B16)


def load_down(copies, at_ref, pieces, wd):
    started = []
    for i, p in enumerate(pieces):
        for j in range(2):
            at = pl.multiple_of(block_of(at_ref, i // 2, 2 * (i % 2) + j) * FIRST, FIRST)
            started.append(copies.start(p.at[pl.ds(j * FIRST, FIRST), :], wd.at[pl.ds(at, FIRST), :]))
    return started


def ffn_kernel(
    at_ref, a2_ref, x1_hbm, oz_hbm, pos_ref, cot_ref, par_ref, ub_ref, py_hbm, pz_hbm,
    y0, y1, y2, y3, z0, z1, z2, z3, d0, d1, d2, d3, wo_hbm, q_hbm,
    dx1_ref, pair_ref, vec_ref, left_ref, dz_ref, db_ref, ys_hbm, zs_hbm, ds_hbm, du_hbm, g_hbm, wd_hbm,
    wy, wz, wd, wo, py, pz, gy, gz, gd, du_all, g_all, x1_ref, oz_ref, sems,
):
    copies = Copies(sems)
    first = load_rows(copies, (y0, y1, y2, y3), wy, pl.ds(0, Y2))
    third = load_down(copies, at_ref, (d0, d1, d2, d3), wd)
    turns = [copies.start(py_hbm, py)]
    second = load_rows(copies, (z0, z1, z2, z3), wz, pl.ds(0, Z2))
    turns.append(copies.start(pz_hbm, pz))
    fourth = [
        copies.start(a, b)
        for a, b in ((x1_hbm, x1_ref), (oz_hbm, oz_ref), (wo_hbm, wo), (q_hbm, pair_ref.at[0]))
    ]
    row = lax.broadcasted_iota(jnp.int32, (HALF, 64), 0)
    dy = []
    for cell in range(2):
        hot = (row == pos_ref[cell : cell + 1, :]).astype(F32).astype(B16)
        dy.append(dot(hot, cot_ref[cell]))
    dy = jnp.concatenate(dy, axis=0)
    dz = dy.astype(B16)
    dz_ref[...] = dz
    outs, unit_sums, da2, at = [], [], None, 0
    for lane, w, grads in ((0, wy, gy), (1, wz, gz)):
        wait((first, second)[lane])
        a2 = a2_ref[lane]
        left_ref[lane] = a2[:, :FIRST]
        chunks, slopes, part = [], [], None
        for at_lane, start, width in CHUNKS:
            if at_lane == lane:
                chunks.append((slice(start, start + width), slice(at, at + width)))
                at += width
        for cols, ff in chunks:
            u = dot(a2, w[:, cols]) + ub_ref[:, ff]
            phi = 0.5 + 0.5 * lax.erf(u * RSQRT2)
            g_all[:, ff] = (u * phi).astype(B16)
            slopes.append(phi + u * (jnp.exp(-0.5 * u * u) * RSQRT2PI))
        if lane == 0:
            wait(third)
            outs.append(copies.start(wd, wd_hbm))
        for (cols, ff), slope in zip(chunks, slopes):
            du = (dot(dz, wd[ff, :], 1, 1) * slope).astype(B16)
            du_all[:, ff] = du
            back = dot(du, w[:, cols], 1, 1)
            part = back if part is None else part + back
            unit_sums.append(row_sum(du.astype(F32)))
            grads[:, cols] = dot(a2[:, FIRST:], du, 0, 0).astype(B16)
        turns[lane].wait()
        back = put_back(part, (py, pz)[lane][...])
        da2 = back if lane == 0 else da2 + back
        if lane == 0:
            outs.append(copies.start(gy, ys_hbm))
    outs += [copies.start(g_all, g_hbm), copies.start(du_all, du_hbm)]
    for i in range(4):
        cols = pl.ds(pl.multiple_of(block_of(at_ref, 1, i) * FIRST, FIRST), FIRST)
        gd[i * FIRST : (i + 1) * FIRST, :] = dot(g_all[:, cols], dz, 0, 0).astype(B16)
    outs.append(copies.start(gd, ds_hbm))
    wait(fourth)
    hat, scale = norm_stats(x1_ref[...])
    dx1 = dy + norm_back(da2, hat, scale, par_ref[1:2])
    dx1_ref[...] = dx1
    db = dx1.astype(B16)
    db_ref[...] = db
    left_ref[2] = oz_ref[:, :FIRST]
    gz[:, Z2:] = dot(oz_ref[:, FIRST:], db, 0, 0).astype(B16)
    outs.append(copies.start(gz, zs_hbm))
    pair_ref[1] = dot(dot(db, wo[...], 1, 1).astype(B16), pz[...], 1, 1).astype(B16)
    sums = jnp.concatenate(unit_sums, axis=1)
    sums = jnp.concatenate([sums[:, g * 512 : (g + 1) * 512] for g in range(6)] + [jnp.zeros((2, 512), F32)], axis=0)
    sums = dot(sums.astype(B16), by_fours())
    vec_ref[:8, :] = par_ref[...]
    vec_ref[8:9, :] = row_sum(da2 * hat)
    vec_ref[9:10, :] = row_sum(da2)
    vec_ref[10:11, :] = row_sum(dz.astype(F32))
    vec_ref[11:12, :] = row_sum(db.astype(F32))
    for q in range(4):
        vec_ref[12 + q : 13 + q, :] = jnp.concatenate(
            [sums[g : g + 1, q * 128 : (q + 1) * 128] for g in range(6)], axis=1
        )
    wait(outs)


def later_hidden_kernel(a2_ref, ub_ref, py_ref, pz_ref, y0, y1, y2, y3, z0, z1, z2, z3, *refs):
    g_ref, wy, wz = refs[-3:]
    for w, pieces in ((wy, (y0, y1, y2, y3)), (wz, (z0, z1, z2, z3))):
        for i, p in enumerate(pieces):
            w[i * PIECE : (i + 1) * PIECE, :] = p[...]
    at = 0
    for lane, start, width in CHUNKS:
        if start == 0:
            a2 = pick(a2_ref[...], (py_ref, pz_ref)[lane][...])
        ff = slice(at, at + width)
        at += width
        u = dot(a2, (wy, wz)[lane][:, start : start + width]) + ub_ref[:, ff]
        g_ref[:, ff] = (u * (0.5 + 0.5 * lax.erf(u * RSQRT2))).astype(B16)


def output_kernel(g_ref, later_g_ref, wd_ref, x1_ref, later_x1_ref, vec_ref, mixed_ref):
    for half, (g, x1) in enumerate(((g_ref, x1_ref), (later_g_ref, later_x1_ref))):
        mixed = (x1[...] + (dot(g[...], wd_ref[...]) + vec_ref[7:8])).astype(B16)
        for cell in range(2):
            to = cell * LEN + half * HALF
            mixed_ref[to : to + HALF, :] = mixed[cell * HALF : (cell + 1) * HALF]


def attention_back_kernel(at_ref, pair_ref, kv_hbm, dq_ref, dk_ref, dv_ref, vec_ref, kv_ref, sems):
    copies = Copies(sems)
    loads = [copies.start(kv_hbm.at[pl.ds(c * LEN, LEN), :], kv_ref.at[pl.ds(c * LEN, LEN), :]) for c in range(2)]
    head_lane = lax.broadcasted_iota(jnp.int32, (HALF, 128), 1) < HEAD_DIM
    key = lax.broadcasted_iota(jnp.int32, (LEN, 1), 0)
    group = 6
    for cell in range(2):
        valid = key < at_ref[4 + cell]
        loads[cell].wait()
        rows = slice(cell * LEN, (cell + 1) * LEN)
        grads = slice(cell * HALF, (cell + 1) * HALF)
        for start in range(0, HEADS // 2, group):
            held = []
            for pair in range(start, start + group):
                at = pair * 128
                q = pair_ref[0, grads, at : at + 128] * SCALE
                k = kv_ref[rows, at : at + 128]
                v = kv_ref[rows, D + at : D + at + 128]
                do = pair_ref[1, grads, at : at + 128]
                q2 = jnp.concatenate([jnp.where(head_lane, q, 0), jnp.where(head_lane, 0, q)], axis=0)
                do2 = jnp.concatenate([jnp.where(head_lane, do, 0), jnp.where(head_lane, 0, do)], axis=0)
                held.append((q2, do2, k, dot(k, q2, 1, 1), dot(v, do2, 1, 1)))
            soft = []
            for q2, do2, k, s, dp in held:
                s = jnp.where(valid, s, -1000000000.0)
                e = jnp.exp(s - jnp.max(s, axis=0, keepdims=True))
                p = e * (1.0 / jnp.sum(e, axis=0, keepdims=True))
                ds = p * (dp - jnp.sum(dp * p, axis=0, keepdims=True))
                soft.append((p.astype(B16), ds.astype(B16)))
            for i, pair in enumerate(range(start, start + group)):
                at = pair * 128
                q2, do2, k, _, _ = held[i]
                p, ds = soft[i]
                dv_ref[rows, at : at + 128] = dot(p, do2).astype(B16)
                dk_ref[rows, at : at + 128] = dot(ds, q2).astype(B16)
                dq = dot(ds, k, 0, 0) * SCALE
                dq_ref[grads, at : at + 128] = jnp.where(head_lane, dq[:HALF], dq[HALF:]).astype(B16)
    vec_ref[0:1, :] = row_sum(dq_ref[...].astype(F32))
    vec_ref[1:2, :] = row_sum(dv_ref[...].astype(F32))
    vec_ref[2:, :] = jnp.zeros((6, D), F32)


def down_other_kernel(at_ref, g_ref, dz_ref, got_ref, keep_ref, send_ref):
    for i in range(4):
        cols = pl.ds(pl.multiple_of(block_of(at_ref, 0, i) * FIRST, FIRST), FIRST)
        got = got_ref[i * FIRST : (i + 1) * FIRST, :].astype(F32)
        grad = (dot(g_ref[:, cols], dz_ref[...], 0, 0) + got).astype(B16)
        out = (keep_ref, send_ref)[i // 2]
        out[i % 2 * FIRST : (i % 2 + 1) * FIRST, :] = grad


def qkv_grads(a1y_ref, a1z_ref, dq_ref, dk_ref, dv_ref, rows):
    a1y, a1z = a1y_ref[:, rows], a1z_ref[:, rows]
    a1q = jnp.concatenate([a1y[:HALF], a1y[LEN : LEN + HALF]], axis=0)
    yield 0, 0, dot(a1q, dq_ref[...], 0, 0)
    yield 0, D, dot(a1y, dk_ref[:, :384], 0, 0)
    yield 1, 0, dot(a1z, dk_ref[:, 384:], 0, 0)
    yield 1, 384, dot(a1z, dv_ref[...], 0, 0)


def qkv_grad_kernel(a1y_ref, a1z_ref, dq_ref, dk_ref, dv_ref, *refs):
    outs = refs[-2:]
    for lane, at, grad in qkv_grads(a1y_ref, a1z_ref, dq_ref, dk_ref, dv_ref, slice(FIRST, D)):
        outs[lane][:, at : at + grad.shape[1]] = grad.astype(B16)


def add_halves(outs, at, grad, got):
    grad = (grad + got.astype(F32)).astype(B16)
    cols = slice(at, at + grad.shape[1])
    outs[0][:, cols] = grad[:PIECE]
    outs[1][:, cols] = grad[PIECE:]


def other_half_kernel(
    left_ref, db_ref, du_ref, gy_ref, gz_ref, a1y_ref, a1z_ref, dq_ref, dk_ref, dv_ref, gy1_ref, gz1_ref,
    *refs,
):
    outs = refs[-4:-2], refs[-2:]
    add_halves(outs[0], 0, dot(left_ref[0], du_ref[:, :Y2], 0, 0), gy_ref[...])
    add_halves(outs[1], 0, dot(left_ref[1], du_ref[:, Y2:], 0, 0), gz_ref[:, :Z2])
    add_halves(outs[1], Z2, dot(left_ref[2], db_ref[...], 0, 0), gz_ref[:, Z2:])
    for lane, at, grad in qkv_grads(a1y_ref, a1z_ref, dq_ref, dk_ref, dv_ref, slice(0, FIRST)):
        got = (gy1_ref, gz1_ref)[lane][:, at : at + grad.shape[1]]
        add_halves(outs[lane], (Y2, Z2 + D)[lane] + at, grad, got)


def input_grad_kernel(
    dq_ref, dk_ref, dv_ref, vec_b_ref, vec_c_ref, x_ref, dx1_ref, py, pz, wy, wz, *refs
):
    out_ref, ek_ref, es_ref, da_ref = refs[-4:]
    dz = dot(dk_ref[:, 384:], wz[:, :384], 1, 1) + dot(dv_ref[...], wz[:, 384:], 1, 1)
    da_ref[...] = put_back(dz, pz[...])
    from_q = dot(dq_ref[...], wy[:, :D], 1, 1)
    dy = dot(dk_ref[:, :384], wy[:, D:], 1, 1)
    zero = jnp.zeros((HALF, D), F32)
    dy += jnp.concatenate([from_q[:HALF], zero, from_q[HALF:], zero], axis=0)
    da = da_ref[...] + put_back(dy, py[...])
    hat, scale = norm_stats(x_ref[...].astype(F32))
    grad = norm_back(da, hat, scale, vec_b_ref[0:1])
    for cell in range(2):
        at = cell * LEN
        out_ref[at : at + HALF, :] = grad[at : at + HALF] + dx1_ref[cell * HALF : (cell + 1) * HALF]
        out_ref[at + HALF : at + LEN, :] = grad[at + HALF : at + LEN]
    lines = [
        row_sum(da * hat), vec_b_ref[8:9], row_sum(da), vec_c_ref[0:1],
        vec_c_ref[1:2], vec_b_ref[11:12], vec_b_ref[9:10], vec_b_ref[10:11],
        vec_b_ref[12:16], jnp.zeros((116, D), F32),
    ]
    ext = dot(py[...], jnp.concatenate(lines, axis=0).astype(B16), 0, 1).astype(B16)
    ek_ref[...] = ext[:FIRST]
    es_ref[...] = ext[FIRST:]


def unpack_kernel(k_ref, g1_ref, g2_ref, g3_ref, qkv_ref, out_ref, up_ref, gains_ref, biases_ref, ub_ref):
    total = k_ref[...] + g1_ref[...].astype(F32) + g2_ref[...].astype(F32) + g3_ref[...].astype(F32)
    y, z = total[:, : Y1 + Y2], total[:, Y1 + Y2 :]
    up_ref[:, :Y2] = y[:, :Y2]
    up_ref[:, Y2:] = z[:, :Z2]
    out_ref[...] = z[:, Z2 : Z2 + D]
    qkv_ref[:, :QKV] = y[:, Y2 : Y2 + QKV]
    qkv_ref[:, QKV:] = z[:, Z2 + D :]
    small = y[:, Y2 + QKV :]
    turned = small.T
    gains_ref[...] = turned[0:2]
    biases_ref[...] = turned[2:8]
    line = jnp.concatenate([small[:, 8:12]] * 6, axis=1)
    mine = lax.broadcasted_iota(jnp.int32, (6, 24), 1) // 4 == lax.broadcasted_iota(jnp.int32, (6, 24), 0)
    ub_ref[...] = row_sum(jnp.where(mine, line, 0.0))


def whole(kernel, outs, mib, flops, scratch=(), smem=0, hbm=(), hbm_outs=()):
    def call(*args):
        in_hbm = pl.BlockSpec(memory_space=pltpu.HBM)
        in_vmem = pl.BlockSpec(memory_space=pltpu.VMEM)
        specs = [pl.BlockSpec(memory_space=pltpu.SMEM)] * smem
        specs += [in_hbm if i in hbm else in_vmem for i in range(smem, len(args))]
        return pl.pallas_call(
            kernel,
            out_shape=outs,
            in_specs=specs,
            out_specs=[in_hbm if i in hbm_outs else in_vmem for i in range(len(outs))],
            scratch_shapes=scratch,
            compiler_params=pltpu.CompilerParams(vmem_limit_bytes=mib * 1024 * 1024),
            cost_estimate=pl.CostEstimate(flops=flops, bytes_accessed=1024, transcendentals=0),
        )(*args)

    return call


def shape(*dims, dtype=B16):
    return jax.ShapeDtypeStruct(dims, dtype)


def swap(v, axis, masks):
    pairs = []
    for flat in range(128):
        at = list(np.unravel_index(flat, SIZES))
        at[ALL.index(axis)] ^= masks[at[1]]
        pairs.append((flat, int(np.ravel_multi_index(at, SIZES))))
    return lax.ppermute(v, ALL, pairs)


NEAR, FAR, OPPOSITE, CORES = (1, 3), (3, 1), (2, 2), (1, 1)


def under(*parts):
    return jnp.concatenate(parts, axis=0)


def beside(*parts):
    return jnp.concatenate(parts, axis=1)


def quadruple(own, axis):
    return under(own, swap(own, axis, NEAR), swap(own, axis, FAR), swap(own, axis, OPPOSITE))


def tie(*arrays):
    return lax.optimization_barrier(arrays)


def doubled(own, axis):
    return under(own, swap(own, axis, NEAR))


def both_cores(near, far):
    return near, far, swap(near, "core", CORES), swap(far, "core", CORES)


def deal(parts, plane):
    return lax.all_to_all(parts, plane, 0, 0)


def plus(own, got):
    return own + got.astype(F32)


def total_of(own, got):
    return own.astype(F32) + got.astype(F32)


def halves(pairs):
    n = pairs[0][0].shape[0] // 2
    keep = beside(*[total_of(own[:n], got[:n]) for own, got in pairs])
    send = beside(*[total_of(own[n:], got[n:]).astype(B16) for own, got in pairs])
    return keep, send


def quarters(total):
    n = total.shape[0] // 4
    return total[:n], [total[i * n : (i + 1) * n].astype(B16) for i in (1, 2, 3)]


def exchange(sends, axis):
    return [swap(v, axis, m) for v, m in zip(sends, (NEAR, FAR, OPPOSITE))]


def local(
    tokens, lengths, positions, cotangent, qkv_weight, out_weight, up_weight, down_weight,
    norm_gains, biases, up_bias,
):
    at = jnp.concatenate([jnp.stack([lax.axis_index(a) for a in ALL]), lengths])

    yz, down = whole(pack_kernel, [shape(6, Y1 + Y2 + Z1 + Z2), shape(16, 24, D)], 60, 1_000)(
        qkv_weight, out_weight, up_weight, down_weight, norm_gains, biases, up_bias.reshape(1, 24)
    )
    yz = quadruple(yz, "x")
    down = deal(down, ("y", "z")).reshape(FIRST, D)
    y = quadruple(yz[:, : Y1 + Y2], "z")
    z = quadruple(yz[:, Y1 + Y2 :], "y")
    y1, z1, y2, z2 = y[:, :Y1], z[:, :Z1], y[:, Y1:], z[:, Z1:]
    down, at, _, _ = tie(down, at, y1, z1)
    near_y, near_z = doubled(y1, "y"), doubled(z1, "z")
    far_y, far_z = swap(near_y, "y", FAR), swap(near_z, "z", FAR)
    near_x = doubled(down, "x")
    near_x, _, _ = tie(near_x, near_y, near_z)
    far_x = swap(near_x, "x", FAR)
    got_y2, got_z2 = swap(y2, "y", NEAR), swap(z2, "z", NEAR)
    yg1, zg1 = both_cores(near_y, far_y), both_cores(near_z, far_z)
    other_x = swap(near_x, "core", CORES)
    got_y2, got_z2, _, _, _ = tie(got_y2, got_z2, near_y, near_z, near_x)
    near_y2 = under(y2, got_y2)
    other_y2 = swap(near_y2, "core", CORES)
    got_z2, other_y2 = tie(got_z2, other_y2)
    near_z2 = under(z2, got_z2)
    far_y2, far_z2 = swap(near_y2, "y", FAR), swap(near_z2, "z", FAR)

    x = tokens.reshape(ROWS, D)
    dma = pltpu.SemaphoreType.DMA
    a1y, a1z, kv, q, oz, x1, a2, par, ub, py, pz, wy, wz, wo = whole(
        attention_kernel,
        [shape(ROWS, D), shape(ROWS, D), shape(ROWS, 2 * D), shape(LEN, D), shape(LEN, D), shape(LEN, D, dtype=F32),
         shape(2, LEN, D), shape(8, D, dtype=F32), shape(1, FF, dtype=F32),
         shape(D, D), shape(D, D), shape(D, QKV), shape(D, QKV), shape(D, D)],
        60, 1_000, smem=1, hbm=range(2, 13), hbm_outs=(0, 1, 2, 9, 10, 11, 12, 13),
        scratch=[pltpu.VMEM((D, Y1), B16), pltpu.VMEM((D, Z1), B16), pltpu.VMEM((D, D), B16),
                 pltpu.VMEM((D, D), B16), pltpu.VMEM((ROWS, D), B16), pltpu.VMEM((ROWS, D), B16),
                 pltpu.VMEM((ROWS, 2 * D), B16), pltpu.VMEM((LEN, D), B16), dma((16,))],
    )(at, x, *yg1, *zg1, near_y2, near_z2, near_x)
    far_x, far_y2, far_z2, a2 = tie(far_x, far_y2, far_z2, a2)
    down = (near_x, far_x, other_x, swap(far_x, "core", CORES))
    yg2 = (near_y2, far_y2, other_y2, swap(far_y2, "core", CORES))
    zg2 = both_cores(near_z2, far_z2)

    dx1, pair, vec_b, left, dz, db, ys2, zs2, xs2, du, g, wd = whole(
        ffn_kernel,
        [shape(LEN, D, dtype=F32), shape(2, LEN, D), shape(16, D, dtype=F32),
         shape(3, LEN, FIRST), shape(LEN, D), shape(LEN, D),
         shape(FIRST, Y2), shape(FIRST, Z2 + D), shape(1536, D), shape(LEN, FF), shape(LEN, FF), shape(FF, D)],
        60, 1_000, smem=1, hbm=(2, 3, *range(8, 24)), hbm_outs=range(6, 12),
        scratch=[pltpu.VMEM((D, Y2), B16), pltpu.VMEM((D, Z2), B16), pltpu.VMEM((FF, D), B16), pltpu.VMEM((D, D), B16),
                 pltpu.VMEM((D, D), B16), pltpu.VMEM((D, D), B16), pltpu.VMEM((FIRST, Y2), B16),
                 pltpu.VMEM((FIRST, Z2 + D), B16), pltpu.VMEM((1536, D), B16), pltpu.VMEM((LEN, FF), B16),
                 pltpu.VMEM((LEN, FF), B16), pltpu.VMEM((LEN, D), F32), pltpu.VMEM((LEN, D), B16), dma((32,))],
    )(at, a2, x1, oz, positions, cotangent, par, ub, py, pz, *yg2, *zg2, *down, wo, q)

    got_x, got_y, got_z = swap(xs2, "core", CORES), swap(ys2, "core", CORES), swap(zs2, "core", CORES)
    dq, dk, dv, vec_c = whole(
        attention_back_kernel,
        [shape(LEN, D), shape(ROWS, D), shape(ROWS, D), shape(8, D, dtype=F32)],
        20, 1_000, smem=1, hbm=(2,), scratch=[pltpu.VMEM((ROWS, 2 * D), B16), dma((2,))],
    )(at, pair, kv)
    ys1, zs1 = whole(qkv_grad_kernel, [shape(FIRST, QKV), shape(FIRST, QKV)], 14, 1_000)(a1y, a1z, dq, dk, dv)
    got_y1, got_z1 = swap(ys1, "core", CORES), swap(zs1, "core", CORES)
    xk, xs = whole(down_other_kernel, [shape(D, D), shape(D, D)], 14, 1_000, smem=1)(at, g, dz, got_x)
    got_x = swap(xs, "x", FAR)
    yk, ys, zk, zs = whole(
        other_half_kernel,
        [shape(PIECE, QKV + Y2), shape(PIECE, QKV + Y2), shape(PIECE, Z1 + Z2), shape(PIECE, Z1 + Z2)],
        24, 1_000, hbm=(12,),
    )(left, db, du, got_y, got_z, a1y, a1z, dq, dk, dv, got_y1, got_z1, xs)
    got_y, got_z = swap(ys, "y", FAR), swap(zs, "z", FAR)
    token_grad, ek, es = whole(
        input_grad_kernel,
        [shape(ROWS, D, dtype=F32), shape(FIRST, 128), shape(FIRST, 128)],
        30, 1_000, hbm=(11, 12), scratch=[pltpu.VMEM((ROWS, D), F32)],
    )(dq, dk, dv, vec_b, vec_c, x, dx1, py, pz, wy, wz, ys, zs)
    kv, es = tie(kv, es)
    x1b, a2b = whole(
        later_attention_kernel, [shape(LEN, D, dtype=F32), shape(LEN, D)], 20, 1_000, smem=1,
        scratch=[pltpu.VMEM((LEN, D), B16), pltpu.VMEM((LEN, D), B16)],
    )(at, x, vec_b, a1y, kv, pz, wy, wo)
    es, a2b, got_y, got_z = tie(es, a2b, got_y, got_z)
    zk, zs = halves([(zk, got_z)])
    yk, ys = halves([(yk, got_y)])
    got_z, got_y = swap(zs, "z", NEAR), swap(ys, "y", NEAR)
    got_e, got_x, _, _ = tie(swap(es, "core", CORES), got_x, ys, zs)
    ek, es = halves([(ek, got_e)])
    got_e = swap(es, "y", FAR)
    a2b, _, _, _ = tie(a2b, ys, zs, es)
    (later_g,) = whole(
        later_hidden_kernel, [shape(LEN, FF)], 22, 1_000,
        scratch=[pltpu.VMEM((D, Y2), B16), pltpu.VMEM((D, Z2), B16)],
    )(a2b, ub, py, pz, *yg2, *zg2)
    later_g, got_e = tie(later_g, got_e)
    xk, xs = halves([(xk, got_x)])
    got_x = swap(xs, "x", NEAR)
    ek, es = halves([(ek, got_e)])
    got_e = swap(es, "y", NEAR)
    later_g, _ = tie(later_g, es)
    (mixed,) = whole(output_kernel, [shape(ROWS, D)], 16, 1_000)(g, later_g, wd, x1, x1b, vec_b)
    mixed, got_y, got_z = tie(mixed, got_y, got_z)
    zk, z_sends = quarters(total_of(zk, got_z))
    yk, y_sends = quarters(beside(total_of(yk, got_y), total_of(ek, got_e)))
    gots_z, gots_y = exchange(z_sends, "y"), exchange(y_sends, "z")
    got_x, gots_z[0], gots_y[0] = tie(got_x, gots_z[0], gots_y[0])
    down = deal(total_of(xk, got_x).astype(B16).reshape(16, 24, D), ("y", "z"))
    total = beside(sum([v.astype(F32) for v in gots_y], yk), sum([v.astype(F32) for v in gots_z], zk))
    keep, sends = quarters(total)
    down_grad = jnp.sum(down.astype(F32), axis=0)
    gots = exchange(sends, "x")
    gots[2], down_grad = tie(gots[2], down_grad)
    qkv_grad, out_grad, up_grad, gains_grad, biases_grad, ub_grad = whole(
        unpack_kernel,
        [shape(6, 3 * D, dtype=F32), shape(6, D, dtype=F32), shape(6, FF, dtype=F32), shape(2, 6, dtype=F32),
         shape(6, 6, dtype=F32), shape(1, 24, dtype=F32)],
        8, 1_000,
    )(keep, *gots)
    return (
        mixed.reshape(2, LEN, D), token_grad.reshape(2, LEN, D), qkv_grad, out_grad, up_grad, down_grad,
        gains_grad, biases_grad, ub_grad.reshape(24),
    )


def solution(mesh):
    fine = Mesh(mesh.devices.reshape(SIZES), ALL)
    rows = lambda n: P(ALL, *([None] * (n - 1)))
    cols = P(None, ALL)
    in_specs = (rows(3), rows(1), rows(2), rows(3), rows(2), rows(2), rows(2), rows(2), cols, cols, rows(1))
    out_specs = (rows(3), rows(3), rows(2), rows(2), rows(2), rows(2), cols, cols, rows(1))
    return jax.shard_map(local, mesh=fine, in_specs=in_specs, out_specs=out_specs, check_vma=False)
```

```python
import functools

import jax
import jax.numpy as jnp
import numpy as np
from jax import lax
from jax.experimental import pallas as pl
from jax.experimental.pallas import tpu as pltpu
from jax.sharding import Mesh, PartitionSpec as P

B16 = jnp.bfloat16
F32 = jnp.float32
HEADS = 12
HEAD_DIM = 64
D = 768
FF = 3072
LEN = 256
HALF = 128
ROWS = 512
PIECE = 192
FIRST = 384
Y1, Y2, Z1, Z2 = 1280, 1792, 1920, 1280
QKV = 1152
ORDER_Y, ORDER_Z = ((2, 4), (3, 1), (0, 32)), ((3, 1), (2, 4), (0, 32))
CHUNKS = ((0, 0, 896), (0, 896, 896), (1, 0, 640), (1, 640, 640))
SCALE = HEAD_DIM**-0.5
ALL = ("x", "core", "y", "z")
SIZES = (4, 2, 4, 4)
RSQRT2 = 0.5**0.5
RSQRT2PI = (2.0 * np.pi) ** -0.5


def dot(a, b, ca=1, cb=0):
    return lax.dot_general(a, b, (((ca,), (cb,)), ((), ())), preferred_element_type=F32)


def pick(a, p):
    return dot(a, p).astype(B16)


def put_back(a, p):
    return dot(a.astype(B16), p, 1, 1)


def norm_stats(v):
    centered = v - jnp.mean(v, axis=-1, keepdims=True)
    variance = jnp.mean(centered * centered, axis=-1, keepdims=True)
    scale = lax.rsqrt(variance + 1e-05)
    return centered * scale, scale


def norm_back(grad, hat, scale, gain):
    g = grad * gain
    mean_g = jnp.mean(g, axis=-1, keepdims=True)
    mean_gh = jnp.mean(g * hat, axis=-1, keepdims=True)
    return scale * (g - mean_g - hat * mean_gh)


def row_sum(v):
    return jnp.sum(v, axis=0, keepdims=True)


def softmax_of(q_one, k_two, valid):
    s = jnp.where(valid, dot(q_one, k_two, 1, 1), -1000000000.0)
    e = jnp.exp(s - jnp.max(s, axis=-1, keepdims=True))
    return e / jnp.sum(e, axis=-1, keepdims=True)


class Copies:
    def __init__(self, sems):
        self.sems, self.used = sems, 0

    def start(self, src, dst):
        copy = pltpu.make_async_copy(src, dst, self.sems.at[self.used])
        self.used += 1
        copy.start()
        return copy


def wait(copies):
    for copy in copies:
        copy.wait()


def load_rows(copies, pieces, dst, cols):
    return [
        copies.start(p.at[:, cols], dst.at[pl.ds(i * PIECE, PIECE), :]) for i, p in enumerate(pieces)
    ]


def pack_kernel(qkv_ref, out_ref, up_ref, down_ref, gains_ref, biases_ref, ub_ref, yz_ref, deal_ref):
    vecs = jnp.concatenate([gains_ref[...], biases_ref[...]], axis=0)
    eye = lax.broadcasted_iota(jnp.int32, (8, 128), 0) == lax.broadcasted_iota(jnp.int32, (8, 128), 1)
    ext = dot(vecs, eye.astype(F32).astype(B16), 0, 0)
    wide = jnp.broadcast_to(ub_ref[...].astype(F32), (6, 24)).astype(B16)
    unit = lax.broadcasted_iota(jnp.int32, (6, 24), 1)
    mine = unit // 4 == lax.broadcasted_iota(jnp.int32, (6, 24), 0)
    shift = lax.broadcasted_iota(jnp.int32, (24, 128), 0) % 4 + 8
    shift = shift == lax.broadcasted_iota(jnp.int32, (24, 128), 1)
    ub = dot(jnp.where(mine, wide, 0), shift.astype(F32).astype(B16))
    at = 0
    for part in (
        qkv_ref[:, :QKV], (ext + ub).astype(B16), up_ref[:, :Y2],
        qkv_ref[:, QKV:], out_ref[...], up_ref[:, Y2:],
    ):
        yz_ref[:, at : at + part.shape[1]] = part
        at += part.shape[1]
    for i in range(16):
        deal_ref[i] = down_ref[...]


def by_fours():
    row = lax.broadcasted_iota(jnp.int32, (512, 512), 0)
    col = lax.broadcasted_iota(jnp.int32, (512, 512), 1)
    return (row == col % 128 * 4 + col // 128).astype(F32).astype(B16)


def turned(step, core):
    gray = step ^ (step >> 1)
    return gray ^ ((gray & 1) * 2 * core)


def one_hot_of(at_ref, order):
    position = lax.broadcasted_iota(jnp.int32, (1, D), 1)
    device = (position * 10923) >> 16
    core = at_ref[1] ^ (device >> 6)
    total = core * 16
    for i, (axis, weight) in enumerate(order):
        total += (at_ref[axis] ^ turned((device >> (4 - 2 * i)) & 3, core)) * weight
    row = lax.broadcasted_iota(jnp.int32, (D, D), 0)
    return (row == total * 6 + position - device * 6).astype(F32).astype(B16)


def block_of(at_ref, half, i):
    core = at_ref[1] ^ half
    return (at_ref[0] ^ turned(i, core)) * 2 + core


def attend(at_ref, cell, q_ref, kv_ref, o_ref):
    head_lane = lax.broadcasted_iota(jnp.int32, (HALF, 128), 1) < HEAD_DIM
    valid = lax.broadcasted_iota(jnp.int32, (1, LEN), 1) < at_ref[4 + cell]
    rows = slice(cell * HALF, (cell + 1) * HALF)
    keys = slice(cell * LEN, (cell + 1) * LEN)
    group = 6
    for start in range(0, HEADS // 2, group):
        scores, probs = [], []
        for pair in range(start, start + group):
            at = pair * 128
            q = q_ref[rows, at : at + 128] * SCALE
            both = jnp.concatenate([jnp.where(head_lane, q, 0), jnp.where(head_lane, 0, q)], axis=0)
            scores.append(dot(both, kv_ref[keys, at : at + 128], 1, 1))
        for s in scores:
            s = jnp.where(valid, s, -1000000000.0)
            e = jnp.exp(s - jnp.max(s, axis=-1, keepdims=True))
            probs.append((e * (1.0 / jnp.sum(e, axis=-1, keepdims=True))).astype(B16))
        for i, pair in enumerate(range(start, start + group)):
            at = pair * 128
            o = dot(probs[i], kv_ref[keys, D + at : D + at + 128])
            o_ref[rows, at : at + 128] = jnp.where(head_lane, o[:HALF], o[HALF:]).astype(B16)


def half_rows(v, half):
    at = half * HALF
    return jnp.concatenate([v[at : at + HALF], v[LEN + at : LEN + at + HALF]], axis=0)


def attention_kernel(at_ref, x_ref, y0, y1, y2, y3, z0, z1, z2, z3, *refs):
    (a1y_hbm, a1z_hbm, kv_hbm, q_ref, oz_ref, x1_ref, a2_ref, par_ref, ub_ref,
     py_hbm, pz_hbm, wy_hbm, wz_hbm, wo_hbm) = refs[-23:-9]
    wy, wz, py, pz, a1y_ref, a1z_ref, kv_ref, o_ref, sems = refs[-9:]
    copies = Copies(sems)
    first = []
    for i, p in enumerate((y0, y1, y2, y3)):
        first.append(copies.start(p, wy.at[pl.ds(i * PIECE, PIECE), :]))
    second = []
    for i, p in enumerate((z0, z1, z2, z3)):
        second.append(copies.start(p, wz.at[pl.ds(i * PIECE, PIECE), :]))
    py[...] = one_hot_of(at_ref, ORDER_Y)
    outs = [copies.start(py, py_hbm)]
    x = x_ref[...].astype(F32)
    hat, _ = norm_stats(x)
    wait(first)
    outs.append(copies.start(wy.at[:, pl.ds(0, QKV)], wy_hbm))
    par = dot(wy[:, QKV:Y1], py[...], 0, 1)
    par_ref[...] = par[:8]
    a1 = (hat * par[0:1] + par[2:3]).astype(B16)
    a1y = pick(a1, py[...])
    a1y_ref[...] = a1y
    outs.append(copies.start(a1y_ref, a1y_hbm))
    q_ref[...] = (dot(half_rows(a1y, 0), wy[:, :D]) + par[3:4]).astype(B16)
    kv_ref[:, :384] = dot(a1y, wy[:, D:QKV]).astype(B16)
    pz[...] = one_hot_of(at_ref, ORDER_Z)
    outs.append(copies.start(pz, pz_hbm))
    wait(second)
    outs.append(copies.start(wz.at[:, pl.ds(0, QKV)], wz_hbm))
    outs.append(copies.start(wz.at[:, pl.ds(QKV, D)], wo_hbm))
    a1z = pick(a1, pz[...])
    a1z_ref[...] = a1z
    outs.append(copies.start(a1z_ref, a1z_hbm))
    kv = dot(a1z, wz[:, :QKV])
    kv_ref[:, 384:D] = kv[:, :384].astype(B16)
    kv_ref[:, D:] = (kv[:, 384:] + par[4:5]).astype(B16)
    outs.append(copies.start(kv_ref, kv_hbm))
    units = [jnp.concatenate([par[8 + q : 9 + q, g * 128 : (g + 1) * 128] for q in range(4)], axis=1) for g in range(6)]
    units = dot(jnp.concatenate(units + units[:2], axis=0).astype(B16), by_fours(), 1, 1)
    for g in range(6):
        ub_ref[:, g * 512 : (g + 1) * 512] = units[g : g + 1]
    attend(at_ref, 0, q_ref, kv_ref, o_ref)
    attend(at_ref, 1, q_ref, kv_ref, o_ref)
    oz = pick(o_ref[...], pz[...])
    oz_ref[...] = oz
    x1 = half_rows(x, 0) + dot(oz, wz[:, QKV:Z1]) + par[5:6]
    hat, _ = norm_stats(x1)
    x1_ref[...] = x1
    a2 = (hat * par[1:2] + par[6:7]).astype(B16)
    a2_ref[0] = pick(a2, py[...])
    a2_ref[1] = pick(a2, pz[...])
    wait(outs)


def later_attention_kernel(at_ref, x_ref, vec_ref, a1y_ref, kv_ref, pz_ref, wy_ref, wo_ref, *refs):
    x1_ref, a2_ref, q, o = refs[-4:]
    q[...] = (dot(half_rows(a1y_ref, 1), wy_ref[:, :D]) + vec_ref[3:4]).astype(B16)
    attend(at_ref, 0, q, kv_ref, o)
    attend(at_ref, 1, q, kv_ref, o)
    x1 = half_rows(x_ref, 1).astype(F32) + dot(pick(o[...], pz_ref[...]), wo_ref[...]) + vec_ref[5:6]
    hat, _ = norm_stats(x1)
    x1_ref[...] = x1
    a2_ref[...] = (hat * vec_ref[1:2] + vec_ref[6:7]).astype(B16)


def load_down(copies, at_ref, pieces, wd):
    started = []
    for i, p in enumerate(pieces):
        for j in range(2):
            at = pl.multiple_of(block_of(at_ref, i // 2, 2 * (i % 2) + j) * FIRST, FIRST)
            started.append(copies.start(p.at[pl.ds(j * FIRST, FIRST), :], wd.at[pl.ds(at, FIRST), :]))
    return started


def ffn_kernel(
    at_ref, a2_ref, x1_hbm, oz_hbm, pos_ref, cot_ref, par_ref, ub_ref, py_hbm, pz_hbm,
    y0, y1, y2, y3, z0, z1, z2, z3, d0, d1, d2, d3, wo_hbm, q_hbm,
    dx1_ref, pair_ref, vec_ref, left_ref, dz_ref, db_ref, ys_hbm, zs_hbm, ds_hbm, du_hbm, g_hbm, wd_hbm,
    wy, wz, wd, wo, py, pz, gy, gz, gd, du_all, g_all, x1_ref, oz_ref, sems,
):
    copies = Copies(sems)
    first = load_rows(copies, (y0, y1, y2, y3), wy, pl.ds(0, Y2))
    third = load_down(copies, at_ref, (d0, d1, d2, d3), wd)
    turns = [copies.start(py_hbm, py)]
    second = load_rows(copies, (z0, z1, z2, z3), wz, pl.ds(0, Z2))
    turns.append(copies.start(pz_hbm, pz))
    fourth = [
        copies.start(a, b)
        for a, b in ((x1_hbm, x1_ref), (oz_hbm, oz_ref), (wo_hbm, wo), (q_hbm, pair_ref.at[0]))
    ]
    row = lax.broadcasted_iota(jnp.int32, (HALF, 64), 0)
    dy = []
    for cell in range(2):
        hot = (row == pos_ref[cell : cell + 1, :]).astype(F32).astype(B16)
        dy.append(dot(hot, cot_ref[cell]))
    dy = jnp.concatenate(dy, axis=0)
    dz = dy.astype(B16)
    dz_ref[...] = dz
    outs, unit_sums, da2, at = [], [], None, 0
    for lane, w, grads in ((0, wy, gy), (1, wz, gz)):
        wait((first, second)[lane])
        a2 = a2_ref[lane]
        left_ref[lane] = a2[:, :FIRST]
        chunks, slopes, part = [], [], None
        for at_lane, start, width in CHUNKS:
            if at_lane == lane:
                chunks.append((slice(start, start + width), slice(at, at + width)))
                at += width
        for cols, ff in chunks:
            u = dot(a2, w[:, cols]) + ub_ref[:, ff]
            phi = 0.5 + 0.5 * lax.erf(u * RSQRT2)
            g_all[:, ff] = (u * phi).astype(B16)
            slopes.append(phi + u * (jnp.exp(-0.5 * u * u) * RSQRT2PI))
        if lane == 0:
            wait(third)
            outs.append(copies.start(wd, wd_hbm))
        for (cols, ff), slope in zip(chunks, slopes):
            du = (dot(dz, wd[ff, :], 1, 1) * slope).astype(B16)
            du_all[:, ff] = du
            back = dot(du, w[:, cols], 1, 1)
            part = back if part is None else part + back
            unit_sums.append(row_sum(du.astype(F32)))
            grads[:, cols] = dot(a2[:, FIRST:], du, 0, 0).astype(B16)
        turns[lane].wait()
        back = put_back(part, (py, pz)[lane][...])
        da2 = back if lane == 0 else da2 + back
        if lane == 0:
            outs.append(copies.start(gy, ys_hbm))
    outs += [copies.start(g_all, g_hbm), copies.start(du_all, du_hbm)]
    for i in range(4):
        cols = pl.ds(pl.multiple_of(block_of(at_ref, 1, i) * FIRST, FIRST), FIRST)
        gd[i * FIRST : (i + 1) * FIRST, :] = dot(g_all[:, cols], dz, 0, 0).astype(B16)
    outs.append(copies.start(gd, ds_hbm))
    wait(fourth)
    hat, scale = norm_stats(x1_ref[...])
    dx1 = dy + norm_back(da2, hat, scale, par_ref[1:2])
    dx1_ref[...] = dx1
    db = dx1.astype(B16)
    db_ref[...] = db
    left_ref[2] = oz_ref[:, :FIRST]
    gz[:, Z2:] = dot(oz_ref[:, FIRST:], db, 0, 0).astype(B16)
    outs.append(copies.start(gz, zs_hbm))
    pair_ref[1] = dot(dot(db, wo[...], 1, 1).astype(B16), pz[...], 1, 1).astype(B16)
    sums = jnp.concatenate(unit_sums, axis=1)
    sums = jnp.concatenate([sums[:, g * 512 : (g + 1) * 512] for g in range(6)] + [jnp.zeros((2, 512), F32)], axis=0)
    sums = dot(sums.astype(B16), by_fours())
    vec_ref[:8, :] = par_ref[...]
    vec_ref[8:9, :] = row_sum(da2 * hat)
    vec_ref[9:10, :] = row_sum(da2)
    vec_ref[10:11, :] = row_sum(dz.astype(F32))
    vec_ref[11:12, :] = row_sum(db.astype(F32))
    for q in range(4):
        vec_ref[12 + q : 13 + q, :] = jnp.concatenate(
            [sums[g : g + 1, q * 128 : (q + 1) * 128] for g in range(6)], axis=1
        )
    wait(outs)


def later_hidden_kernel(a2_ref, ub_ref, py_ref, pz_ref, y0, y1, y2, y3, z0, z1, z2, z3, *refs):
    g_ref, wy, wz = refs[-3:]
    for w, pieces in ((wy, (y0, y1, y2, y3)), (wz, (z0, z1, z2, z3))):
        for i, p in enumerate(pieces):
            w[i * PIECE : (i + 1) * PIECE, :] = p[...]
    at = 0
    for lane, start, width in CHUNKS:
        if start == 0:
            a2 = pick(a2_ref[...], (py_ref, pz_ref)[lane][...])
        ff = slice(at, at + width)
        at += width
        u = dot(a2, (wy, wz)[lane][:, start : start + width]) + ub_ref[:, ff]
        g_ref[:, ff] = (u * (0.5 + 0.5 * lax.erf(u * RSQRT2))).astype(B16)


def output_kernel(g_ref, later_g_ref, wd_ref, x1_ref, later_x1_ref, vec_ref, mixed_ref):
    for half, (g, x1) in enumerate(((g_ref, x1_ref), (later_g_ref, later_x1_ref))):
        mixed = (x1[...] + (dot(g[...], wd_ref[...]) + vec_ref[7:8])).astype(B16)
        for cell in range(2):
            to = cell * LEN + half * HALF
            mixed_ref[to : to + HALF, :] = mixed[cell * HALF : (cell + 1) * HALF]


def attention_back_kernel(at_ref, pair_ref, kv_hbm, dq_ref, dk_ref, dv_ref, vec_ref, kv_ref, sems):
    copies = Copies(sems)
    loads = [copies.start(kv_hbm.at[pl.ds(c * LEN, LEN), :], kv_ref.at[pl.ds(c * LEN, LEN), :]) for c in range(2)]
    head_lane = lax.broadcasted_iota(jnp.int32, (HALF, 128), 1) < HEAD_DIM
    key = lax.broadcasted_iota(jnp.int32, (LEN, 1), 0)
    group = 6
    for cell in range(2):
        valid = key < at_ref[4 + cell]
        loads[cell].wait()
        rows = slice(cell * LEN, (cell + 1) * LEN)
        grads = slice(cell * HALF, (cell + 1) * HALF)
        for start in range(0, HEADS // 2, group):
            held = []
            for pair in range(start, start + group):
                at = pair * 128
                q = pair_ref[0, grads, at : at + 128] * SCALE
                k = kv_ref[rows, at : at + 128]
                v = kv_ref[rows, D + at : D + at + 128]
                do = pair_ref[1, grads, at : at + 128]
                q2 = jnp.concatenate([jnp.where(head_lane, q, 0), jnp.where(head_lane, 0, q)], axis=0)
                do2 = jnp.concatenate([jnp.where(head_lane, do, 0), jnp.where(head_lane, 0, do)], axis=0)
                held.append((q2, do2, k, dot(k, q2, 1, 1), dot(v, do2, 1, 1)))
            soft = []
            for q2, do2, k, s, dp in held:
                s = jnp.where(valid, s, -1000000000.0)
                e = jnp.exp(s - jnp.max(s, axis=0, keepdims=True))
                p = e * (1.0 / jnp.sum(e, axis=0, keepdims=True))
                ds = p * (dp - jnp.sum(dp * p, axis=0, keepdims=True))
                soft.append((p.astype(B16), ds.astype(B16)))
            for i, pair in enumerate(range(start, start + group)):
                at = pair * 128
                q2, do2, k, _, _ = held[i]
                p, ds = soft[i]
                dv_ref[rows, at : at + 128] = dot(p, do2).astype(B16)
                dk_ref[rows, at : at + 128] = dot(ds, q2).astype(B16)
                dq = dot(ds, k, 0, 0) * SCALE
                dq_ref[grads, at : at + 128] = jnp.where(head_lane, dq[:HALF], dq[HALF:]).astype(B16)
    vec_ref[0:1, :] = row_sum(dq_ref[...].astype(F32))
    vec_ref[1:2, :] = row_sum(dv_ref[...].astype(F32))
    vec_ref[2:, :] = jnp.zeros((6, D), F32)


def down_other_kernel(at_ref, g_ref, dz_ref, got_ref, keep_ref, send_ref):
    for i in range(4):
        cols = pl.ds(pl.multiple_of(block_of(at_ref, 0, i) * FIRST, FIRST), FIRST)
        got = got_ref[i * FIRST : (i + 1) * FIRST, :].astype(F32)
        grad = (dot(g_ref[:, cols], dz_ref[...], 0, 0) + got).astype(B16)
        out = (keep_ref, send_ref)[i // 2]
        out[i % 2 * FIRST : (i % 2 + 1) * FIRST, :] = grad


def qkv_grads(a1y_ref, a1z_ref, dq_ref, dk_ref, dv_ref, rows):
    a1y, a1z = a1y_ref[:, rows], a1z_ref[:, rows]
    a1q = jnp.concatenate([a1y[:HALF], a1y[LEN : LEN + HALF]], axis=0)
    yield 0, 0, dot(a1q, dq_ref[...], 0, 0)
    yield 0, D, dot(a1y, dk_ref[:, :384], 0, 0)
    yield 1, 0, dot(a1z, dk_ref[:, 384:], 0, 0)
    yield 1, 384, dot(a1z, dv_ref[...], 0, 0)


def qkv_grad_kernel(a1y_ref, a1z_ref, dq_ref, dk_ref, dv_ref, *refs):
    outs = refs[-2:]
    for lane, at, grad in qkv_grads(a1y_ref, a1z_ref, dq_ref, dk_ref, dv_ref, slice(FIRST, D)):
        outs[lane][:, at : at + grad.shape[1]] = grad.astype(B16)


def add_halves(outs, at, grad, got):
    grad = (grad + got.astype(F32)).astype(B16)
    cols = slice(at, at + grad.shape[1])
    outs[0][:, cols] = grad[:PIECE]
    outs[1][:, cols] = grad[PIECE:]


def other_half_kernel(
    left_ref, db_ref, du_ref, gy_ref, gz_ref, a1y_ref, a1z_ref, dq_ref, dk_ref, dv_ref, gy1_ref, gz1_ref,
    *refs,
):
    outs = refs[-4:-2], refs[-2:]
    add_halves(outs[0], 0, dot(left_ref[0], du_ref[:, :Y2], 0, 0), gy_ref[...])
    add_halves(outs[1], 0, dot(left_ref[1], du_ref[:, Y2:], 0, 0), gz_ref[:, :Z2])
    add_halves(outs[1], Z2, dot(left_ref[2], db_ref[...], 0, 0), gz_ref[:, Z2:])
    for lane, at, grad in qkv_grads(a1y_ref, a1z_ref, dq_ref, dk_ref, dv_ref, slice(0, FIRST)):
        got = (gy1_ref, gz1_ref)[lane][:, at : at + grad.shape[1]]
        add_halves(outs[lane], (Y2, Z2 + D)[lane] + at, grad, got)


def input_grad_kernel(
    dq_ref, dk_ref, dv_ref, vec_b_ref, vec_c_ref, x_ref, dx1_ref, py, pz, wy, wz, *refs
):
    out_ref, ek_ref, es_ref, da_ref = refs[-4:]
    dz = dot(dk_ref[:, 384:], wz[:, :384], 1, 1) + dot(dv_ref[...], wz[:, 384:], 1, 1)
    da_ref[...] = put_back(dz, pz[...])
    from_q = dot(dq_ref[...], wy[:, :D], 1, 1)
    dy = dot(dk_ref[:, :384], wy[:, D:], 1, 1)
    zero = jnp.zeros((HALF, D), F32)
    dy += jnp.concatenate([from_q[:HALF], zero, from_q[HALF:], zero], axis=0)
    da = da_ref[...] + put_back(dy, py[...])
    hat, scale = norm_stats(x_ref[...].astype(F32))
    grad = norm_back(da, hat, scale, vec_b_ref[0:1])
    for cell in range(2):
        at = cell * LEN
        out_ref[at : at + HALF, :] = grad[at : at + HALF] + dx1_ref[cell * HALF : (cell + 1) * HALF]
        out_ref[at + HALF : at + LEN, :] = grad[at + HALF : at + LEN]
    lines = [
        row_sum(da * hat), vec_b_ref[8:9], row_sum(da), vec_c_ref[0:1],
        vec_c_ref[1:2], vec_b_ref[11:12], vec_b_ref[9:10], vec_b_ref[10:11],
        vec_b_ref[12:16], jnp.zeros((116, D), F32),
    ]
    ext = dot(py[...], jnp.concatenate(lines, axis=0).astype(B16), 0, 1).astype(B16)
    ek_ref[...] = ext[:FIRST]
    es_ref[...] = ext[FIRST:]


def unpack_kernel(k_ref, g1_ref, g2_ref, g3_ref, qkv_ref, out_ref, up_ref, gains_ref, biases_ref, ub_ref):
    total = k_ref[...] + g1_ref[...].astype(F32) + g2_ref[...].astype(F32) + g3_ref[...].astype(F32)
    y, z = total[:, : Y1 + Y2], total[:, Y1 + Y2 :]
    up_ref[:, :Y2] = y[:, :Y2]
    up_ref[:, Y2:] = z[:, :Z2]
    out_ref[...] = z[:, Z2 : Z2 + D]
    qkv_ref[:, :QKV] = y[:, Y2 : Y2 + QKV]
    qkv_ref[:, QKV:] = z[:, Z2 + D :]
    small = y[:, Y2 + QKV :]
    turned = small.T
    gains_ref[...] = turned[0:2]
    biases_ref[...] = turned[2:8]
    line = jnp.concatenate([small[:, 8:12]] * 6, axis=1)
    mine = lax.broadcasted_iota(jnp.int32, (6, 24), 1) // 4 == lax.broadcasted_iota(jnp.int32, (6, 24), 0)
    ub_ref[...] = row_sum(jnp.where(mine, line, 0.0))


def whole(kernel, outs, mib, flops, scratch=(), smem=0, hbm=(), hbm_outs=()):
    def call(*args):
        in_hbm = pl.BlockSpec(memory_space=pltpu.HBM)
        in_vmem = pl.BlockSpec(memory_space=pltpu.VMEM)
        specs = [pl.BlockSpec(memory_space=pltpu.SMEM)] * smem
        specs += [in_hbm if i in hbm else in_vmem for i in range(smem, len(args))]
        return pl.pallas_call(
            kernel,
            out_shape=outs,
            in_specs=specs,
            out_specs=[in_hbm if i in hbm_outs else in_vmem for i in range(len(outs))],
            scratch_shapes=scratch,
            compiler_params=pltpu.CompilerParams(vmem_limit_bytes=mib * 1024 * 1024),
            cost_estimate=pl.CostEstimate(flops=flops, bytes_accessed=1024, transcendentals=0),
        )(*args)

    return call


def shape(*dims, dtype=B16):
    return jax.ShapeDtypeStruct(dims, dtype)


def swap(v, axis, masks):
    pairs = []
    for flat in range(128):
        at = list(np.unravel_index(flat, SIZES))
        at[ALL.index(axis)] ^= masks[at[1]]
        pairs.append((flat, int(np.ravel_multi_index(at, SIZES))))
    return lax.ppermute(v, ALL, pairs)


NEAR, FAR, OPPOSITE, CORES = (1, 3), (3, 1), (2, 2), (1, 1)


def under(*parts):
    return jnp.concatenate(parts, axis=0)


def beside(*parts):
    return jnp.concatenate(parts, axis=1)


def quadruple(own, axis):
    return under(own, swap(own, axis, NEAR), swap(own, axis, FAR), swap(own, axis, OPPOSITE))


def tie(*arrays):
    return lax.optimization_barrier(arrays)


def doubled(own, axis):
    return under(own, swap(own, axis, NEAR))


def both_cores(near, far):
    return near, far, swap(near, "core", CORES), swap(far, "core", CORES)


def deal(parts, plane):
    return lax.all_to_all(parts, plane, 0, 0)


def plus(own, got):
    return own + got.astype(F32)


def total_of(own, got):
    return own.astype(F32) + got.astype(F32)


def halves(pairs):
    n = pairs[0][0].shape[0] // 2
    keep = beside(*[total_of(own[:n], got[:n]) for own, got in pairs])
    send = beside(*[total_of(own[n:], got[n:]).astype(B16) for own, got in pairs])
    return keep, send


def quarters(total):
    n = total.shape[0] // 4
    return total[:n], [total[i * n : (i + 1) * n].astype(B16) for i in (1, 2, 3)]


def exchange(sends, axis):
    return [swap(v, axis, m) for v, m in zip(sends, (NEAR, FAR, OPPOSITE))]


def local(
    tokens, lengths, positions, cotangent, qkv_weight, out_weight, up_weight, down_weight,
    norm_gains, biases, up_bias,
):
    at = jnp.concatenate([jnp.stack([lax.axis_index(a) for a in ALL]), lengths])

    yz, down = whole(pack_kernel, [shape(6, Y1 + Y2 + Z1 + Z2), shape(16, 24, D)], 60, 1_000)(
        qkv_weight, out_weight, up_weight, down_weight, norm_gains, biases, up_bias.reshape(1, 24)
    )
    yz = quadruple(yz, "x")
    down = deal(down, ("y", "z")).reshape(FIRST, D)
    y = quadruple(yz[:, : Y1 + Y2], "z")
    z = quadruple(yz[:, Y1 + Y2 :], "y")
    y1, z1, y2, z2 = y[:, :Y1], z[:, :Z1], y[:, Y1:], z[:, Z1:]
    down, at, _, _ = tie(down, at, y1, z1)
    near_y, near_z = doubled(y1, "y"), doubled(z1, "z")
    far_y, far_z = swap(near_y, "y", FAR), swap(near_z, "z", FAR)
    near_x = doubled(down, "x")
    near_x, _, _ = tie(near_x, near_y, near_z)
    far_x = swap(near_x, "x", FAR)
    got_y2, got_z2 = swap(y2, "y", NEAR), swap(z2, "z", NEAR)
    yg1, zg1 = both_cores(near_y, far_y), both_cores(near_z, far_z)
    other_x = swap(near_x, "core", CORES)
    got_y2, got_z2, _, _, _ = tie(got_y2, got_z2, near_y, near_z, near_x)
    near_y2 = under(y2, got_y2)
    other_y2 = swap(near_y2, "core", CORES)
    got_z2, other_y2 = tie(got_z2, other_y2)
    near_z2 = under(z2, got_z2)
    far_y2, far_z2 = swap(near_y2, "y", FAR), swap(near_z2, "z", FAR)

    x = tokens.reshape(ROWS, D)
    dma = pltpu.SemaphoreType.DMA
    a1y, a1z, kv, q, oz, x1, a2, par, ub, py, pz, wy, wz, wo = whole(
        attention_kernel,
        [shape(ROWS, D), shape(ROWS, D), shape(ROWS, 2 * D), shape(LEN, D), shape(LEN, D), shape(LEN, D, dtype=F32),
         shape(2, LEN, D), shape(8, D, dtype=F32), shape(1, FF, dtype=F32),
         shape(D, D), shape(D, D), shape(D, QKV), shape(D, QKV), shape(D, D)],
        60, 1_000, smem=1, hbm=range(2, 13), hbm_outs=(0, 1, 2, 9, 10, 11, 12, 13),
        scratch=[pltpu.VMEM((D, Y1), B16), pltpu.VMEM((D, Z1), B16), pltpu.VMEM((D, D), B16),
                 pltpu.VMEM((D, D), B16), pltpu.VMEM((ROWS, D), B16), pltpu.VMEM((ROWS, D), B16),
                 pltpu.VMEM((ROWS, 2 * D), B16), pltpu.VMEM((LEN, D), B16), dma((16,))],
    )(at, x, *yg1, *zg1, near_y2, near_z2, near_x)
    far_x, far_y2, far_z2, a2 = tie(far_x, far_y2, far_z2, a2)
    down = (near_x, far_x, other_x, swap(far_x, "core", CORES))
    yg2 = (near_y2, far_y2, other_y2, swap(far_y2, "core", CORES))
    zg2 = both_cores(near_z2, far_z2)

    dx1, pair, vec_b, left, dz, db, ys2, zs2, xs2, du, g, wd = whole(
        ffn_kernel,
        [shape(LEN, D, dtype=F32), shape(2, LEN, D), shape(16, D, dtype=F32),
         shape(3, LEN, FIRST), shape(LEN, D), shape(LEN, D),
         shape(FIRST, Y2), shape(FIRST, Z2 + D), shape(1536, D), shape(LEN, FF), shape(LEN, FF), shape(FF, D)],
        60, 1_000, smem=1, hbm=(2, 3, *range(8, 24)), hbm_outs=range(6, 12),
        scratch=[pltpu.VMEM((D, Y2), B16), pltpu.VMEM((D, Z2), B16), pltpu.VMEM((FF, D), B16), pltpu.VMEM((D, D), B16),
                 pltpu.VMEM((D, D), B16), pltpu.VMEM((D, D), B16), pltpu.VMEM((FIRST, Y2), B16),
                 pltpu.VMEM((FIRST, Z2 + D), B16), pltpu.VMEM((1536, D), B16), pltpu.VMEM((LEN, FF), B16),
                 pltpu.VMEM((LEN, FF), B16), pltpu.VMEM((LEN, D), F32), pltpu.VMEM((LEN, D), B16), dma((32,))],
    )(at, a2, x1, oz, positions, cotangent, par, ub, py, pz, *yg2, *zg2, *down, wo, q)

    got_x, got_y, got_z = swap(xs2, "core", CORES), swap(ys2, "core", CORES), swap(zs2, "core", CORES)
    dq, dk, dv, vec_c = whole(
        attention_back_kernel,
        [shape(LEN, D), shape(ROWS, D), shape(ROWS, D), shape(8, D, dtype=F32)],
        20, 1_000, smem=1, hbm=(2,), scratch=[pltpu.VMEM((ROWS, 2 * D), B16), dma((2,))],
    )(at, pair, kv)
    ys1, zs1 = whole(qkv_grad_kernel, [shape(FIRST, QKV), shape(FIRST, QKV)], 14, 1_000)(a1y, a1z, dq, dk, dv)
    got_y1, got_z1 = swap(ys1, "core", CORES), swap(zs1, "core", CORES)
    xk, xs = whole(down_other_kernel, [shape(D, D), shape(D, D)], 14, 1_000, smem=1)(at, g, dz, got_x)
    got_x = swap(xs, "x", FAR)
    yk, ys, zk, zs = whole(
        other_half_kernel,
        [shape(PIECE, QKV + Y2), shape(PIECE, QKV + Y2), shape(PIECE, Z1 + Z2), shape(PIECE, Z1 + Z2)],
        24, 1_000, hbm=(12,),
    )(left, db, du, got_y, got_z, a1y, a1z, dq, dk, dv, got_y1, got_z1, xs)
    got_y, got_z = swap(ys, "y", FAR), swap(zs, "z", FAR)
    token_grad, ek, es = whole(
        input_grad_kernel,
        [shape(ROWS, D, dtype=F32), shape(FIRST, 128), shape(FIRST, 128)],
        30, 1_000, hbm=(11, 12), scratch=[pltpu.VMEM((ROWS, D), F32)],
    )(dq, dk, dv, vec_b, vec_c, x, dx1, py, pz, wy, wz, ys, zs)
    kv, es = tie(kv, es)
    x1b, a2b = whole(
        later_attention_kernel, [shape(LEN, D, dtype=F32), shape(LEN, D)], 20, 1_000, smem=1,
        scratch=[pltpu.VMEM((LEN, D), B16), pltpu.VMEM((LEN, D), B16)],
    )(at, x, vec_b, a1y, kv, pz, wy, wo)
    es, a2b, got_y, got_z = tie(es, a2b, got_y, got_z)
    zk, zs = halves([(zk, got_z)])
    yk, ys = halves([(yk, got_y)])
    got_z, got_y = swap(zs, "z", NEAR), swap(ys, "y", NEAR)
    got_e, _, _ = tie(swap(es, "core", CORES), ys, zs)
    ek, es = halves([(ek, got_e)])
    got_e = swap(es, "y", FAR)
    a2b, _, _, _ = tie(a2b, ys, zs, es)
    (later_g,) = whole(
        later_hidden_kernel, [shape(LEN, FF)], 22, 1_000,
        scratch=[pltpu.VMEM((D, Y2), B16), pltpu.VMEM((D, Z2), B16)],
    )(a2b, ub, py, pz, *yg2, *zg2)
    later_g, got_e, got_x = tie(later_g, got_e, got_x)
    xk, xs = halves([(xk, got_x)])
    got_x = swap(xs, "x", NEAR)
    ek, es = halves([(ek, got_e)])
    got_e = swap(es, "y", NEAR)
    later_g, _ = tie(later_g, es)
    (mixed,) = whole(output_kernel, [shape(ROWS, D)], 16, 1_000)(g, later_g, wd, x1, x1b, vec_b)
    mixed, got_y, got_z = tie(mixed, got_y, got_z)
    zk, z_sends = quarters(total_of(zk, got_z))
    yk, y_sends = quarters(beside(total_of(yk, got_y), total_of(ek, got_e)))
    gots_z, gots_y = exchange(z_sends, "y"), exchange(y_sends, "z")
    got_x, gots_z[0], gots_y[0] = tie(got_x, gots_z[0], gots_y[0])
    down = deal(total_of(xk, got_x).astype(B16).reshape(16, 24, D), ("y", "z"))
    total = beside(sum([v.astype(F32) for v in gots_y], yk), sum([v.astype(F32) for v in gots_z], zk))
    keep, sends = quarters(total)
    down_grad = jnp.sum(down.astype(F32), axis=0)
    gots = exchange(sends, "x")
    gots[2], down_grad = tie(gots[2], down_grad)
    qkv_grad, out_grad, up_grad, gains_grad, biases_grad, ub_grad = whole(
        unpack_kernel,
        [shape(6, 3 * D, dtype=F32), shape(6, D, dtype=F32), shape(6, FF, dtype=F32), shape(2, 6, dtype=F32),
         shape(6, 6, dtype=F32), shape(1, 24, dtype=F32)],
        8, 1_000,
    )(keep, *gots)
    return (
        mixed.reshape(2, LEN, D), token_grad.reshape(2, LEN, D), qkv_grad, out_grad, up_grad, down_grad,
        gains_grad, biases_grad, ub_grad.reshape(24),
    )


def solution(mesh):
    fine = Mesh(mesh.devices.reshape(SIZES), ALL)
    rows = lambda n: P(ALL, *([None] * (n - 1)))
    cols = P(None, ALL)
    in_specs = (rows(3), rows(1), rows(2), rows(3), rows(2), rows(2), rows(2), rows(2), cols, cols, rows(1))
    out_specs = (rows(3), rows(3), rows(2), rows(2), rows(2), rows(2), cols, cols, rows(1))
    return jax.shard_map(local, mesh=fine, in_specs=in_specs, out_specs=out_specs, check_vma=False)
```
